32 devices in a mesh: rows: 2 (over core), blk: 4 (over z), tp: 4 (over y, x).
Axes of the slice: x: 2, y: 2, z: 4, core: 2. Of those that a mesh axis runs over, the one named last changes fastest.
Arguments:
- tokens: bfloat16 [3072, 768], P(('rows', 'blk'), 'tp'), may hold values from -18 to 18
- cotangent: bfloat16 [3072, 768], P(('rows', 'blk'), 'tp'), may hold values from -54 to 54
- segment_ids: int32 [2, 1536], P('rows'), may hold values from 0 to 1535, as said below
- matrices: float32 [768, 2880], P('tp')
- vectors: float32 [12, 768], P(None, 'tp'), may hold values from -2 to 2
- moment_mat: float32 [768, 2880], P('tp'), may hold values from -64 to 64
- square_mat: float32 [768, 2880], P('tp'), may hold values from 1 to 100
- moment_vec: float32 [12, 768], P(None, 'tp'), may hold values from -64 to 64
- square_vec: float32 [12, 768], P(None, 'tp'), may hold values from 1 to 100
Outputs:
- output: bfloat16 [3072, 768], P(('rows', 'blk'), 'tp')
- input_grad: float32 [3072, 768], P(('rows', 'blk'), 'tp')
- matrix_grad: float32 [768, 2880], P('tp')
- vector_grad: float32 [12, 768], P(None, 'tp')
- new_moment_mat: float32 [768, 2880], P('tp')
- new_square_mat: float32 [768, 2880], P('tp')
- new_moment_vec: float32 [12, 768], P(None, 'tp')
- new_square_vec: float32 [12, 768], P(None, 'tp')
- new_matrices: float32 [768, 2880], P('tp')
- new_vectors: float32 [12, 768], P(None, 'tp')
The draws below stay inside these ranges and needn't reach their ends.
Inputs may be any that keep to these rules, and one draw needn't show every extreme that they name: `segment_ids`: along each row of 1536 tokens a token's value is the position within the row of its document's first token, so values never fall along a row. One document of each row begins within the row's first 384 tokens, after its first token, and ends within its last 384 tokens, before its last; every other document has at most 512 tokens.
All inputs are finite; a program needn't handle non-finite values.
Results may differ from the reference program's by a relative error of at most 0.017.
Values may be sent and summed in bfloat16 or wider, within the bound.
A program may use at most 128 MiB of HBM per device.

```python
import math
from functools import partial
import jax
import jax.numpy as jnp
from jax import lax

D = 768
H = 12
FF = 3072
GROUPS = 4
TOK_DEV = 384
SHORT = 512
HD = 64
GW = 192
HG = 768
COLS = 2880
NVEC = 12
ROW = 1536
PACKED = 2
TOKENS = 3072


def draw_tokens(key, part):
    key = jax.random.fold_in(key, 1)
    column_ramp = 3.0 ** (jnp.arange(D, dtype=jnp.float32) / (D - 1))
    values = jax.random.truncated_normal(key, -6.0, 6.0, (TOKENS, D), jnp.float32)
    return (values * column_ramp[None, :]).astype(jnp.bfloat16)


def draw_cotangent(key, part):
    key = jax.random.fold_in(key, 2)
    column_ramp = 3.0 ** (jnp.arange(D, dtype=jnp.float32) / (D - 1))
    values = jax.random.truncated_normal(key, -6.0, 6.0, (TOKENS, D), jnp.float32)
    return (values * column_ramp[None, :]).astype(jnp.bfloat16)


def draw_matrices(key, part):
    key = jax.random.fold_in(key, 3)
    row_ramp = (3.0 ** (jnp.arange(D, dtype=jnp.float32) / (D - 1)))[:, None]
    columns = jnp.arange(COLS)[None, :]
    spread = jnp.where(columns < 3 * GW, GW ** (-0.5) / row_ramp, jnp.where(columns < 3 * GW + D, 0.5 * ROW ** 0.25 * D ** (-0.5) * row_ramp, jnp.where(columns < 3 * GW + D + HG, GW ** (-0.5) * row_ramp, HG ** (-0.5) * row_ramp)))
    values = jax.random.truncated_normal(key, -6.0, 6.0, (D, COLS), jnp.float32)
    return (values * spread).astype(jnp.float32)


def draw_vectors(key, part):
    key = jax.random.fold_in(key, 4)
    values = jax.random.truncated_normal(key, -6.0, 6.0, (NVEC, D), jnp.float32)
    row_number = jnp.arange(NVEC)[:, None]
    gain_rows = (row_number == 3) | (row_number == NVEC - 2)
    return jnp.where(gain_rows, 1.0 + 0.1 * values, 0.3 * values).astype(jnp.float32)


def draw_segment_ids(key, part):
    key = jax.random.fold_in(key, 5)
    key_start, key_end, key_cut, key_offset = jax.random.split(key, 4)
    long_start = jax.random.randint(key_start, (PACKED, 1), 1, TOK_DEV)
    long_end = ROW - jax.random.randint(key_end, (PACKED, 1), 1, TOK_DEV)
    offset = jax.random.randint(key_offset, (PACKED, 1), 0, SHORT)
    position = jnp.arange(ROW, dtype=jnp.int32)[None, :]
    cuts = jax.random.randint(key_cut, (PACKED, ROW), 0, max(SHORT // 4, 1)) == 0
    inside = (position > long_start) & (position < long_end)
    first = (position == 0) | (position == long_start) | (position == long_end) | ((position + offset) % SHORT == 0) | cuts
    first = first & jnp.logical_not(inside)
    marks = jnp.where(first, position, 0).astype(jnp.int32)
    return jax.lax.cummax(marks, axis=1).astype(jnp.int32)


def level_of(own_key, extent, cuts, low, top_value):
    level, own = 1.0, jax.random.fold_in(own_key, 6)
    for axis_at, shards_of in cuts:
        steps = jnp.exp(jax.random.uniform(jax.random.fold_in(own, axis_at), (shards_of,), jnp.float32, low / len(cuts), top_value / len(cuts)))
        level = level * jnp.repeat(steps, extent[axis_at] // shards_of).reshape([-1 if axis == axis_at else 1 for axis in range(len(extent))])
    return level


def gaussian(key, shape, scale, bound, shards=(), held_as=jnp.bfloat16):
    level = level_of(key, shape, shards, -0.22, 0.18) if shards else 1.0
    drawn = jax.random.normal(key, shape, jnp.float32) * scale * level
    return jnp.minimum(jnp.maximum(drawn, -bound), bound).astype(held_as)


def setup_inputs(seed: int = 0) -> dict:
    arg_keys = jax.random.split(jax.random.key(seed), 10)
    return {
        "tokens": draw_tokens(jax.random.fold_in(arg_keys[9], 71), 0),
        "cotangent": draw_cotangent(jax.random.fold_in(arg_keys[9], 71), 0),
        "segment_ids": draw_segment_ids(jax.random.fold_in(arg_keys[9], 71), 0),
        "matrices": draw_matrices(jax.random.fold_in(arg_keys[9], 71), 0),
        "vectors": draw_vectors(jax.random.fold_in(arg_keys[9], 71), 0),
        "moment_mat": gaussian(arg_keys[5], (D, COLS), 10.0, 64.0, ((0, 4),), jnp.float32),
        "square_mat": jnp.clip(jnp.exp(math.log(100.0) - 4.6051702 * jax.random.uniform(arg_keys[6], (D, COLS), jnp.float32) ** level_of(arg_keys[6], (D, COLS), ((0, 4),), -0.2, 0.2)), 1.0, 100.0),
        "moment_vec": gaussian(arg_keys[7], (NVEC, D), 10.0, 64.0, ((1, 4),), jnp.float32),
        "square_vec": jnp.clip(jnp.exp(math.log(100.0) - 4.6051702 * jax.random.uniform(arg_keys[8], (NVEC, D), jnp.float32) ** level_of(arg_keys[8], (NVEC, D), ((1, 4),), -0.2, 0.2)), 1.0, 100.0),
    }


eps_norm = 1e-12
beta_one = 0.9
beta_two = 0.999
adam_eps = 1e-06
step_count = 100.0
decay_rate = 0.01
learn_rate = 0.04
matrix_rate = 1.0

@jax.custom_vjp
def low(v):
    return lax.optimization_barrier(v.astype(jnp.bfloat16)).astype(jnp.float32)

@jax.custom_vjp
def low_back(v):
    return v

def low_keep(v):
    return (low(v), None)

def low_pass(kept, grad):
    return (grad,)

def back_keep(v):
    return (v, None)

def back_low(kept, grad):
    return (low(grad),)
low.defvjp(low_keep, low_pass)
low_back.defvjp(back_keep, back_low)

def grouped_product(inputs, weight, out_width):
    rows_now = inputs.shape[0]
    parts = inputs.reshape(rows_now, GROUPS, GW)
    blocks = weight.reshape(GROUPS, GW, out_width)
    return jnp.einsum('ngi,gio->ngo', parts, blocks, precision=lax.Precision.HIGHEST).reshape(rows_now, GROUPS * out_width)

def layer_norm(hidden, gain, shift):
    center = hidden - lax.optimization_barrier(jnp.mean(hidden, axis=-1, keepdims=True))
    spread = lax.optimization_barrier(jnp.mean(center * center, axis=-1, keepdims=True))
    return center * lax.rsqrt(spread + eps_norm) * gain + shift

def one_head(pieces, same_doc):
    queries, keys_now, values_now = pieces
    scores = low_back(jnp.dot(queries, keys_now.T, precision=lax.Precision.HIGHEST) * HD ** (-0.5))
    scores = jnp.where(same_doc, scores, -1e+30)
    log_total = jax.nn.logsumexp(scores, axis=-1, keepdims=True)
    return jnp.dot(low(jnp.exp(scores - log_total)), values_now, precision=lax.Precision.HIGHEST)

def block_forward(inputs, mats, vecs, same_doc):
    weights = low(mats)
    rows_now = inputs.shape[0]
    offset = 3 * GW + D
    queries = low_back(low(grouped_product(inputs, weights[:, :GW], GW) + vecs[0]))
    keys_all = low_back(low(grouped_product(inputs, weights[:, GW:2 * GW], GW)))
    values_all = low_back(low(grouped_product(inputs, weights[:, 2 * GW:3 * GW], GW) + vecs[1]))

    def by_head(field):
        return field.reshape(rows_now, H, HD).transpose(1, 0, 2)
    context = lax.map(jax.checkpoint(partial(one_head, same_doc=same_doc)), (by_head(queries), by_head(keys_all), by_head(values_all)))
    context = low_back(low(context.transpose(1, 0, 2).reshape(rows_now, D)))
    attended = low_back(jnp.dot(context, weights[:, 3 * GW:offset], precision=lax.Precision.HIGHEST) + vecs[2])
    middle = layer_norm(inputs + attended, vecs[3], vecs[4])
    bias_rows = FF // D
    hidden_bias = vecs[5:5 + bias_rows].reshape(bias_rows, GROUPS, GW).transpose(1, 0, 2).reshape(FF)
    pre_act = low_back(grouped_product(low(middle), weights[:, offset:offset + HG], HG) + hidden_bias)
    activated = low(jax.nn.gelu(pre_act, approximate=False))
    parts = activated.reshape(rows_now, GROUPS, HG)
    blocks = weights[:, offset + HG:].reshape(GROUPS, GW, HG)
    ffn_out = jnp.einsum('ngj,gcj->ngc', parts, blocks, precision=lax.Precision.HIGHEST).reshape(rows_now, D)
    ffn_out = low_back(ffn_out + vecs[5 + bias_rows])
    return layer_norm(middle + ffn_out, vecs[6 + bias_rows], vecs[7 + bias_rows])

def lamb_moments(gradient, first_moment, second_moment):
    first_new = beta_one * first_moment + (1.0 - beta_one) * gradient
    second_new = beta_two * second_moment + (1.0 - beta_two) * gradient * gradient
    update = first_new / (1.0 - beta_one ** step_count) / (jnp.sqrt(second_new / (1.0 - beta_two ** step_count)) + adam_eps)
    return (first_new, second_new, update)

def reference(tokens, cotangent, segment_ids, matrices, vectors, moment_mat, square_mat, moment_vec, square_vec):
    inputs = tokens.astype(jnp.float32).reshape(PACKED, ROW, D)
    cotangents = cotangent.astype(jnp.float32).reshape(PACKED, ROW, D)

    def row_step(running, pieces):
        row_input, row_cot, row_ids = pieces
        same_doc = row_ids[:, None] == row_ids[None, :]
        output_now, pullback = jax.vjp(lambda first_arg, mats_arg, vecs_arg: block_forward(first_arg, mats_arg, vecs_arg, same_doc), row_input, matrices, vectors)
        grad_input, grad_mats, grad_vecs = pullback(row_cot)
        return ((running[0] + grad_mats, running[1] + grad_vecs), (output_now, grad_input))
    start = (jnp.zeros_like(matrices), jnp.zeros_like(vectors))
    (matrix_grad, vector_grad), (outputs, input_grads) = lax.scan(row_step, start, (inputs, cotangents, segment_ids))
    output = outputs.reshape(TOKENS, D).astype(jnp.bfloat16)
    input_grad = input_grads.reshape(TOKENS, D)
    new_moment_mat, new_square_mat, update_mat = lamb_moments(matrix_grad, moment_mat, square_mat)
    update_mat = update_mat + decay_rate * matrices
    bounds = [0, GW, 2 * GW, 3 * GW, 3 * GW + D, 3 * GW + D + HG, COLS]
    pieces_new = []
    for index in range(len(bounds) - 1):
        weight_part = matrices[:, bounds[index]:bounds[index + 1]]
        update_part = update_mat[:, bounds[index]:bounds[index + 1]]
        trust_ratio = jnp.sqrt(jnp.sum(weight_part * weight_part) / (jnp.sum(update_part * update_part) + 1e-12))
        pieces_new.append(weight_part - matrix_rate * trust_ratio * update_part)
    new_matrices = jnp.concatenate(pieces_new, axis=1)
    new_moment_vec, new_square_vec, update_vec = lamb_moments(vector_grad, moment_vec, square_vec)
    new_vectors = vectors - learn_rate * update_vec
    return (output, input_grad, matrix_grad, vector_grad, new_moment_mat, new_square_mat, new_moment_vec, new_square_vec, new_matrices, new_vectors)
```

```python
import math
from functools import partial

import jax
import jax.numpy as jnp
from jax import lax
from jax.experimental import pallas as pl
from jax.experimental.pallas import tpu as pltpu
from jax.sharding import PartitionSpec as P

HD = 64
HG = 768
MESH = pl.DeviceIdType.MESH
f32 = jnp.float32
bf16 = jnp.bfloat16

eps_norm = 1e-12
beta_one = 0.9
beta_two = 0.999
adam_eps = 1e-06
step_count = 100.0
decay_rate = 0.01
learn_rate = 0.04
matrix_rate = 1.0
NEG = -1e30


def nn(a, b):
    return jnp.dot(a, b, preferred_element_type=f32)


def nt(a, b, **kw):
    return lax.dot_general(a, b, (((1,), (1,)), ((), ())), preferred_element_type=f32, **kw)


def eye(n, dtype=bf16):
    rows = lax.broadcasted_iota(jnp.int32, (n, n), 0)
    cols = lax.broadcasted_iota(jnp.int32, (n, n), 1)
    return (rows == cols).astype(dtype)


def flip(a):
    return nt(eye(a.shape[1]), a)


def split_bf16(a):
    high = a.astype(bf16)
    return high, (a - high.astype(f32)).astype(bf16)


def lane_sums(a):
    return nt(jnp.ones((8, a.shape[1]), bf16), a)[0:1]


def lane_sums_f32(a):
    high, low = split_bf16(a)
    return lane_sums(high) + lane_sums(low)


def lamb_moments(gradient, first_moment, second_moment):
    first_new = beta_one * first_moment + (1.0 - beta_one) * gradient
    second_new = beta_two * second_moment + (1.0 - beta_two) * gradient * gradient
    update = (
        first_new
        / (1.0 - beta_one**step_count)
        / (jnp.sqrt(second_new / (1.0 - beta_two**step_count)) + adam_eps)
    )
    return first_new, second_new, update


def gelu_pair(pre):
    half = 0.5 * (1.0 + lax.erf(pre * (2.0**-0.5)))
    slope = half + pre * (jnp.exp(-0.5 * pre * pre) * ((2.0 * math.pi) ** -0.5))
    return pre * half, slope


class Sizes:
    def __init__(self, mesh_shape, tokens, row_count):
        self.nr = mesh_shape["rows"]
        self.nb = mesh_shape["blk"]
        self.nt = mesh_shape["tp"]
        self.t, self.g = tokens
        self.d = self.g * self.nt
        self.heads = self.g // HD
        self.row = row_count
        self.wide = self.heads * self.t
        self.half = HG // 2
        self.keep = self.nb <= 8
        owners = self.nb
        while self.nb % owners or self.g % (16 * owners):
            owners -= 1
        self.owners = owners
        self.rq = self.g // owners
        o = 3 * self.g
        self.lo = (o + self.d + HG, o + self.d, o, 0)
        self.width = (HG, HG, self.d, o)


def scratch_of(s):
    V = pltpu.VMEM
    D = pltpu.SemaphoreType.DMA
    T, G, nb, ntp = s.t, s.g, s.nb, s.nt
    kept = nb if s.keep else 1
    shapes = dict(
        xall=V((nb, T, G), bf16),
        xtall=V((kept, G, T), bf16),
        xtf=V((ntp, G, T), bf16),
        wot=V((ntp, s.d, G), bf16),
        vec=V((ntp, 16, G), f32),
        ctxg=V((ntp, G, T), bf16),
        st1=V((ntp, 8, T), f32),
        dmg=V((ntp, G, T), bf16),
        st2=V((ntp, 8, T), f32),
        nrm=V((ntp, 16, 128), f32),
        dxs=V((nb, T, G), bf16),
        dxr=V((nb, T, G), bf16),
        gsrc=V((4, 2, G, s.half), bf16),
        gcore=V((4, G, s.half), bf16),
        ghalf=V((4, s.owners, s.rq, s.half), bf16),
        gz=V((4, nb, s.rq, s.half), bf16),
        gfin=V((4, 2, s.owners, s.rq, s.half), bf16),
        vgl=V((16, G), f32),
        vgc=V((16, G), f32),
        vgs=V((16, G), f32),
        vgz=V((nb, 16, G), f32),
        mom=V((G, s.lo[0] + HG), f32),
        squ=V((G, s.lo[0] + HG), f32),
        wq_t=V((G, G), bf16),
        wk=V((G, G), bf16),
        wk_t=V((G, G), bf16),
        wv=V((G, G), bf16),
        wv_t=V((G, G), bf16),
        wo=V((G, s.d), bf16),
        w1=V((G, HG), bf16),
        w1_t=V((HG, G), bf16),
        w2=V((G, HG), bf16),
        w2_t=V((HG, G), bf16),
        qz=V((G, s.wide), bf16),
        dcz=V((G, s.wide), bf16),
        idk=V((kept, T, 128), f32),
        ebuf=V((kept, T, s.wide), bf16),
        mrec=V((nb, 1, s.wide), f32),
        mrun=V((1, s.wide), f32),
        lrun=V((1, s.wide), f32),
        acc=V((G, T), f32),
        delta=V((1, s.wide), f32),
        lse=V((1, s.wide), f32),
        n1f=V((ntp, G, T), f32),
        datt=V((s.d, T), bf16),
        act=V((HG, T), bf16),
        slope=V((HG, T), f32),
        mid=V((G, T), f32),
        dqt=V((G, T), f32),
        gkv=V((2, G, G), f32),
        dsb=V((T, s.wide), bf16),
        pb=V((T, s.wide), bf16),
        vb=V((1, G), f32),
        dxo=V((T, G), f32),
        x_s=D((nb,)), x_r=D((nb,)),
        xt_s=D((ntp,)), xt_r=D((ntp,)),
        wo_s=D((ntp,)), wo_r=D((ntp,)),
        vec_s=D((ntp,)), vec_r=D((ntp,)),
        ctx_s=D((ntp,)), ctx_r=D((ntp,)),
        st1_s=D((ntp,)), st1_r=D((ntp,)),
        dmg_s=D((ntp,)), dmg_r=D((ntp,)),
        st2_s=D((ntp,)), st2_r=D((ntp,)),
        nrm_s=D((ntp,)), nrm_r=D((ntp,)),
        dx_s=D((nb,)), dx_r=D((nb,)),
        gc_s=D((4,)), gc_r=D((4,)),
        gz_s=D((4, nb)), gz_r=D((4, nb)),
        ga_s=D((4, nb)), ga_r=D((4, nb)),
        gd_s=D((4,)), gd_r=D((4,)),
        vc_s=D((1,)), vc_r=D((1,)),
        vz_s=D((nb,)), vz_r=D((nb,)),
        loc=D((2,)),
    )
    return list(shapes.keys()), list(shapes.values())


def layer_kernel(s, names, x_ref, cot_ref, ids_ref, w_ref, v_ref, mom_hbm, squ_hbm,
                 out_ref, ig_ref, g_ref, vg_ref, ratio_ref, *scratch):
    r = dict(zip(names, scratch))
    T, G, nb, ntp = s.t, s.g, s.nb, s.nt
    c, b, t = lax.axis_index("rows"), lax.axis_index("blk"), lax.axis_index("tp")
    core = (1 - c, b, t)
    tx, ty = t % 2, t // 2
    tp_peers = [ty * 2 + (1 - tx), (1 - ty) * 2 + tx, 3 - t]
    z_peers = [(b + o) % nb for o in range(1, nb)]

    def tp_dev(k):
        return (c, b, k)

    def z_dev(k):
        return (c, k, t)

    sent = []

    def copy(src, dst, ssem, rsem, dev):
        return pltpu.make_async_remote_copy(
            src_ref=src, dst_ref=dst, send_sem=ssem, recv_sem=rsem, device_id=dev, device_id_type=MESH
        )

    def push(src, dst, ssem, rsem, dev):
        one = copy(src, dst, ssem, rsem, dev)
        one.start()
        sent.append(one)

    def arrive(dst, ssem, rsem, dev):
        copy(dst, dst, ssem, rsem, dev).wait_recv()

    def tp_push(name):
        for k in tp_peers:
            push(r[name].at[t], r[name].at[t], r[SEM[name] + "_s"].at[k],
                 r[SEM[name] + "_r"].at[t], tp_dev(k))

    def tp_wait(name, k):
        arrive(r[name].at[k], r[SEM[name] + "_s"].at[k], r[SEM[name] + "_r"].at[k], tp_dev(k))

    SEM = dict(xtf="xt", wot="wo", vec="vec", ctxg="ctx", st1="st1", dmg="dmg", st2="st2", nrm="nrm")

    barrier = pltpu.get_barrier_semaphore()
    pl.semaphore_signal(barrier, 1, device_id=core, device_id_type=MESH)
    for k in tp_peers:
        pl.semaphore_signal(barrier, 1, device_id=tp_dev(k), device_id_type=MESH)
    for k in z_peers:
        pl.semaphore_signal(barrier, 1, device_id=z_dev(k), device_id_type=MESH)
    local_m = pltpu.make_async_copy(mom_hbm, r["mom"], r["loc"].at[0])
    local_s = pltpu.make_async_copy(squ_hbm, r["squ"], r["loc"].at[1])
    local_m.start()
    local_s.start()

    x_own = x_ref[...]
    r["xall"][b] = x_own
    x_t = flip(x_own).astype(bf16)
    if s.keep:
        r["xtall"][b] = x_t
    r["xtf"][t] = x_t
    r["vec"][t, 0:12, :] = v_ref[...]
    r["vec"][t, 12:16, :] = jnp.zeros((4, G), f32)
    w_o = w_ref[:, s.lo[2]:s.lo[2] + s.d].astype(bf16)
    r["wo"][...] = w_o
    r["wot"][t] = flip(w_o).astype(bf16)
    pl.semaphore_wait(barrier, 1 + (ntp - 1) + (nb - 1))

    for k in z_peers:
        push(r["xall"].at[b], r["xall"].at[b], r["x_s"].at[k], r["x_r"].at[b], z_dev(k))
    tp_push("vec")
    tp_push("xtf")
    tp_push("wot")

    w_q = w_ref[:, 0:G].astype(bf16)
    w_k = w_ref[:, G:2 * G].astype(bf16)
    w_v = w_ref[:, 2 * G:3 * G].astype(bf16)
    r["wq_t"][...] = flip(w_q).astype(bf16)
    r["wk"][...] = w_k
    r["wk_t"][...] = flip(w_k).astype(bf16)
    r["wv"][...] = w_v
    r["wv_t"][...] = flip(w_v).astype(bf16)
    w_1 = w_ref[:, s.lo[1]:s.lo[1] + HG].astype(bf16)
    w_2 = w_ref[:, s.lo[0]:s.lo[0] + HG].astype(bf16)
    r["w1"][...] = w_1
    r["w1_t"][...] = flip(w_1).astype(bf16)
    r["w2"][...] = w_2
    r["w2_t"][...] = flip(w_2).astype(bf16)

    def columns_of(vec):
        return nt(eye(G, f32), vec, precision=lax.Precision.HIGHEST)

    v_cols = columns_of(r["vec"][t])

    def v_col(k):
        return v_cols[:, k:k + 1]

    bias_v_row = v_ref[1:2, :]
    bias_v_col = v_col(1)

    scaling = HD**-0.5
    q_t = (nt(r["wq_t"][...], x_own) + v_col(0)).astype(bf16)
    q_t = (q_t.astype(f32) * scaling)
    head_of = lax.broadcasted_iota(jnp.int32, (G, T), 0) // HD

    def by_head(a):
        return [jnp.where(head_of == h, a, 0.0).astype(bf16) for h in range(s.heads)]

    for h, part in enumerate(by_head(q_t)):
        r["qz"][:, h * T:(h + 1) * T] = part

    def ids_of(j):
        return ids_ref[:, pl.ds(pl.multiple_of(j * T, 128), T)].astype(f32)

    def id_columns(j):
        ids = ids_of(j)
        high = jnp.floor(ids * (1.0 / 128.0))
        low = ids - 128.0 * high
        high, low = (jnp.broadcast_to(a, (128, T)).astype(bf16) for a in (high, low))
        return 128.0 * nt(eye(T), high) + nt(eye(T), low)

    if s.keep:
        for k in range(nb):
            r["idk"][k] = id_columns(k)
    id_q = ids_of(b)

    r["mrun"][...] = jnp.full((1, s.wide), NEG, f32)
    r["lrun"][...] = jnp.zeros((1, s.wide), f32)
    r["acc"][...] = jnp.zeros((G, T), f32)

    def same_doc(j):
        keys = r["idk"][j] if s.keep else id_columns(j)
        return jnp.concatenate([keys] * (T // 128), axis=1) == id_q

    def forward_block(j):
        x_j = r["xall"][j]
        keys = nn(x_j, r["wk"][...]).astype(bf16)
        vals_t = (nt(r["wv_t"][...], x_j) + bias_v_col).astype(bf16)
        mask = same_doc(j)
        for h in range(s.heads):
            cols = slice(h * T, (h + 1) * T)
            rows = slice(h * HD, (h + 1) * HD)
            score = jnp.where(mask, nn(keys, r["qz"][:, cols]), NEG)
            old = r["mrun"][:, cols]
            top = jnp.maximum(old, jnp.max(score, axis=0, keepdims=True))
            fade = jnp.exp(old - top)
            e = jnp.exp(score - top)
            r["lrun"][:, cols] = r["lrun"][:, cols] * fade + jnp.sum(e, axis=0, keepdims=True)
            e = e.astype(bf16)
            if s.keep:
                r["ebuf"][j, :, cols] = e
                r["mrec"][j, :, cols] = top
            r["mrun"][:, cols] = top
            r["acc"][rows, :] = r["acc"][rows, :] * fade + nn(vals_t[rows, :], e)

    forward_block(b)

    def forward_remote(o):
        j = (b + o) % nb
        arrive(r["xall"].at[j], r["x_s"].at[j], r["x_r"].at[j], z_dev(j))
        if s.keep:
            r["xtall"][j] = flip(r["xall"][j]).astype(bf16)
        forward_block(j)

    def each_remote(body):
        if nb <= 4:
            for o in range(1, nb):
                body(o)
        else:
            lax.fori_loop(1, nb, lambda o, _: (body(o), 0)[1], 0)

    each_remote(forward_remote)

    r["lse"][...] = r["mrun"][...] + jnp.log(r["lrun"][...])
    context = jnp.concatenate(
        [
            r["acc"][h * HD:(h + 1) * HD, :] / r["lrun"][:, h * T:(h + 1) * T]
            for h in range(s.heads)
        ],
        axis=0,
    )
    r["acc"][...] = context
    r["ctxg"][t] = context.astype(bf16)
    tp_push("ctxg")

    for k in tp_peers:
        tp_wait("vec", k)
        tp_wait("xtf", k)
        tp_wait("wot", k)
    att = nn(r["wot"][t], r["ctxg"][t])
    for k in tp_peers:
        tp_wait("ctxg", k)
        att = att + nn(r["wot"][k], r["ctxg"][k])
    hidden = []
    for k in range(ntp):
        bias = columns_of(r["vec"][k])[:, 2:3]
        hidden.append(r["xtf"][k].astype(f32) + att[k * G:(k + 1) * G] + bias)
    mean1 = sum(jnp.sum(a, axis=0, keepdims=True) for a in hidden) / s.d
    hidden = [a - mean1 for a in hidden]
    var1 = sum(jnp.sum(a * a, axis=0, keepdims=True) for a in hidden) / s.d
    inv1 = lax.rsqrt(var1 + eps_norm)
    for k in range(ntp):
        r["n1f"][k] = hidden[k] * inv1
    gain1 = v_col(3)
    mid = r["n1f"][t] * gain1 + v_col(4)
    mid_low = mid.astype(bf16)
    r["mid"][...] = mid

    bias_rows = HG // G
    hid_bias = jnp.concatenate([v_col(5 + k) for k in range(bias_rows)], axis=0)
    pre = nn(r["w1_t"][...], mid_low) + hid_bias
    act, slope = gelu_pair(pre)
    r["act"][...] = act.astype(bf16)
    r["slope"][...] = slope
    h2 = mid + nn(r["w2"][...], r["act"][...]) + v_col(5 + bias_rows)
    gain2 = v_col(6 + bias_rows)
    shift2 = v_col(7 + bias_rows)
    cot = flip(cot_ref[...])
    scaled = cot * gain2
    sum1 = jnp.sum(h2, axis=0, keepdims=True)
    h2c = h2 - sum1 / G
    sum2 = jnp.sum(h2c * h2c, axis=0, keepdims=True)
    sum3 = jnp.sum(scaled, axis=0, keepdims=True)
    sum4 = jnp.sum(scaled * h2c, axis=0, keepdims=True)
    r["st1"][t] = jnp.concatenate([sum1, sum2, sum3, sum4, jnp.zeros((4, T), f32)], axis=0)
    tp_push("st1")
    for k in tp_peers:
        tp_wait("st1", k)
    stats = [r["st1"][k] for k in range(ntp)]
    mean2 = sum(a[0:1] for a in stats) / s.d
    offs = [a[0:1] / G - mean2 for a in stats]
    var2 = sum(a[1:2] + G * o * o for a, o in zip(stats, offs)) / s.d
    inv2 = lax.rsqrt(var2 + eps_norm)
    first = sum(a[2:3] for a in stats) / s.d
    second = sum(a[3:4] + a[2:3] * o for a, o in zip(stats, offs)) * inv2 / s.d
    n2 = (h2 - mean2) * inv2
    out_ref[...] = nt(eye(T), (n2 * gain2 + shift2).astype(bf16)).astype(bf16)
    d2 = inv2 * (scaled - first - n2 * second)
    dffn = d2.astype(bf16)
    dact = nn(r["w2_t"][...], dffn)
    dpre = (dact * r["slope"][...]).astype(bf16)
    dmid = d2 + nn(r["w1"][...], dpre)
    n1 = r["n1f"][t]
    dmg = dmid * gain1
    part1 = jnp.sum(dmg, axis=0, keepdims=True)
    part2 = jnp.sum(dmg * n1, axis=0, keepdims=True)
    r["st2"][t] = jnp.concatenate([part1, part2, jnp.zeros((6, T), f32)], axis=0)
    r["dmg"][t] = dmg.astype(bf16)
    tp_push("st2")
    tp_push("dmg")

    def sum_start(m):
        push(r["gsrc"].at[m, 1 - c], r["gcore"].at[m], r["gc_s"].at[m], r["gc_r"].at[m], core)

    def sum_spread(m):
        arrive(r["gcore"].at[m], r["gc_s"].at[m], r["gc_r"].at[m], core)
        both = (r["gsrc"][m, c].astype(f32) + r["gcore"][m].astype(f32)).astype(bf16)
        for k in range(s.owners):
            r["ghalf"][m, k] = both[k * s.rq:(k + 1) * s.rq]

        def to_owner(j):
            push_or = copy(r["ghalf"].at[m, j], r["gz"].at[m, b], r["gz_s"].at[m, j], r["gz_r"].at[m, b], z_dev(j))
            push_or.start()

        for j in z_peers:
            if s.owners < nb:
                pl.when(j < s.owners)(partial(to_owner, j))
            else:
                to_owner(j)

    def owner_only(body):
        if s.owners < nb:
            pl.when(b < s.owners)(body)
        else:
            body()

    def sum_own(m):
        def body():
            for j in z_peers:
                arrive(r["gz"].at[m, j], r["gz_s"].at[m, 0], r["gz_r"].at[m, j], z_dev(j))
            r["gz"][m, b] = r["ghalf"][m, b]
            total = r["gz"][m, 0].astype(f32)
            for j in range(1, nb):
                total = total + r["gz"][m, j].astype(f32)
            r["gfin"][m, c, b] = total.astype(bf16)
            for j in z_peers:
                copy(r["gfin"].at[m, c, b], r["gfin"].at[m, c, b], r["ga_s"].at[m, j], r["ga_r"].at[m, b], z_dev(j)).start()

        owner_only(body)

    def sum_share(m):
        for j in z_peers:
            def got(j=j):
                arrive(r["gfin"].at[m, c, j], r["ga_s"].at[m, 0], r["ga_r"].at[m, j], z_dev(j))
            if s.owners < nb:
                pl.when(j < s.owners)(got)
            else:
                got()
        push(r["gfin"].at[m, c], r["gfin"].at[m, c], r["gd_s"].at[m], r["gd_r"].at[m], core)

    def sum_done(m):
        arrive(r["gfin"].at[m, 1 - c], r["gd_s"].at[m], r["gd_r"].at[m], core)

    def sum_sends_done(m):
        for j in z_peers:
            def done(j=j):
                copy(r["ghalf"].at[m, j], r["gz"].at[m, b], r["gz_s"].at[m, j], r["gz_r"].at[m, b], z_dev(j)).wait_send()
            if s.owners < nb:
                pl.when(j < s.owners)(done)
            else:
                done()

        def body():
            for j in z_peers:
                copy(r["gfin"].at[m, c, b], r["gfin"].at[m, c, b], r["ga_s"].at[m, j], r["ga_r"].at[m, b], z_dev(j)).wait_send()

        owner_only(body)

    def keep_grad(m, grad):
        r["gsrc"][m, 0] = grad[:, 0:s.half].astype(bf16)
        r["gsrc"][m, 1] = grad[:, s.half:].astype(bf16)

    keep_grad(0, nt(dffn, r["act"][...]))
    sum_start(0)
    keep_grad(1, nt(mid_low, dpre))
    sum_start(1)
    vgl = r["vgl"]
    vgl[12:16, :] = jnp.zeros((4, G), f32)
    vgl[3:4, :] = lane_sums_f32(dmid * n1)
    vgl[4:5, :] = lane_sums_f32(dmid)
    hid_sum = lane_sums(dpre)
    for k in range(bias_rows):
        vgl[5 + k:6 + k, :] = hid_sum[:, k * G:(k + 1) * G]
    vgl[5 + bias_rows:6 + bias_rows, :] = lane_sums(dffn)
    vgl[6 + bias_rows:7 + bias_rows, :] = lane_sums_f32(cot * n2)
    vgl[7 + bias_rows:8 + bias_rows, :] = lane_sums_f32(cot)

    for k in tp_peers:
        tp_wait("st2", k)
    stats = [r["st2"][k] for k in range(ntp)]
    first = sum(a[0:1] for a in stats) / s.d
    second = sum(a[1:2] for a in stats) / s.d
    d1_own = inv1 * (dmg - first - n1 * second)
    for k in tp_peers:
        tp_wait("dmg", k)
    for k in range(ntp):
        part = inv1 * (r["dmg"][k].astype(f32) - first - r["n1f"][k] * second)
        r["datt"][k * G:(k + 1) * G, :] = part.astype(bf16)
    vgl[2:3, :] = lane_sums(d1_own.astype(bf16))
    dctx = nn(r["wo"][...], r["datt"][...]).astype(bf16).astype(f32)
    for h, part in enumerate(by_head(dctx)):
        r["dcz"][:, h * T:(h + 1) * T] = part
        rows = slice(h * HD, (h + 1) * HD)
        r["delta"][:, h * T:(h + 1) * T] = jnp.sum(dctx[rows] * r["acc"][rows, :], axis=0, keepdims=True)
    sum_spread(0)
    sum_spread(1)
    keep_grad(2, nt(r["ctxg"][t], r["datt"][...]))
    sum_start(2)
    d1_high, d1_low = split_bf16(d1_own)
    r["dxo"][...] = nt(eye(T), d1_high) + nt(eye(T), d1_low)

    r["dqt"][...] = jnp.zeros((G, T), f32)
    r["gkv"][...] = jnp.zeros((2, G, G), f32)
    r["vb"][...] = jnp.zeros((1, G), f32)

    def backward_block(j):
        x_j = r["xall"][j]
        keys_t = nt(r["wk_t"][...], x_j).astype(bf16)
        vals = (nn(x_j, r["wv"][...]) + bias_v_row).astype(bf16)
        if not s.keep:
            keys = nn(x_j, r["wk"][...]).astype(bf16)
            mask = same_doc(j)
        for h in range(s.heads):
            cols = slice(h * T, (h + 1) * T)
            rows = slice(h * HD, (h + 1) * HD)
            if s.keep:
                weight = jnp.exp(r["mrec"][j, :, cols] - r["lse"][:, cols])
                p = r["ebuf"][j, :, cols].astype(f32) * weight
            else:
                p = jnp.exp(jnp.where(mask, nn(keys, r["qz"][:, cols]), NEG) - r["lse"][:, cols])
            dp = nn(vals, r["dcz"][:, cols])
            ds = (p * (dp - r["delta"][:, cols])).astype(bf16)
            r["dsb"][:, cols] = ds
            r["pb"][:, cols] = p.astype(bf16)
            r["dqt"][rows, :] += nn(keys_t[rows, :], ds)
        dk = nt(r["dsb"][...], r["qz"][...]).astype(bf16)
        dv = nt(r["pb"][...], r["dcz"][...]).astype(bf16)
        x_jt = r["xtall"][j] if s.keep else flip(x_j).astype(bf16)
        r["gkv"][0] += nn(x_jt, dk)
        r["gkv"][1] += nn(x_jt, dv)
        r["vb"][...] += jnp.sum(dv.astype(f32), axis=0, keepdims=True)
        return nn(dk, r["wk_t"][...]) + nn(dv, r["wv_t"][...])

    def backward_remote(o):
        j = (b + o) % nb
        r["dxs"][j] = backward_block(j).astype(bf16)
        copy(r["dxs"].at[j], r["dxr"].at[b], r["dx_s"].at[j], r["dx_r"].at[b], z_dev(j)).start()
        if nb <= 4:
            stages = {1: (sum_own, 0, 1), 2: (sum_share, 0, 1), 3: (sum_spread, 2)}
            if o in stages:
                for m in stages[o][1:]:
                    stages[o][0](m)

    each_remote(backward_remote)
    if nb < 4 or nb > 4:
        sum_own(0)
        sum_own(1)
        sum_share(0)
        sum_share(1)
        sum_spread(2)
    dx = backward_block(b)
    dq_t = (r["dqt"][...] * scaling).astype(bf16)
    r["gsrc"][3, 0, :, 0:G] = nt(r["xtall"][b], dq_t).astype(bf16)
    r["gsrc"][3, 0, :, G:2 * G] = r["gkv"][0].astype(bf16)
    r["gsrc"][3, 1, :, 0:G] = r["gkv"][1].astype(bf16)
    r["gsrc"][3, 1, :, G:2 * G] = jnp.zeros((G, G), bf16)
    sum_start(3)
    vgl[0:1, :] = lane_sums(dq_t)
    vgl[1:2, :] = r["vb"][...]
    push(vgl, r["vgc"], r["vc_s"].at[0], r["vc_r"].at[0], core)
    r["dxo"][...] += dx + nn(nt(eye(T), dq_t).astype(bf16), r["wq_t"][...])
    sum_own(2)
    sum_spread(3)
    arrive(r["vgc"], r["vc_s"].at[0], r["vc_r"].at[0], core)
    r["vgs"][...] = vgl[...] + r["vgc"][...]
    r["vgz"][b] = r["vgs"][...]
    for j in z_peers:
        push(r["vgs"], r["vgz"].at[b], r["vz_s"].at[j], r["vz_r"].at[b], z_dev(j))
    sum_share(2)
    local_m.wait()
    local_s.wait()

    def norms_of(m):
        rows = []
        for h in range(2):
            lo = s.lo[m] + h * s.half
            wide = min(s.half, s.lo[m] + s.width[m] - lo)
            grad = jnp.concatenate([r["gfin"][m, h, k] for k in range(s.owners)], axis=0)[:, :wide]
            w = w_ref[:, lo:lo + wide]
            _, _, u = lamb_moments(grad.astype(f32), r["mom"][:, lo:lo + wide], r["squ"][:, lo:lo + wide])
            u = u + decay_rate * w
            rows.append((jnp.sum(w * w, axis=0, keepdims=True), jnp.sum(u * u, axis=0, keepdims=True)))
        return rows

    def total(a):
        return jnp.broadcast_to(jnp.sum(a, axis=1, keepdims=True), (1, 128))

    sums = {}
    for m in (0, 1):
        sum_done(m)
        sums[m] = norms_of(m)
    sum_own(3)
    sum_done(2)
    sums[2] = norms_of(2)
    for j in z_peers:
        arrive(r["dxr"].at[j], r["dx_s"].at[j], r["dx_r"].at[j], z_dev(j))
    got = r["dxo"][...]
    for j in z_peers:
        got = got + r["dxr"][j].astype(f32)
    ig_ref[...] = got
    sum_share(3)
    for j in z_peers:
        arrive(r["vgz"].at[j], r["vz_s"].at[j], r["vz_r"].at[j], z_dev(j))
    vg = r["vgz"][0]
    for j in range(1, nb):
        vg = vg + r["vgz"][j]
    vg_ref[...] = vg[0:12]
    sum_done(3)
    sums[3] = norms_of(3)
    packed = []
    for which in range(2):
        lead = sums[3][0][which]
        packed += [total(lead[:, 0:G]), total(lead[:, G:2 * G]), total(sums[3][1][which])]
        packed += [total(sums[m][0][which] + sums[m][1][which]) for m in (2, 1, 0)]
        packed += [jnp.zeros((2, 128), f32)]
    r["nrm"][t] = jnp.concatenate(packed, axis=0)
    tp_push("nrm")
    for m in range(4):
        for h in range(2):
            for k in range(s.owners):
                g_ref[m, h, k] = r["gfin"][m, h, k]
    for k in tp_peers:
        tp_wait("nrm", k)
    norms = r["nrm"][0]
    for k in range(1, ntp):
        norms = norms + r["nrm"][k]
    ratio_ref[...] = jnp.sqrt(norms[0:8] / (norms[8:16] + 1e-12))

    for one in sent:
        one.wait_send()
    for m in range(4):
        sum_sends_done(m)
    for j in z_peers:
        copy(r["dxs"].at[j], r["dxr"].at[b], r["dx_s"].at[j], r["dx_r"].at[b], z_dev(j)).wait_send()


def finish_kernel(s, out_in, ig_in, w_ref, mom_ref, squ_ref, g_ref, ratio_ref, v_ref, vg_ref, mv_ref, sv_ref,
                  out_ref, ig_ref, gm_ref, gv_ref, nm_ref, ns_ref, nmv_ref, nsv_ref, nw_ref, nv_ref, grad):
    out_ref[...] = out_in[...]
    ig_ref[...] = ig_in[...]
    for m in range(4):
        for h in range(2):
            lo = s.lo[m] + h * s.half
            wide = min(s.half, s.lo[m] + s.width[m] - lo)
            grad[:, lo:lo + wide] = g_ref[m, h, 0, :, 0:wide].astype(f32)
    cols = s.lo[0] + HG
    g = grad[:, 0:cols]
    gm_ref[...] = g
    new_m, new_s, u = lamb_moments(g, mom_ref[...], squ_ref[...])
    nm_ref[...] = new_m
    ns_ref[...] = new_s
    w = w_ref[...]
    u = u + decay_rate * w
    col = lax.broadcasted_iota(jnp.int32, (1, cols), 1)
    ratio = jnp.broadcast_to(ratio_ref[5:6, 0:1], (1, cols))
    for k, edge in ((4, s.lo[0]), (3, s.lo[1]), (2, s.lo[2]), (1, 2 * s.g), (0, s.g)):
        ratio = jnp.where(col < edge, ratio_ref[k:k + 1, 0:1], ratio)
    nw_ref[...] = w - matrix_rate * ratio * u

    @pl.when(pl.program_id(0) == 0)
    def _():
        vg = vg_ref[...]
        gv_ref[...] = vg
        new_mv, new_sv, uv = lamb_moments(vg, mv_ref[...], sv_ref[...])
        nmv_ref[...] = new_mv
        nsv_ref[...] = new_sv
        nv_ref[...] = v_ref[...] - learn_rate * uv


def local(mesh_shape, tokens, cotangent, segment_ids, matrices, vectors, moment_mat, square_mat, moment_vec, square_vec):
    s = Sizes(mesh_shape, tokens.shape, segment_ids.shape[1])
    names, scratch = scratch_of(s)
    vmem = pl.BlockSpec(memory_space=pltpu.VMEM)
    S = jax.ShapeDtypeStruct
    output, input_grad, grads, vector_grad, ratio = pl.pallas_call(
        partial(layer_kernel, s, names),
        out_shape=(
            S(tokens.shape, bf16),
            S(tokens.shape, f32),
            S((4, 2, s.owners, s.rq, s.half), bf16),
            S(vectors.shape, f32),
            S((8, 128), f32),
        ),
        in_specs=[vmem] * 5 + [pl.BlockSpec(memory_space=pl.ANY)] * 2,
        out_specs=(vmem,) * 5,
        scratch_shapes=scratch,
        compiler_params=pltpu.CompilerParams(
            collective_id=0, has_side_effects=True, vmem_limit_bytes=60 * 2**20
        ),
        name="layer",
    )(tokens, cotangent, segment_ids, matrices, vectors, moment_mat, square_mat)

    steps = s.owners
    tok = s.t // steps

    def rows(a, n):
        return pl.BlockSpec((n, a.shape[1]), lambda i: (i, 0))

    def whole(a):
        return pl.BlockSpec(a.shape, lambda i: (0, 0))

    mat = rows(matrices, s.rq)
    vec = whole(vectors)
    return pl.pallas_call(
        partial(finish_kernel, s),
        grid=(steps,),
        out_shape=(
            S(tokens.shape, bf16),
            S(tokens.shape, f32),
            S(matrices.shape, f32),
            S(vectors.shape, f32),
            S(matrices.shape, f32),
            S(matrices.shape, f32),
            S(vectors.shape, f32),
            S(vectors.shape, f32),
            S(matrices.shape, f32),
            S(vectors.shape, f32),
        ),
        in_specs=[
            rows(tokens, tok), rows(tokens, tok), mat, mat, mat,
            pl.BlockSpec((4, 2, 1, s.rq, s.half), lambda i: (0, 0, i, 0, 0)),
            pl.BlockSpec((8, 128), lambda i: (0, 0)), vec, vec, vec, vec,
        ],
        out_specs=(rows(tokens, tok), rows(tokens, tok), mat, vec, mat, mat, vec, vec, mat, vec),
        scratch_shapes=[pltpu.VMEM((s.rq, s.lo[0] + HG), f32)],
        compiler_params=pltpu.CompilerParams(vmem_limit_bytes=40 * 2**20),
        name="finish",
    )(output, input_grad, matrices, moment_mat, square_mat, grads, ratio, vectors, vector_grad, moment_vec, square_vec)


def solution(mesh):
    return jax.shard_map(
        partial(local, dict(mesh.shape)),
        mesh=mesh,
        in_specs=(
            P(("rows", "blk"), "tp"),
            P(("rows", "blk"), "tp"),
            P("rows", None),
            P("tp", None),
            P(None, "tp"),
            P("tp", None),
            P("tp", None),
            P(None, "tp"),
            P(None, "tp"),
        ),
        out_specs=(
            P(("rows", "blk"), "tp"),
            P(("rows", "blk"), "tp"),
            P("tp", None),
            P(None, "tp"),
            P("tp", None),
            P("tp", None),
            P(None, "tp"),
            P(None, "tp"),
            P("tp", None),
            P(None, "tp"),
        ),
        check_vma=False,
    )
```

```python
import math
from functools import partial
from types import SimpleNamespace

import jax
import jax.numpy as jnp
from jax import lax
from jax.experimental import pallas as pl
from jax.experimental.pallas import tpu as pltpu
from jax.sharding import PartitionSpec as P

HD = 64
HG = 768
MESH = pl.DeviceIdType.MESH
f32 = jnp.float32
bf16 = jnp.bfloat16

eps_norm = 1e-12
beta_one = 0.9
beta_two = 0.999
adam_eps = 1e-06
step_count = 100.0
decay_rate = 0.01
learn_rate = 0.04
matrix_rate = 1.0
NEG = -1e30


def nn(a, b):
    return jnp.dot(a, b, preferred_element_type=f32)


def nt(a, b, **kw):
    return lax.dot_general(a, b, (((1,), (1,)), ((), ())), preferred_element_type=f32, **kw)


def eye(n, dtype=bf16):
    rows = lax.broadcasted_iota(jnp.int32, (n, n), 0)
    cols = lax.broadcasted_iota(jnp.int32, (n, n), 1)
    return (rows == cols).astype(dtype)


def flip(a):
    return nt(eye(a.shape[1]), a)


def split_bf16(a):
    high = a.astype(bf16)
    return high, (a - high.astype(f32)).astype(bf16)


def lane_sums(a):
    return nt(jnp.ones((8, a.shape[1]), bf16), a)[0:1]


def lane_sums_f32(a):
    high, low = split_bf16(a)
    return lane_sums(high) + lane_sums(low)


def lamb_moments(gradient, first_moment, second_moment):
    first_new = beta_one * first_moment + (1.0 - beta_one) * gradient
    second_new = beta_two * second_moment + (1.0 - beta_two) * gradient * gradient
    update = (
        first_new
        / (1.0 - beta_one**step_count)
        / (jnp.sqrt(second_new / (1.0 - beta_two**step_count)) + adam_eps)
    )
    return first_new, second_new, update


def gelu_pair(pre):
    half = 0.5 * (1.0 + lax.erf(pre * (2.0**-0.5)))
    slope = half + pre * (jnp.exp(-0.5 * pre * pre) * ((2.0 * math.pi) ** -0.5))
    return pre * half, slope


class Sizes:
    def __init__(self, mesh_shape, tokens, row_count):
        self.nr = mesh_shape["rows"]
        self.nb = mesh_shape["blk"]
        self.nt = mesh_shape["tp"]
        self.g, self.t = tokens
        self.d = self.g * self.nt
        self.heads = self.g // HD
        self.row = row_count
        self.ch = 128
        self.nc = self.t // self.ch
        self.wc = self.heads * self.ch
        self.half = HG // 2
        self.keep = self.nb <= 4
        owners = self.nb
        while self.nb % owners or self.g % (16 * owners):
            owners -= 1
        self.owners = owners
        self.rq = self.g // owners
        o = 3 * self.g
        self.lo = (o + self.d + HG, o + self.d, o, 0)
        self.width = (HG, HG, self.d, o)
        self.cols = self.lo[0] + HG
        self.vmem = (48 if self.keep else 62) * 2**20


def scratch_of(s):
    V = pltpu.VMEM
    D = pltpu.SemaphoreType.DMA
    T, G, nb, ntp, nc, CH = s.t, s.g, s.nb, s.nt, s.nc, s.ch
    kept = nb if s.keep else 1
    shapes = dict(
        w=V((G, s.cols), f32),
        v=V((12, G), f32),
        ids=V((1, s.row), jnp.int32),
        cot=V((G, T), bf16),
        mom=V((G, s.cols), f32),
        squ=V((G, s.cols), f32),
        xt=V((nb, G, T), bf16),
        xtf=V((ntp, G, T), bf16),
        wot=V((ntp, 2, s.d // 2, G), bf16),
        vec=V((ntp, 16, G), f32),
        ctxg=V((nc, s.d, CH), bf16),
        st1=V((nc, ntp, 8, CH), f32),
        dmgg=V((nc, s.d, CH), bf16),
        st2=V((nc, ntp, 8, CH), f32),
        nrm=V((ntp, 16, 128), f32),
        dxr=V((nb, G, T), bf16),
        gcore=V((4, G, s.half), bf16),
        gz=V((4, nb, s.rq, s.half), bf16),
        gfin=V((4, 2, s.owners, s.rq, s.half), bf16),
        vgc=V((16, G), f32),
        vgz=V((nb, 16, G), f32),
        dxs=V((nb, G, T), bf16),
        gsrc=V((4, 2, G, s.half), bf16),
        ghalf=V((4, s.owners, s.rq, s.half), bf16),
        vgl=V((16, G), f32),
        vgs=V((16, G), f32),
        x=V((kept, T, G), bf16),
        keys_t=V((kept, G, T), bf16),
        vals=V((kept, T, G), bf16),
        wq=V((G, G), bf16),
        wq_t=V((G, G), bf16),
        wk=V((G, G), bf16),
        wk_t=V((G, G), bf16),
        wv=V((G, G), bf16),
        wv_t=V((G, G), bf16),
        wo=V((G, s.d), bf16),
        wof=V((s.d, s.d), bf16),
        w1=V((G, HG), bf16),
        w1_t=V((HG, G), bf16),
        w2=V((G, HG), bf16),
        w2_t=V((HG, G), bf16),
        qz=V((nc, G, s.wc), bf16),
        dcz=V((nc, G, s.wc), bf16),
        idk=V((kept, T, 128), f32),
        ebuf=V((kept, nc, T, s.wc), bf16),
        mrec=V((kept, nc, 1, s.wc), f32),
        mrun=V((nc, 1, s.wc), f32),
        lrun=V((nc, 1, s.wc), f32),
        acc=V((G, T), f32),
        ctxl=V((G, T), bf16),
        delta=V((nc, 1, s.wc), f32),
        lse=V((nc, 1, s.wc), f32),
        n1f=V((nc, s.d, CH), f32),
        inv1=V((nc, 1, CH), f32),
        datt=V((s.d, T), bf16),
        act=V((HG, T), bf16),
        slope=V((HG, T), f32),
        dpre=V((HG, T), bf16),
        midl=V((G, T), bf16),
        dffn=V((G, T), bf16),
        h2=V((G, T), f32),
        cn2=V((G, T), f32),
        dmid=V((G, T), f32),
        dmn1=V((G, T), f32),
        dqt=V((G, T), f32),
        dkb=V((kept, T, G), f32),
        dvb=V((kept, T, G), f32),
        gkv=V((2, G, G), f32),
        vb=V((1, G), f32),
        dxo=V((G, T), f32),
        x_s=D((nb,)), x_r=D((nb,)),
        xtf_s=D((ntp,)), xtf_r=D((ntp,)),
        wot_s=D((ntp,)), wot_r=D((ntp,)),
        woc_s=D((ntp,)), woc_r=D((ntp,)),
        vec_s=D((ntp,)), vec_r=D((ntp,)),
        ctx_s=D((nc, ntp)), ctx_r=D((nc, ntp)),
        st1_s=D((nc, ntp)), st1_r=D((nc, ntp)),
        dmg_s=D((nc, ntp)), dmg_r=D((nc, ntp)),
        st2_s=D((nc, ntp)), st2_r=D((nc, ntp)),
        nrm_s=D((ntp,)), nrm_r=D((ntp,)),
        dx_s=D((nb,)), dx_r=D((nb,)),
        gc_s=D((4,)), gc_r=D((4,)),
        gz_s=D((4, nb)), gz_r=D((4, nb)),
        ga_s=D((4, nb)), ga_r=D((4, nb)),
        gd_s=D((4,)), gd_r=D((4,)),
        vc_s=D((1,)), vc_r=D((1,)),
        vz_s=D((nb,)), vz_r=D((nb,)),
        loc=D((8,)),
        put=D((8,)),
    )
    return list(shapes.keys()), list(shapes.values())


def layer_kernel(s, names, x_hbm, cot_hbm, ids_hbm, w_hbm, v_hbm, mom_hbm, squ_hbm,
                 out_hbm, ig_hbm, g_hbm, vg_hbm, ratio_hbm, out_ref, ig_ref, vg_ref, ratio_ref, *scratch):
    r = SimpleNamespace(**dict(zip(names, scratch)))
    T, G, nb, ntp, nc, CH = s.t, s.g, s.nb, s.nt, s.nc, s.ch
    c, b, t = lax.axis_index("rows"), lax.axis_index("blk"), lax.axis_index("tp")
    core = (1 - c, b, t)
    tx, ty = t % 2, t // 2
    tp_peers = [ty * 2 + (1 - tx), (1 - ty) * 2 + tx, 3 - t]
    if nb == 4:
        z_peers = [b + 1 - 2 * (b % 2), (b + 2) % 4, 3 - b]
    else:
        z_peers = [(b + o) % nb for o in range(1, nb)]

    def tp_dev(k):
        return (c, b, k)

    def z_dev(k):
        return (c, k, t)

    sent = []
    pending = {}

    def copy(src, dst, ssem, rsem, dev):
        return pltpu.make_async_remote_copy(
            src_ref=src, dst_ref=dst, send_sem=ssem, recv_sem=rsem, device_id=dev, device_id_type=MESH
        )

    def push(key, src, dst, ssem, rsem, dev, here, here_sem):
        one = copy(src, dst, ssem, rsem, dev)
        one.start()
        sent.append(one)
        pending[key] = copy(here, here, ssem, here_sem, dev)

    def arrive(key):
        pending.pop(key).wait_recv()

    def tp_push(key, at, sems):
        ssem, rsem = sems
        for i, k in enumerate(tp_peers):
            push((key, i), at(t), at(t), ssem(k), rsem(t), tp_dev(k), at(k), rsem(k))

    def tp_arrive(key):
        for i in range(ntp - 1):
            arrive((key, i))

    def sems(leaving, landing, *lead):
        return lambda k: leaving.at[lead + (k,)], lambda k: landing.at[lead + (k,)]

    def group(k):
        return pl.ds(pl.multiple_of(k * G, G), G)

    def load(i, src, dst):
        one = pltpu.make_async_copy(src, dst, r.loc.at[i])
        one.start()
        return one

    stored = []

    def store(src, dst):
        one = pltpu.make_async_copy(src, dst, r.put.at[len(stored)])
        one.start()
        stored.append(one)

    barrier = pltpu.get_barrier_semaphore()
    pl.semaphore_signal(barrier, 1, device_id=core, device_id_type=MESH)
    for k in tp_peers:
        pl.semaphore_signal(barrier, 1, device_id=tp_dev(k), device_id_type=MESH)
    for k in z_peers:
        pl.semaphore_signal(barrier, 1, device_id=z_dev(k), device_id_type=MESH)
    load_x = load(0, x_hbm, r.xt.at[b])
    load_v = load(1, v_hbm, r.v)
    load_ids = load(2, ids_hbm, r.ids)
    load_w = load(3, w_hbm, r.w)
    load_cot = load(4, cot_hbm, r.cot)
    load_m = load(5, mom_hbm, r.mom)
    load_s = load(6, squ_hbm, r.squ)
    load_x.wait()
    load_v.wait()
    load_ids.wait()
    r.xtf[t] = r.xt[b]
    r.vec[t, 0:12, :] = r.v[...]
    r.vec[t, 12:16, :] = jnp.zeros((4, G), f32)
    load_w.wait()
    w_ref = r.w
    w_o = w_ref[:, s.lo[2]:s.lo[2] + s.d].astype(bf16)
    r.wo[...] = w_o
    w_ot = flip(w_o).astype(bf16)
    r.wot[t, 0] = w_ot[:s.d // 2]
    r.wot[t, 1] = w_ot[s.d // 2:]
    pl.semaphore_wait(barrier, 1 + (ntp - 1) + (nb - 1))

    for i, j in enumerate(z_peers):
        push(("x", i), r.xt.at[b], r.xt.at[b], r.x_s.at[j], r.x_r.at[b], z_dev(j), r.xt.at[j], r.x_r.at[j])
    tp_push("vec", lambda k: r.vec.at[k], sems(r.vec_s, r.vec_r))
    tp_push("xtf", lambda k: r.xtf.at[k], sems(r.xtf_s, r.xtf_r))
    tp_push("wot", lambda k: r.wot.at[k, c], sems(r.wot_s, r.wot_r))

    w_q = w_ref[:, 0:G].astype(bf16)
    w_k = w_ref[:, G:2 * G].astype(bf16)
    w_v = w_ref[:, 2 * G:3 * G].astype(bf16)
    r.wq[...] = w_q
    r.wq_t[...] = flip(w_q).astype(bf16)
    r.wk[...] = w_k
    r.wk_t[...] = flip(w_k).astype(bf16)
    r.wv[...] = w_v
    r.wv_t[...] = flip(w_v).astype(bf16)

    def columns_of(vec):
        return nt(eye(G, f32), vec, precision=lax.Precision.HIGHEST)

    v_cols = columns_of(r.vec[t])

    def v_col(k):
        return v_cols[:, k:k + 1]

    bias_v_row = r.v[1:2, :]
    bias_v_col = v_col(1)

    scaling = HD**-0.5
    q_t = (nn(r.wq_t[...], r.xt[b]) + v_col(0)).astype(bf16)
    q_t = q_t.astype(f32) * scaling
    head_of = lax.broadcasted_iota(jnp.int32, (G, CH), 0) // HD

    def by_head(a):
        return jnp.concatenate([jnp.where(head_of == h, a, 0.0).astype(bf16) for h in range(s.heads)], axis=1)

    def lanes(k):
        return slice(k * CH, (k + 1) * CH)

    def head_rows(h):
        return slice(h * HD, (h + 1) * HD)

    for k in range(nc):
        r.qz[k] = by_head(q_t[:, lanes(k)])

    def ids_of(j):
        return r.ids[:, pl.ds(pl.multiple_of(j * T, 128), T)].astype(f32)

    def id_columns(j):
        ids = ids_of(j)
        high = jnp.floor(ids * (1.0 / 128.0))
        low = ids - 128.0 * high
        high, low = (jnp.broadcast_to(a, (128, T)).astype(bf16) for a in (high, low))
        return 128.0 * nt(eye(T), high) + nt(eye(T), low)

    if s.keep:
        for k in range(nb):
            r.idk[k] = id_columns(k)
    id_q = ids_of(b)

    r.mrun[...] = jnp.full((nc, 1, s.wc), NEG, f32)
    r.lrun[...] = jnp.zeros((nc, 1, s.wc), f32)
    r.acc[...] = jnp.zeros((G, T), f32)

    def same_doc(j, k):
        ids = r.idk[j] if s.keep else id_columns(j)
        return jnp.concatenate([ids == id_q[:, lanes(k)]] * s.heads, axis=1)

    def forward_block(j, after=None):
        x_jt = r.xt[j]
        x_j = flip(x_jt).astype(bf16)
        keys = nn(x_j, r.wk[...]).astype(bf16)
        vals_t = (nn(r.wv_t[...], x_jt) + bias_v_col).astype(bf16)
        for k in range(nc):
            score = jnp.where(same_doc(j, k), nn(keys, r.qz[k]), NEG)
            old = r.mrun[k]
            top = jnp.maximum(old, jnp.max(score, axis=0, keepdims=True))
            fade = jnp.exp(old - top)
            e = jnp.exp(score - top)
            r.lrun[k] = r.lrun[k] * fade + jnp.sum(e, axis=0, keepdims=True)
            e = e.astype(bf16)
            if s.keep:
                r.ebuf[j, k] = e
                r.mrec[j, k] = top
            r.mrun[k] = top
            for h in range(s.heads):
                rows = head_rows(h)
                r.acc[rows, lanes(k)] = r.acc[rows, lanes(k)] * fade[:, lanes(h)] + nn(vals_t[rows, :], e[:, lanes(h)])
            if after is not None:
                after(k)
        if s.keep:
            r.x[j] = x_j
            r.keys_t[j] = nn(r.wk_t[...], x_jt).astype(bf16)
            r.vals[j] = (nn(x_j, r.wv[...]) + bias_v_row).astype(bf16)

    forward_block(b)

    w_1 = w_ref[:, s.lo[1]:s.lo[1] + HG].astype(bf16)
    w_2 = w_ref[:, s.lo[0]:s.lo[0] + HG].astype(bf16)
    r.w1[...] = w_1
    r.w1_t[...] = flip(w_1).astype(bf16)
    r.w2[...] = w_2
    r.w2_t[...] = flip(w_2).astype(bf16)
    load_cot.wait()
    load_m.wait()
    load_s.wait()

    def context_ready(k):
        r.lse[k] = r.mrun[k] + jnp.log(r.lrun[k])
        inverse = 1.0 / r.lrun[k]
        parts = [r.acc[head_rows(h), lanes(k)] * inverse[:, lanes(h)] for h in range(s.heads)]
        context = jnp.concatenate(parts, axis=0)
        r.acc[:, lanes(k)] = context
        context = context.astype(bf16)
        r.ctxl[:, lanes(k)] = context
        r.ctxg[k, group(t), :] = context
        tp_push(("ctx", k), lambda d: r.ctxg.at[k, group(d), :], sems(r.ctx_s, r.ctx_r, k))

    if s.keep:
        for i, j in enumerate(z_peers):
            arrive(("x", i))
            forward_block(j, context_ready if i == nb - 2 else None)
    else:
        def forward_remote(o, _):
            j = (b + o) % nb
            copy(r.xt.at[j], r.xt.at[j], r.x_s.at[j], r.x_r.at[j], z_dev(j)).wait_recv()
            forward_block(j)
            return 0

        lax.fori_loop(1, nb, forward_remote, 0)
        for i in range(nb - 1):
            pending.pop(("x", i))
        for k in range(nc):
            context_ready(k)

    tp_arrive("wot")
    for i, k in enumerate(tp_peers):
        push(("woc", i), r.wot.at[k, c], r.wot.at[k, c], r.woc_s.at[k], r.woc_r.at[k], core, r.wot.at[k, 1 - c], r.woc_r.at[k])
    tp_arrive("vec")
    tp_arrive("xtf")
    out_bias = [columns_of(r.vec[k])[:, 2:3] for k in range(ntp)]
    tp_arrive("woc")
    for k in range(ntp):
        for h in range(2):
            r.wof[h * (s.d // 2):(h + 1) * (s.d // 2), k * G:(k + 1) * G] = r.wot[k, h]

    gain1 = v_col(3)
    bias_rows = HG // G
    hid_bias = jnp.concatenate([v_col(5 + k) for k in range(bias_rows)], axis=0)
    gain2 = v_col(6 + bias_rows)
    shift2 = v_col(7 + bias_rows)

    def forward_chunk(k):
        tp_arrive(("ctx", k))
        att = nn(r.wof[...], r.ctxg[k])
        hidden = [
            r.xtf[d][:, lanes(k)].astype(f32) + att[d * G:(d + 1) * G] + out_bias[d] for d in range(ntp)
        ]
        mean = sum(jnp.sum(a, axis=0, keepdims=True) for a in hidden) / s.d
        hidden = [a - mean for a in hidden]
        var = sum(jnp.sum(a * a, axis=0, keepdims=True) for a in hidden) / s.d
        inv = lax.rsqrt(var + eps_norm)
        r.inv1[k] = inv
        for d in range(ntp):
            r.n1f[k, d * G:(d + 1) * G, :] = hidden[d] * inv
        mid = r.n1f[k, group(t), :] * gain1 + v_col(4)
        mid_low = mid.astype(bf16)
        r.midl[:, lanes(k)] = mid_low
        act, slope = gelu_pair(nn(r.w1_t[...], mid_low) + hid_bias)
        act = act.astype(bf16)
        r.act[:, lanes(k)] = act
        r.slope[:, lanes(k)] = slope
        h2 = mid + nn(r.w2[...], act) + v_col(5 + bias_rows)
        r.h2[:, lanes(k)] = h2
        scaled = r.cot[:, lanes(k)].astype(f32) * gain2
        sum1 = jnp.sum(h2, axis=0, keepdims=True)
        h2c = h2 - sum1 / G
        sum2 = jnp.sum(h2c * h2c, axis=0, keepdims=True)
        sum3 = jnp.sum(scaled, axis=0, keepdims=True)
        sum4 = jnp.sum(scaled * h2c, axis=0, keepdims=True)
        r.st1[k, t] = jnp.concatenate([sum1, sum2, sum3, sum4, jnp.zeros((4, CH), f32)], axis=0)
        tp_push(("st1", k), lambda d: r.st1.at[k, d], sems(r.st1_s, r.st1_r, k))

    def backward_chunk(k):
        tp_arrive(("st1", k))
        stats = [r.st1[k, d] for d in range(ntp)]
        mean = sum(a[0:1] for a in stats) / s.d
        offs = [a[0:1] / G - mean for a in stats]
        var = sum(a[1:2] + G * o * o for a, o in zip(stats, offs)) / s.d
        inv = lax.rsqrt(var + eps_norm)
        first = sum(a[2:3] for a in stats) / s.d
        second = sum(a[3:4] + a[2:3] * o for a, o in zip(stats, offs)) * inv / s.d
        n2 = (r.h2[:, lanes(k)] - mean) * inv
        out_ref[:, lanes(k)] = (n2 * gain2 + shift2).astype(bf16)
        cot = r.cot[:, lanes(k)].astype(f32)
        r.cn2[:, lanes(k)] = cot * n2
        d2 = inv * (cot * gain2 - first - n2 * second)
        dffn = d2.astype(bf16)
        r.dffn[:, lanes(k)] = dffn
        dpre = (nn(r.w2_t[...], dffn) * r.slope[:, lanes(k)]).astype(bf16)
        r.dpre[:, lanes(k)] = dpre
        dmid = d2 + nn(r.w1[...], dpre)
        r.dmid[:, lanes(k)] = dmid
        n1 = r.n1f[k, group(t), :]
        r.dmn1[:, lanes(k)] = dmid * n1
        dmg = dmid * gain1
        part1 = jnp.sum(dmg, axis=0, keepdims=True)
        part2 = jnp.sum(dmg * n1, axis=0, keepdims=True)
        r.st2[k, t] = jnp.concatenate([part1, part2, jnp.zeros((6, CH), f32)], axis=0)
        r.dmgg[k, group(t), :] = dmg.astype(bf16)
        tp_push(("st2", k), lambda d: r.st2.at[k, d], sems(r.st2_s, r.st2_r, k))
        tp_push(("dmg", k), lambda d: r.dmgg.at[k, group(d), :], sems(r.dmg_s, r.dmg_r, k))

    for k in range(nc):
        forward_chunk(k)
    for k in range(nc):
        backward_chunk(k)
    store(out_ref, out_hbm)

    def sum_start(m):
        push(("gc", m), r.gsrc.at[m, 1 - c], r.gcore.at[m], r.gc_s.at[m], r.gc_r.at[m], core, r.gcore.at[m], r.gc_r.at[m])

    def when_owner(j, body):
        if s.owners < nb:
            pl.when(j < s.owners)(body)
        else:
            body()

    def to_owner(m, j):
        return copy(r.ghalf.at[m, j], r.gz.at[m, b], r.gz_s.at[m, j], r.gz_r.at[m, b], z_dev(j))

    def to_all(m, j):
        mine = r.gfin.at[m, c, b]
        return copy(mine, mine, r.ga_s.at[m, j], r.ga_r.at[m, b], z_dev(j))

    def sum_spread(m):
        arrive(("gc", m))
        both = (r.gsrc[m, c].astype(f32) + r.gcore[m].astype(f32)).astype(bf16)
        for k in range(s.owners):
            r.ghalf[m, k] = both[k * s.rq:(k + 1) * s.rq]
        for j in z_peers:
            when_owner(j, lambda: to_owner(m, j).start())

    def sum_own(m):
        def body():
            for j in z_peers:
                copy(r.gz.at[m, j], r.gz.at[m, j], r.gz_s.at[m, 0], r.gz_r.at[m, j], z_dev(j)).wait_recv()
            r.gz[m, b] = r.ghalf[m, b]
            total = r.gz[m, 0].astype(f32)
            for j in range(1, nb):
                total = total + r.gz[m, j].astype(f32)
            r.gfin[m, c, b] = total.astype(bf16)
            for j in z_peers:
                to_all(m, j).start()

        when_owner(b, body)

    def sum_share(m):
        for j in z_peers:
            slot = r.gfin.at[m, c, j]
            when_owner(j, lambda: copy(slot, slot, r.ga_s.at[m, 0], r.ga_r.at[m, j], z_dev(j)).wait_recv())
        push(("gd", m), r.gfin.at[m, c], r.gfin.at[m, c], r.gd_s.at[m], r.gd_r.at[m], core, r.gfin.at[m, 1 - c], r.gd_r.at[m])

    def sum_done(m):
        arrive(("gd", m))
        store(r.gfin.at[m], g_hbm.at[m])

    def sum_sends_done(m):
        for j in z_peers:
            when_owner(j, lambda: to_owner(m, j).wait_send())

        def body():
            for j in z_peers:
                to_all(m, j).wait_send()

        when_owner(b, body)

    def keep_grad(m, grad):
        r.gsrc[m, 0] = grad[:, 0:s.half].astype(bf16)
        r.gsrc[m, 1] = grad[:, s.half:].astype(bf16)

    keep_grad(0, nt(r.dffn[...], r.act[...]))
    sum_start(0)
    keep_grad(1, nt(r.midl[...], r.dpre[...]))
    sum_start(1)
    vgl = r.vgl
    vgl[12:16, :] = jnp.zeros((4, G), f32)
    vgl[3:4, :] = lane_sums_f32(r.dmn1[...])
    vgl[4:5, :] = lane_sums_f32(r.dmid[...])
    hid_sum = lane_sums(r.dpre[...])
    for k in range(bias_rows):
        vgl[5 + k:6 + k, :] = hid_sum[:, k * G:(k + 1) * G]
    vgl[5 + bias_rows:6 + bias_rows, :] = lane_sums(r.dffn[...])
    vgl[6 + bias_rows:7 + bias_rows, :] = lane_sums_f32(r.cn2[...])
    vgl[7 + bias_rows:8 + bias_rows, :] = lane_sums(r.cot[...])

    def context_chunk(k):
        tp_arrive(("st2", k))
        stats = [r.st2[k, d] for d in range(ntp)]
        first = sum(a[0:1] for a in stats) / s.d
        second = sum(a[1:2] for a in stats) / s.d
        inv = r.inv1[k]
        own = inv * (r.dmid[:, lanes(k)] * gain1 - first - r.n1f[k, group(t), :] * second)
        r.dxo[:, lanes(k)] = own
        tp_arrive(("dmg", k))
        for d in range(ntp):
            rows = slice(d * G, (d + 1) * G)
            part = inv * (r.dmgg[k, rows, :].astype(f32) - first - r.n1f[k, rows, :] * second)
            r.datt[rows, lanes(k)] = part.astype(bf16)
        dctx = nn(r.wo[...], r.datt[:, lanes(k)]).astype(bf16).astype(f32)
        r.dcz[k] = by_head(dctx)
        parts = [
            jnp.sum(dctx[head_rows(h)] * r.acc[head_rows(h), lanes(k)], axis=0, keepdims=True)
            for h in range(s.heads)
        ]
        r.delta[k] = jnp.concatenate(parts, axis=1)

    r.dqt[...] = jnp.zeros((G, T), f32)
    r.gkv[...] = jnp.zeros((2, G, G), f32)
    r.vb[...] = jnp.zeros((1, G), f32)

    def pair_terms(j, chunks):
        if s.keep:
            keys_t, vals = r.keys_t[j], r.vals[j]
        else:
            x_jt = r.xt[j]
            x_j = flip(x_jt).astype(bf16)
            keys_t = nn(r.wk_t[...], x_jt).astype(bf16)
            vals = (nn(x_j, r.wv[...]) + bias_v_row).astype(bf16)
            keys = nn(x_j, r.wk[...]).astype(bf16)
        dk = dv = None
        for k in chunks:
            if s.keep:
                p = r.ebuf[j, k].astype(f32) * jnp.exp(r.mrec[j, k] - r.lse[k])
            else:
                p = jnp.exp(jnp.where(same_doc(j, k), nn(keys, r.qz[k]), NEG) - r.lse[k])
            ds = (p * (nn(vals, r.dcz[k]) - r.delta[k])).astype(bf16)
            p = p.astype(bf16)
            for h in range(s.heads):
                r.dqt[head_rows(h), lanes(k)] += nn(keys_t[head_rows(h), :], ds[:, lanes(h)])
            dk_k, dv_k = nt(ds, r.qz[k]), nt(p, r.dcz[k])
            dk, dv = (dk_k, dv_k) if dk is None else (dk + dk_k, dv + dv_k)
        return dk, dv

    def finish_block(j, dk, dv):
        dk, dv = dk.astype(bf16), dv.astype(bf16)
        x_jt = r.xt[j]
        r.gkv[0] += nn(x_jt, dk)
        r.gkv[1] += nn(x_jt, dv)
        r.vb[...] += jnp.sum(dv.astype(f32), axis=0, keepdims=True)
        return nt(r.wk[...], dk) + nt(r.wv[...], dv)

    def dx_send(j):
        return copy(r.dxs.at[j], r.dxr.at[b], r.dx_s.at[j], r.dx_r.at[b], z_dev(j))

    if s.keep:
        context_chunk(0)
        sum_spread(0)
        sum_spread(1)
        for j in z_peers + [b]:
            r.dkb[j], r.dvb[j] = pair_terms(j, [0])
        for k in range(1, nc):
            context_chunk(k)
        keep_grad(2, nt(r.ctxl[...], r.datt[...]))
        sum_start(2)
        vgl[2:3, :] = lane_sums(r.dxo[...].astype(bf16))
        sum_own(0)
        sum_own(1)
        for i, j in enumerate(z_peers):
            dk, dv = pair_terms(j, range(1, nc))
            r.dxs[j] = finish_block(j, dk + r.dkb[j], dv + r.dvb[j]).astype(bf16)
            dx_send(j).start()
            if i == 0:
                sum_spread(2)
            if i == nb - 2:
                sum_share(0)
                sum_share(1)
        dk, dv = pair_terms(b, range(1, nc))
        r.dxo[...] += finish_block(b, dk + r.dkb[b], dv + r.dvb[b])
    else:
        for k in range(nc):
            context_chunk(k)
        keep_grad(2, nt(r.ctxl[...], r.datt[...]))
        sum_start(2)
        vgl[2:3, :] = lane_sums(r.dxo[...].astype(bf16))

        def backward_remote(o, _):
            j = (b + o) % nb
            r.dxs[j] = finish_block(j, *pair_terms(j, range(nc))).astype(bf16)
            dx_send(j).start()
            return 0

        lax.fori_loop(1, nb, backward_remote, 0)
        r.dxo[...] += finish_block(b, *pair_terms(b, range(nc)))
        for m in (0, 1, 2):
            sum_spread(m)
        sum_own(0)
        sum_own(1)
        sum_share(0)
        sum_share(1)
    dq_t = (r.dqt[...] * scaling).astype(bf16)
    r.gsrc[3, 0, :, 0:G] = nt(r.xt[b], dq_t).astype(bf16)
    r.gsrc[3, 0, :, G:2 * G] = r.gkv[0].astype(bf16)
    r.gsrc[3, 1, :, 0:G] = r.gkv[1].astype(bf16)
    r.gsrc[3, 1, :, G:2 * G] = jnp.zeros((G, G), bf16)
    sum_start(3)
    vgl[0:1, :] = lane_sums(dq_t)
    vgl[1:2, :] = r.vb[...]
    push(("vc",), vgl, r.vgc, r.vc_s.at[0], r.vc_r.at[0], core, r.vgc, r.vc_r.at[0])
    sum_spread(3)
    arrive(("vc",))
    r.vgs[...] = vgl[...] + r.vgc[...]
    r.vgz[b] = r.vgs[...]
    for i, j in enumerate(z_peers):
        push(("vz", i), r.vgs, r.vgz.at[b], r.vz_s.at[j], r.vz_r.at[b], z_dev(j), r.vgz.at[j], r.vz_r.at[j])
    r.dxo[...] += nn(r.wq[...], dq_t)
    sum_own(2)

    def norms_of(m):
        rows = []
        for h in range(2):
            lo = s.lo[m] + h * s.half
            wide = min(s.half, s.lo[m] + s.width[m] - lo)
            grad = jnp.concatenate([r.gfin[m, h, k] for k in range(s.owners)], axis=0)[:, :wide]
            w = w_ref[:, lo:lo + wide]
            _, _, u = lamb_moments(grad.astype(f32), r.mom[:, lo:lo + wide], r.squ[:, lo:lo + wide])
            u = u + decay_rate * w
            rows.append((jnp.sum(w * w, axis=0, keepdims=True), jnp.sum(u * u, axis=0, keepdims=True)))
        return rows

    def total(a):
        return jnp.broadcast_to(jnp.sum(a, axis=1, keepdims=True), (1, 128))

    sums = {}
    for m in (0, 1):
        sum_done(m)
        sums[m] = norms_of(m)
    sum_own(3)
    sum_share(2)
    for i, j in enumerate(z_peers):
        copy(r.dxr.at[j], r.dxr.at[j], r.dx_s.at[j], r.dx_r.at[j], z_dev(j)).wait_recv()
        r.dxo[...] += r.dxr[j].astype(f32)
    ig_ref[...] = r.dxo[...]
    store(ig_ref, ig_hbm)
    sum_done(2)
    sums[2] = norms_of(2)
    sum_share(3)
    for i in range(nb - 1):
        arrive(("vz", i))
    vg = r.vgz[0]
    for j in range(1, nb):
        vg = vg + r.vgz[j]
    vg_ref[...] = vg[0:12]
    store(vg_ref, vg_hbm)
    sum_done(3)
    sums[3] = norms_of(3)
    packed = []
    for which in range(2):
        lead = sums[3][0][which]
        packed += [total(lead[:, 0:G]), total(lead[:, G:2 * G]), total(sums[3][1][which])]
        packed += [total(sums[m][0][which] + sums[m][1][which]) for m in (2, 1, 0)]
        packed += [jnp.zeros((2, 128), f32)]
    r.nrm[t] = jnp.concatenate(packed, axis=0)
    tp_push("nrm", lambda k: r.nrm.at[k], sems(r.nrm_s, r.nrm_r))
    tp_arrive("nrm")
    norms = r.nrm[0]
    for k in range(1, ntp):
        norms = norms + r.nrm[k]
    ratio_ref[...] = jnp.sqrt(norms[0:8] / (norms[8:16] + 1e-12))
    store(ratio_ref, ratio_hbm)

    for one in sent:
        one.wait_send()
    for m in range(4):
        sum_sends_done(m)
    for j in z_peers:
        dx_send(j).wait_send()
    for one in stored:
        one.wait()


def finish_kernel(s, out_in, ig_in, w_ref, mom_ref, squ_ref, g_ref, ratio_ref, v_ref, vg_ref, mv_ref, sv_ref,
                  out_ref, ig_ref, gm_ref, gv_ref, nm_ref, ns_ref, nmv_ref, nsv_ref, nw_ref, nv_ref, grad):
    out_ref[...] = out_in[...]
    ig_ref[...] = ig_in[...]
    for m in range(4):
        for h in range(2):
            lo = s.lo[m] + h * s.half
            wide = min(s.half, s.lo[m] + s.width[m] - lo)
            grad[:, lo:lo + wide] = g_ref[m, h, 0, :, 0:wide].astype(f32)
    cols = s.cols
    g = grad[...]
    gm_ref[...] = g
    new_m, new_s, u = lamb_moments(g, mom_ref[...], squ_ref[...])
    nm_ref[...] = new_m
    ns_ref[...] = new_s
    w = w_ref[...]
    u = u + decay_rate * w
    col = lax.broadcasted_iota(jnp.int32, (1, cols), 1)
    ratio = jnp.broadcast_to(ratio_ref[5:6, 0:1], (1, cols))
    for k, edge in ((4, s.lo[0]), (3, s.lo[1]), (2, s.lo[2]), (1, 2 * s.g), (0, s.g)):
        ratio = jnp.where(col < edge, ratio_ref[k:k + 1, 0:1], ratio)
    nw_ref[...] = w - matrix_rate * ratio * u

    @pl.when(pl.program_id(0) == 0)
    def _():
        vg = vg_ref[...]
        gv_ref[...] = vg
        new_mv, new_sv, uv = lamb_moments(vg, mv_ref[...], sv_ref[...])
        nmv_ref[...] = new_mv
        nsv_ref[...] = new_sv
        nv_ref[...] = v_ref[...] - learn_rate * uv


def local(mesh_shape, tokens, cotangent, segment_ids, matrices, vectors, moment_mat, square_mat, moment_vec, square_vec):
    tokens, cotangent = tokens.T, cotangent.T
    s = Sizes(mesh_shape, tokens.shape, segment_ids.shape[1])
    names, scratch = scratch_of(s)
    hbm = pl.BlockSpec(memory_space=pltpu.HBM)
    S = jax.ShapeDtypeStruct
    small = [
        pltpu.VMEM(tokens.shape, bf16), pltpu.VMEM(tokens.shape, f32),
        pltpu.VMEM(vectors.shape, f32), pltpu.VMEM((8, 128), f32),
    ]
    given = (tokens, cotangent, segment_ids, matrices, vectors, moment_mat, square_mat)
    output, input_grad, grads, vector_grad, ratio = pl.pallas_call(
        partial(layer_kernel, s, names),
        out_shape=(
            S(tokens.shape, bf16),
            S(tokens.shape, f32),
            S((4, 2, s.owners, s.rq, s.half), bf16),
            S(vectors.shape, f32),
            S((8, 128), f32),
        ),
        in_specs=[hbm] * 7,
        out_specs=(hbm,) * 5,
        scratch_shapes=small + scratch,
        compiler_params=pltpu.CompilerParams(
            collective_id=0, has_side_effects=True, vmem_limit_bytes=s.vmem
        ),
        name="layer",
    )(*(pltpu.with_memory_space_constraint(a, pltpu.HBM) for a in given))

    steps = s.owners

    def rows(a, n):
        return pl.BlockSpec((n, a.shape[1]), lambda i: (i, 0))

    def whole(a):
        return pl.BlockSpec(a.shape, lambda i: (0, 0))

    mat = rows(matrices, s.rq)
    vec = whole(vectors)
    results = pl.pallas_call(
        partial(finish_kernel, s),
        grid=(steps,),
        out_shape=(
            S(tokens.shape, bf16),
            S(tokens.shape, f32),
            S(matrices.shape, f32),
            S(vectors.shape, f32),
            S(matrices.shape, f32),
            S(matrices.shape, f32),
            S(vectors.shape, f32),
            S(vectors.shape, f32),
            S(matrices.shape, f32),
            S(vectors.shape, f32),
        ),
        in_specs=[
            rows(tokens, s.rq), rows(tokens, s.rq), mat, mat, mat,
            pl.BlockSpec((4, 2, 1, s.rq, s.half), lambda i: (0, 0, i, 0, 0)),
            pl.BlockSpec((8, 128), lambda i: (0, 0)), vec, vec, vec, vec,
        ],
        out_specs=(rows(tokens, s.rq), rows(tokens, s.rq), mat, vec, mat, mat, vec, vec, mat, vec),
        scratch_shapes=[pltpu.VMEM((s.rq, s.lo[0] + HG), f32)],
        compiler_params=pltpu.CompilerParams(vmem_limit_bytes=40 * 2**20),
        name="finish",
    )(output, input_grad, matrices, moment_mat, square_mat, grads, ratio, vectors, vector_grad, moment_vec, square_vec)
    return (results[0].T, results[1].T) + tuple(results[2:])


def solution(mesh):
    return jax.shard_map(
        partial(local, dict(mesh.shape)),
        mesh=mesh,
        in_specs=(
            P(("rows", "blk"), "tp"),
            P(("rows", "blk"), "tp"),
            P("rows", None),
            P("tp", None),
            P(None, "tp"),
            P("tp", None),
            P("tp", None),
            P(None, "tp"),
            P(None, "tp"),
        ),
        out_specs=(
            P(("rows", "blk"), "tp"),
            P(("rows", "blk"), "tp"),
            P("tp", None),
            P(None, "tp"),
            P("tp", None),
            P("tp", None),
            P(None, "tp"),
            P(None, "tp"),
            P("tp", None),
            P(None, "tp"),
        ),
        check_vma=False,
    )
```

```python
import math
from functools import partial
from types import SimpleNamespace

import jax
import jax.numpy as jnp
from jax import lax
from jax.experimental import pallas as pl
from jax.experimental.pallas import tpu as pltpu
from jax.sharding import PartitionSpec as P

HD = 64
HG = 768
MESH = pl.DeviceIdType.MESH
f32 = jnp.float32
bf16 = jnp.bfloat16

eps_norm = 1e-12
beta_one = 0.9
beta_two = 0.999
adam_eps = 1e-06
step_count = 100.0
decay_rate = 0.01
learn_rate = 0.04
matrix_rate = 1.0
NEG = -1e30


def nn(a, b):
    return jnp.dot(a, b, preferred_element_type=f32)


def nt(a, b, **kw):
    return lax.dot_general(a, b, (((1,), (1,)), ((), ())), preferred_element_type=f32, **kw)


def eye(n, dtype=bf16):
    rows = lax.broadcasted_iota(jnp.int32, (n, n), 0)
    cols = lax.broadcasted_iota(jnp.int32, (n, n), 1)
    return (rows == cols).astype(dtype)


def flip(a):
    return nt(eye(a.shape[1]), a)


def split_bf16(a):
    high = a.astype(bf16)
    return high, (a - high.astype(f32)).astype(bf16)


def lane_sums(a):
    return nt(jnp.ones((8, a.shape[1]), bf16), a)[0:1]


def lane_sums_f32(a):
    high, low = split_bf16(a)
    return lane_sums(high) + lane_sums(low)


def lamb_moments(gradient, first_moment, second_moment):
    first_new = beta_one * first_moment + (1.0 - beta_one) * gradient
    second_new = beta_two * second_moment + (1.0 - beta_two) * gradient * gradient
    update = (
        first_new
        / (1.0 - beta_one**step_count)
        / (jnp.sqrt(second_new / (1.0 - beta_two**step_count)) + adam_eps)
    )
    return first_new, second_new, update


def gelu_pair(pre):
    half = 0.5 * (1.0 + lax.erf(pre * (2.0**-0.5)))
    slope = half + pre * (jnp.exp(-0.5 * pre * pre) * ((2.0 * math.pi) ** -0.5))
    return pre * half, slope


class Sizes:
    def __init__(self, mesh_shape, tokens, row_count):
        self.nr = mesh_shape["rows"]
        self.nb = mesh_shape["blk"]
        self.nt = mesh_shape["tp"]
        self.g, self.t = tokens
        self.d = self.g * self.nt
        self.heads = self.g // HD
        self.row = row_count
        self.ch = 128
        self.nc = self.t // self.ch
        self.wc = self.heads * self.ch
        self.half = HG // 2
        self.keep = self.nb <= 4
        self.line = self.nb == 4
        owners = self.nb
        while self.nb % owners or self.g % (16 * owners):
            owners -= 1
        self.owners = owners
        self.rq = self.g // owners
        tiles = 3 * self.g * self.g // (16 * 128)
        self.pr = -(-tiles // (self.nr * owners)) * 16
        self.ph = self.pr * owners
        self.pack = self.ph * self.nr
        o = 3 * self.g
        self.lo = (o + self.d + HG, o + self.d, o, 0)
        self.width = (HG, HG, self.d, o)
        self.cols = self.lo[0] + HG
        self.vmem = (48 if self.keep else 62) * 2**20


def scratch_of(s):
    V = pltpu.VMEM
    D = pltpu.SemaphoreType.DMA
    T, G, nb, ntp, nc, CH = s.t, s.g, s.nb, s.nt, s.nc, s.ch
    kept = nb if s.keep else 1
    shapes = dict(
        w=V((G, s.cols), f32),
        v=V((12, G), f32),
        ids=V((1, s.row), jnp.int32),
        cot=V((G, T), bf16),
        mom=V((G, s.cols), f32),
        squ=V((G, s.cols), f32),
        xt=V((nb, G, T), bf16),
        xtf=V((ntp, G, T), bf16),
        wot=V((ntp, 2, G // 2, s.d), bf16),
        vec=V((ntp, 16, G), f32),
        ctxg=V((nc, s.d, CH), bf16),
        st1=V((nc, ntp, 8, CH), f32),
        dmgg=V((nc, s.d, CH), bf16),
        st2=V((nc, ntp, 8, CH), f32),
        nrm=V((ntp, 8, 128), f32),
        dxr=V((nb, G, T), bf16),
        dxa=V((nb if s.line else 1, G, T), bf16),
        gcore=V((3, G, s.half), bf16),
        gend=V((3, G, s.half) if s.line else (1, 16, 128), bf16),
        gcross=V((3, G, s.half) if s.line else (1, 16, 128), bf16),
        gz=V((1, 1, 16, 128) if s.line else (3, nb, s.rq, s.half), bf16),
        gfin=V((3, 2, G, s.half), bf16),
        qcore=V((s.ph, 128), bf16),
        qz_in=V((nb, s.pr, 128), bf16),
        qfin=V((s.pack, 128), bf16),
        nq=V((s.nr, nb, 8, 128), f32),
        nqt=V((ntp, 8, 128), f32),
        upd=V((8, 128), f32),
        vgc=V((16, G), f32),
        vgz=V((nb, 16, G), f32),
        dxs=V((nb, G, T), bf16),
        gsrc=V((3, 2, G, s.half), bf16),
        ghalf=V((3, G, s.half), bf16),
        gmid=V((3, G, s.half) if s.line else (1, 16, 128), bf16),
        qsrc=V((s.pack, 128), bf16),
        qhalf=V((s.ph, 128), bf16),
        gq=V((2, G, s.half), bf16),
        pw=V((s.pack, 128), f32),
        pm=V((s.pack, 128), f32),
        ps=V((s.pack, 128), f32),
        vgl=V((16, G), f32),
        vgs=V((16, G), f32),
        x=V((kept, T, G), bf16),
        keys_t=V((kept, G, T), bf16),
        vals=V((kept, T, G), bf16),
        wq=V((G, G), bf16),
        wq_t=V((G, G), bf16),
        wk=V((G, G), bf16),
        wk_t=V((G, G), bf16),
        wv=V((G, G), bf16),
        wv_t=V((G, G), bf16),
        wof=V((s.d, s.d), bf16),
        w1=V((G, HG), bf16),
        w1_t=V((HG, G), bf16),
        w2=V((G, HG), bf16),
        w2_t=V((HG, G), bf16),
        qz=V((nc, G, s.wc), bf16),
        dcz=V((nc, G, s.wc), bf16),
        idk=V((kept, T, 128), f32),
        ebuf=V((kept, nc, T, s.wc), bf16),
        mrec=V((kept, nc, 1, s.wc), f32),
        mrun=V((nc, 1, s.wc), f32),
        lrun=V((nc, 1, s.wc), f32),
        acc=V((G, T), f32),
        ctxl=V((G, T), bf16),
        delta=V((nc, 1, s.wc), f32),
        lse=V((nc, 1, s.wc), f32),
        n1f=V((nc, s.d, CH), f32),
        inv1=V((nc, 1, CH), f32),
        datt=V((s.d, T), bf16),
        act=V((HG, T), bf16),
        slope=V((HG, T), f32),
        dpre=V((HG, T), bf16),
        midl=V((G, T), bf16),
        dffn=V((G, T), bf16),
        h2=V((G, T), f32),
        cn2=V((G, T), f32),
        dmid=V((G, T), f32),
        dmn1=V((G, T), f32),
        dqt=V((G, T), f32),
        dkb=V((kept, T, G), f32),
        dvb=V((kept, T, G), f32),
        gkv=V((2, G, G), f32),
        vb=V((1, G), f32),
        dxo=V((G, T), f32),
        x_s=D((nb,)), x_r=D((nb,)), xf_s=D((1,)),
        xtf_s=D((ntp,)), xtf_r=D((ntp,)),
        wot_s=D((ntp,)), wot_r=D((ntp,)),
        woc_s=D((ntp,)), woc_r=D((ntp,)),
        vec_s=D((ntp,)), vec_r=D((ntp,)),
        ctx_s=D((nc, ntp)), ctx_r=D((nc, ntp)),
        st1_s=D((nc, ntp)), st1_r=D((nc, ntp)),
        dmg_s=D((nc, ntp)), dmg_r=D((nc, ntp)),
        st2_s=D((nc, ntp)), st2_r=D((nc, ntp)),
        nrm_s=D((ntp,)), nrm_r=D((ntp,)),
        dx_s=D((nb,)), dx_r=D((nb,)),
        da_s=D((nb,)), da_r=D((nb,)),
        gc_s=D((3,)), gc_r=D((3,)),
        ge_s=D((3,)), ge_r=D((3,)),
        gx_s=D((3,)), gx_r=D((3,)),
        gz_s=D((3, nb)), gz_r=D((3, nb)),
        ga_s=D((3, nb)), ga_r=D((3, nb)),
        gd_s=D((3,)), gd_r=D((3,)),
        qc_s=D((1,)), qc_r=D((1,)),
        qz_s=D((nb,)), qz_r=D((nb,)),
        qa_s=D((nb,)), qa_r=D((nb,)),
        qd_s=D((1,)), qd_r=D((1,)),
        nq_s=D((s.nr, nb)), nq_r=D((s.nr, nb)),
        nqt_s=D((ntp,)), nqt_r=D((ntp,)),
        vc_s=D((1,)), vc_r=D((1,)),
        vz_s=D((nb,)), vz_r=D((nb,)),
        loc=D((8,)),
        put=D((8,)),
    )
    return list(shapes.keys()), list(shapes.values())


def layer_kernel(s, names, x_hbm, cot_hbm, ids_hbm, w_hbm, v_hbm, mom_hbm, squ_hbm,
                 out_hbm, ig_hbm, g_hbm, vg_hbm, ratio_hbm, out_ref, ig_ref, vg_ref, ratio_ref, *scratch):
    r = SimpleNamespace(**dict(zip(names, scratch)))
    T, G, nb, ntp, nc, CH = s.t, s.g, s.nb, s.nt, s.nc, s.ch
    c, b, t = lax.axis_index("rows"), lax.axis_index("blk"), lax.axis_index("tp")
    core = (1 - c, b, t)
    tx, ty = t % 2, t // 2
    tp_peers = [ty * 2 + (1 - tx), (1 - ty) * 2 + tx, 3 - t]
    if nb == 4:
        z_peers = [b + 1 - 2 * (b % 2), (b + 2) % 4, 3 - b]
    else:
        z_peers = [(b + o) % nb for o in range(1, nb)]

    def tp_dev(k):
        return (c, b, k)

    def z_dev(k):
        return (c, k, t)

    sent = []
    pending = {}

    def copy(src, dst, ssem, rsem, dev):
        return pltpu.make_async_remote_copy(
            src_ref=src, dst_ref=dst, send_sem=ssem, recv_sem=rsem, device_id=dev, device_id_type=MESH
        )

    def push(key, src, dst, ssem, rsem, dev, here, here_sem):
        one = copy(src, dst, ssem, rsem, dev)
        one.start()
        sent.append(one)
        pending[key] = copy(here, here, ssem, here_sem, dev)

    def arrive(key):
        pending.pop(key).wait_recv()

    sent_if = []

    def push_if(who, src, dst, ssem, rsem, dev):
        one = copy(src, dst, ssem, rsem, dev)
        pl.when(who)(lambda: one.start())
        sent_if.append((who, one))

    def tp_push(key, at, sems):
        ssem, rsem = sems
        for i, k in enumerate(tp_peers):
            push((key, i), at(t), at(t), ssem(k), rsem(t), tp_dev(k), at(k), rsem(k))

    def tp_arrive(key):
        for i in range(ntp - 1):
            arrive((key, i))

    def sems(leaving, landing, *lead):
        return lambda k: leaving.at[lead + (k,)], lambda k: landing.at[lead + (k,)]

    def group(k):
        return pl.ds(pl.multiple_of(k * G, G), G)

    def load(i, src, dst):
        one = pltpu.make_async_copy(src, dst, r.loc.at[i])
        one.start()
        return one

    stored = []

    def store(src, dst):
        one = pltpu.make_async_copy(src, dst, r.put.at[len(stored)])
        one.start()
        stored.append(one)

    barrier = pltpu.get_barrier_semaphore()
    pl.semaphore_signal(barrier, 1, device_id=core, device_id_type=MESH)
    for k in tp_peers:
        pl.semaphore_signal(barrier, 1, device_id=tp_dev(k), device_id_type=MESH)
    for k in z_peers:
        pl.semaphore_signal(barrier, 1, device_id=z_dev(k), device_id_type=MESH)
        pl.semaphore_signal(barrier, 1, device_id=(1 - c, k, t), device_id_type=MESH)
    load_x = load(0, x_hbm, r.xt.at[b])
    load_v = load(1, v_hbm, r.v)
    load_ids = load(2, ids_hbm, r.ids)
    load_w = load(3, w_hbm, r.w)
    load_cot = load(4, cot_hbm, r.cot)
    load_m = load(5, mom_hbm, r.mom)
    load_s = load(6, squ_hbm, r.squ)
    load_x.wait()
    load_v.wait()
    r.vec[t, 0:12, :] = r.v[...]
    r.vec[t, 12:16, :] = jnp.zeros((4, G), f32)
    pl.semaphore_wait(barrier, 1 + (ntp - 1) + 2 * (nb - 1))

    if s.line:
        inner = (b == 1) | (b == 2)
        outer = (b == 0) | (b == 3)
        for i in (1, 0):
            j = z_peers[i]
            push(("x", i), r.xt.at[b], r.xt.at[b], r.x_s.at[j], r.x_r.at[b], z_dev(j), r.xt.at[j], r.x_r.at[j])
        j = z_peers[2]
        push_if(inner, r.xt.at[b], r.xt.at[b], r.x_s.at[j], r.x_r.at[b], z_dev(j))
        pending[("x", 2)] = copy(r.xt.at[j], r.xt.at[j], r.x_s.at[j], r.x_r.at[j], z_dev(j))
    else:
        for i, j in enumerate(z_peers):
            push(("x", i), r.xt.at[b], r.xt.at[b], r.x_s.at[j], r.x_r.at[b], z_dev(j), r.xt.at[j], r.x_r.at[j])
    for i, k in enumerate(tp_peers):
        push(("xtf", i), r.xt.at[b], r.xtf.at[t], r.xtf_s.at[k], r.xtf_r.at[t], tp_dev(k), r.xtf.at[k], r.xtf_r.at[k])
    tp_push("vec", lambda k: r.vec.at[k], sems(r.vec_s, r.vec_r))
    load_w.wait()
    w_ref = r.w
    w_o = w_ref[:, s.lo[2]:s.lo[2] + s.d].astype(bf16)
    for h in range(2):
        r.wot[t, h] = w_o[h * (G // 2):(h + 1) * (G // 2)]
    tp_push("wot", lambda k: r.wot.at[k, c], sems(r.wot_s, r.wot_r))
    r.xtf[t] = r.xt[b]
    load_ids.wait()

    w_q = w_ref[:, 0:G].astype(bf16)
    w_k = w_ref[:, G:2 * G].astype(bf16)
    w_v = w_ref[:, 2 * G:3 * G].astype(bf16)
    r.wq[...] = w_q
    r.wq_t[...] = flip(w_q).astype(bf16)
    r.wk[...] = w_k
    r.wk_t[...] = flip(w_k).astype(bf16)
    r.wv[...] = w_v
    r.wv_t[...] = flip(w_v).astype(bf16)

    def columns_of(vec):
        return nt(eye(G, f32), vec, precision=lax.Precision.HIGHEST)

    v_cols = columns_of(r.vec[t])

    def v_col(k):
        return v_cols[:, k:k + 1]

    bias_v_row = r.v[1:2, :]
    bias_v_col = v_col(1)

    scaling = HD**-0.5
    q_t = (nn(r.wq_t[...], r.xt[b]) + v_col(0)).astype(bf16)
    q_t = q_t.astype(f32) * scaling
    head_of = lax.broadcasted_iota(jnp.int32, (G, CH), 0) // HD

    def by_head(a):
        return jnp.concatenate([jnp.where(head_of == h, a, 0.0).astype(bf16) for h in range(s.heads)], axis=1)

    def lanes(k):
        return slice(k * CH, (k + 1) * CH)

    def head_rows(h):
        return slice(h * HD, (h + 1) * HD)

    for k in range(nc):
        r.qz[k] = by_head(q_t[:, lanes(k)])

    def ids_of(j):
        return r.ids[:, pl.ds(pl.multiple_of(j * T, 128), T)].astype(f32)

    def id_columns(j):
        ids = ids_of(j)
        high = jnp.floor(ids * (1.0 / 128.0))
        low = ids - 128.0 * high
        high, low = (jnp.broadcast_to(a, (128, T)).astype(bf16) for a in (high, low))
        return 128.0 * nt(eye(T), high) + nt(eye(T), low)

    if s.keep:
        for k in range(nb):
            r.idk[k] = id_columns(k)
    id_q = ids_of(b)

    r.mrun[...] = jnp.full((nc, 1, s.wc), NEG, f32)
    r.lrun[...] = jnp.zeros((nc, 1, s.wc), f32)
    r.acc[...] = jnp.zeros((G, T), f32)

    def same_doc(j, k):
        ids = r.idk[j] if s.keep else id_columns(j)
        return jnp.concatenate([ids == id_q[:, lanes(k)]] * s.heads, axis=1)

    def forward_block(j, after=None):
        x_jt = r.xt[j]
        x_j = flip(x_jt).astype(bf16)
        keys = nn(x_j, r.wk[...]).astype(bf16)
        vals_t = (nn(r.wv_t[...], x_jt) + bias_v_col).astype(bf16)
        for k in range(nc):
            score = jnp.where(same_doc(j, k), nn(keys, r.qz[k]), NEG)
            old = r.mrun[k]
            top = jnp.maximum(old, jnp.max(score, axis=0, keepdims=True))
            fade = jnp.exp(old - top)
            e = jnp.exp(score - top)
            r.lrun[k] = r.lrun[k] * fade + jnp.sum(e, axis=0, keepdims=True)
            e = e.astype(bf16)
            if s.keep:
                r.ebuf[j, k] = e
                r.mrec[j, k] = top
            r.mrun[k] = top
            for h in range(s.heads):
                rows = head_rows(h)
                r.acc[rows, lanes(k)] = r.acc[rows, lanes(k)] * fade[:, lanes(h)] + nn(vals_t[rows, :], e[:, lanes(h)])
            if after is not None:
                after(k)
        if s.keep:
            r.x[j] = x_j
            r.keys_t[j] = nn(r.wk_t[...], x_jt).astype(bf16)
            r.vals[j] = (nn(x_j, r.wv[...]) + bias_v_row).astype(bf16)

    forward_block(b)
    if s.line:
        far = z_peers[1]
        here = copy(r.xt.at[far], r.xt.at[far], r.x_s.at[far], r.x_r.at[far], z_dev(far))
        on = copy(r.xt.at[far], r.xt.at[far], r.xf_s.at[0], r.x_r.at[far], z_dev(3 - far))

        @pl.when(inner)
        def _():
            here.wait_recv()
            on.start()

        sent_if.append((inner, on))

    w_1 = w_ref[:, s.lo[1]:s.lo[1] + HG].astype(bf16)
    w_2 = w_ref[:, s.lo[0]:s.lo[0] + HG].astype(bf16)
    r.w1[...] = w_1
    r.w1_t[...] = flip(w_1).astype(bf16)
    r.w2[...] = w_2
    r.w2_t[...] = flip(w_2).astype(bf16)
    load_cot.wait()
    load_m.wait()
    load_s.wait()

    def packed(a):
        parts = [a[:, k * 128:(k + 1) * 128] for k in range(3 * G // 128)]
        rest = a[:, 3 * G // 128 * 128:]
        parts += [jnp.concatenate([rest[:G // 2], rest[G // 2:]], axis=1)]
        parts += [jnp.zeros((s.pack - 3 * G * G // 128, 128), a.dtype)]
        return jnp.concatenate(parts, axis=0)

    def unpacked(a):
        parts = [a[k * G:(k + 1) * G] for k in range(3 * G // 128)]
        rest = a[3 * G // 128 * G:3 * G * G // 128]
        parts += [jnp.concatenate([rest[:, :64], rest[:, 64:]], axis=0)]
        return jnp.concatenate(parts, axis=1)

    r.pw[...] = packed(w_ref[:, 0:3 * G])
    r.pm[...] = packed(r.mom[:, 0:3 * G])
    r.ps[...] = packed(r.squ[:, 0:3 * G])

    def total(a):
        return jnp.broadcast_to(jnp.sum(jnp.sum(a, axis=0, keepdims=True), axis=1, keepdims=True), (1, 128))

    def columns(m):
        return w_ref[:, s.lo[m]:s.lo[m] + s.width[m]]

    lead = columns(3)
    weight_sums = [total(a * a) for a in (lead[:, 0:G], lead[:, G:2 * G], lead[:, 2 * G:], columns(2), columns(1), columns(0))]
    r.nrm[t] = jnp.concatenate(weight_sums + [jnp.zeros((2, 128), f32)], axis=0)
    tp_push("nrm", lambda k: r.nrm.at[k], sems(r.nrm_s, r.nrm_r))

    def context_ready(k):
        r.lse[k] = r.mrun[k] + jnp.log(r.lrun[k])
        inverse = 1.0 / r.lrun[k]
        parts = [r.acc[head_rows(h), lanes(k)] * inverse[:, lanes(h)] for h in range(s.heads)]
        context = jnp.concatenate(parts, axis=0)
        r.acc[:, lanes(k)] = context
        context = context.astype(bf16)
        r.ctxl[:, lanes(k)] = context
        r.ctxg[k, group(t), :] = context
        tp_push(("ctx", k), lambda d: r.ctxg.at[k, group(d), :], sems(r.ctx_s, r.ctx_r, k))

    if s.keep:
        for i, j in enumerate(z_peers):
            if s.line and i == 1:
                pl.when(outer)(lambda: pending.pop(("x", 1)).wait_recv())
            else:
                arrive(("x", i))
            forward_block(j, context_ready if i == nb - 2 else None)
    else:
        def forward_remote(o, _):
            j = (b + o) % nb
            copy(r.xt.at[j], r.xt.at[j], r.x_s.at[j], r.x_r.at[j], z_dev(j)).wait_recv()
            forward_block(j)
            return 0

        lax.fori_loop(1, nb, forward_remote, 0)
        for i in range(nb - 1):
            pending.pop(("x", i))
        for k in range(nc):
            context_ready(k)

    if s.keep:
        for j in range(nb):
            for k in range(nc):
                r.ebuf[j, k] = (r.ebuf[j, k].astype(f32) * jnp.exp(r.mrec[j, k] - r.lse[k])).astype(bf16)

    tp_arrive("wot")
    for i, k in enumerate(tp_peers):
        push(("woc", i), r.wot.at[k, c], r.wot.at[k, c], r.woc_s.at[k], r.woc_r.at[k], core, r.wot.at[k, 1 - c], r.woc_r.at[k])
    tp_arrive("vec")
    tp_arrive("xtf")
    tp_arrive("nrm")
    out_bias = [columns_of(r.vec[k])[:, 2:3] for k in range(ntp)]
    tp_arrive("woc")

    def output_rows(k):
        return jnp.concatenate([r.wot[k, 0], r.wot[k, 1]], axis=0)

    for k in range(ntp):
        r.wof[:, k * G:(k + 1) * G] = flip(output_rows(k)).astype(bf16)

    gain1 = v_col(3)
    bias_rows = HG // G
    hid_bias = jnp.concatenate([v_col(5 + k) for k in range(bias_rows)], axis=0)
    gain2 = v_col(6 + bias_rows)
    shift2 = v_col(7 + bias_rows)

    def forward_chunk(k):
        tp_arrive(("ctx", k))
        att = nn(r.wof[...], r.ctxg[k])
        hidden = [
            r.xtf[d][:, lanes(k)].astype(f32) + att[d * G:(d + 1) * G] + out_bias[d] for d in range(ntp)
        ]
        mean = sum(jnp.sum(a, axis=0, keepdims=True) for a in hidden) / s.d
        hidden = [a - mean for a in hidden]
        var = sum(jnp.sum(a * a, axis=0, keepdims=True) for a in hidden) / s.d
        inv = lax.rsqrt(var + eps_norm)
        r.inv1[k] = inv
        for d in range(ntp):
            r.n1f[k, d * G:(d + 1) * G, :] = hidden[d] * inv
        mid = r.n1f[k, group(t), :] * gain1 + v_col(4)
        mid_low = mid.astype(bf16)
        r.midl[:, lanes(k)] = mid_low
        act, slope = gelu_pair(nn(r.w1_t[...], mid_low) + hid_bias)
        act = act.astype(bf16)
        r.act[:, lanes(k)] = act
        r.slope[:, lanes(k)] = slope
        h2 = mid + nn(r.w2[...], act) + v_col(5 + bias_rows)
        r.h2[:, lanes(k)] = h2
        scaled = r.cot[:, lanes(k)].astype(f32) * gain2
        sum1 = jnp.sum(h2, axis=0, keepdims=True)
        h2c = h2 - sum1 / G
        sum2 = jnp.sum(h2c * h2c, axis=0, keepdims=True)
        sum3 = jnp.sum(scaled, axis=0, keepdims=True)
        sum4 = jnp.sum(scaled * h2c, axis=0, keepdims=True)
        r.st1[k, t] = jnp.concatenate([sum1, sum2, sum3, sum4, jnp.zeros((4, CH), f32)], axis=0)
        tp_push(("st1", k), lambda d: r.st1.at[k, d], sems(r.st1_s, r.st1_r, k))

    def backward_chunk(k):
        tp_arrive(("st1", k))
        stats = [r.st1[k, d] for d in range(ntp)]
        mean = sum(a[0:1] for a in stats) / s.d
        offs = [a[0:1] / G - mean for a in stats]
        var = sum(a[1:2] + G * o * o for a, o in zip(stats, offs)) / s.d
        inv = lax.rsqrt(var + eps_norm)
        first = sum(a[2:3] for a in stats) / s.d
        second = sum(a[3:4] + a[2:3] * o for a, o in zip(stats, offs)) * inv / s.d
        n2 = (r.h2[:, lanes(k)] - mean) * inv
        out_ref[:, lanes(k)] = (n2 * gain2 + shift2).astype(bf16)
        cot = r.cot[:, lanes(k)].astype(f32)
        r.cn2[:, lanes(k)] = cot * n2
        d2 = inv * (cot * gain2 - first - n2 * second)
        dffn = d2.astype(bf16)
        r.dffn[:, lanes(k)] = dffn
        dpre = (nn(r.w2_t[...], dffn) * r.slope[:, lanes(k)]).astype(bf16)
        r.dpre[:, lanes(k)] = dpre
        dmid = d2 + nn(r.w1[...], dpre)
        r.dmid[:, lanes(k)] = dmid
        n1 = r.n1f[k, group(t), :]
        r.dmn1[:, lanes(k)] = dmid * n1
        dmg = dmid * gain1
        part1 = jnp.sum(dmg, axis=0, keepdims=True)
        part2 = jnp.sum(dmg * n1, axis=0, keepdims=True)
        r.st2[k, t] = jnp.concatenate([part1, part2, jnp.zeros((6, CH), f32)], axis=0)
        r.dmgg[k, group(t), :] = dmg.astype(bf16)
        tp_push(("st2", k), lambda d: r.st2.at[k, d], sems(r.st2_s, r.st2_r, k))
        tp_push(("dmg", k), lambda d: r.dmgg.at[k, group(d), :], sems(r.dmg_s, r.dmg_r, k))

    for k in range(nc):
        forward_chunk(k)
    for k in range(nc):
        backward_chunk(k)
    store(out_ref, out_hbm)

    def sum_start(m):
        push(("gc", m), r.gsrc.at[m, 1 - c], r.gcore.at[m], r.gc_s.at[m], r.gc_r.at[m], core, r.gcore.at[m], r.gc_r.at[m])

    def add_low(a, b):
        return (a.astype(f32) + b.astype(f32)).astype(bf16)

    def when_owner(j, body):
        if s.owners < nb:
            pl.when(j < s.owners)(body)
        else:
            body()

    def quarter(j):
        return pl.ds(pl.multiple_of(j * s.rq, 16), s.rq)

    def to_owner(m, j):
        return r.ghalf.at[m, quarter(j)], r.gz.at[m, b], r.gz_s.at[m, j], r.gz_r.at[m, b], z_dev(j)

    def to_all(m, j):
        mine = r.gfin.at[m, c, quarter(b)]
        return mine, mine, r.ga_s.at[m, j], r.ga_r.at[m, b], z_dev(j)

    beside, across = (z_peers[0], z_peers[2]) if s.line else (None, None)

    def landed(ref, sem, dev):
        copy(ref, ref, sem, sem, dev).wait_recv()

    def sum_spread(m):
        arrive(("gc", m))
        r.ghalf[m] = add_low(r.gsrc[m, c], r.gcore[m])
        if s.line:
            push_if(outer, r.ghalf.at[m], r.gend.at[m], r.ge_s.at[m], r.ge_r.at[m], z_dev(beside))
        else:
            for j in z_peers:
                when_owner(j, lambda: copy(*to_owner(m, j)).start())

    def sum_cross(m):
        if s.line:
            one = copy(r.gmid.at[m], r.gcross.at[m], r.gx_s.at[m], r.gx_r.at[m], z_dev(across))

            @pl.when(inner)
            def _():
                landed(r.gend.at[m], r.ge_r.at[m], z_dev(beside))
                r.gmid[m] = add_low(r.ghalf[m], r.gend[m])
                one.start()

            sent_if.append((inner, one))

    def sum_own(m):
        if s.line:
            mine = r.gfin.at[m, c]
            one = copy(mine, mine, r.ga_s.at[m, 0], r.ga_r.at[m, 0], z_dev(beside))

            @pl.when(inner)
            def _():
                landed(r.gcross.at[m], r.gx_r.at[m], z_dev(across))
                r.gfin[m, c] = add_low(r.gmid[m], r.gcross[m])
                one.start()
                r.upd[m:m + 1, :] = norm_of(m)

            sent_if.append((inner, one))
        else:
            def body():
                for j in z_peers:
                    landed(r.gz.at[m, j], r.gz_r.at[m, j], z_dev(j))
                r.gz[m, b] = r.ghalf[m, quarter(b)]
                sums = r.gz[m, 0].astype(f32)
                for j in range(1, nb):
                    sums = sums + r.gz[m, j].astype(f32)
                r.gfin[m, c, quarter(b)] = sums.astype(bf16)
                for j in z_peers:
                    copy(*to_all(m, j)).start()
                r.upd[m:m + 1, :] = norm_of(m, b)

            when_owner(b, body)

    def norm_of(m, piece=None):
        here = slice(None) if piece is None else quarter(piece)

        def own_half(ref):
            first, second = (ref[here, s.lo[m] + h * s.half:s.lo[m] + (h + 1) * s.half] for h in range(2))
            return jnp.where(c == 0, first, second)

        _, _, u = lamb_moments(r.gfin[m, c, here].astype(f32), own_half(r.mom), own_half(r.squ))
        u = u + decay_rate * own_half(w_ref)
        return total(u * u)

    def sum_share(m):
        if s.line:
            pl.when(outer)(lambda: landed(r.gfin.at[m, c], r.ga_r.at[m, 0], z_dev(beside)))
        else:
            for j in z_peers:
                when_owner(j, lambda: landed(r.gfin.at[m, c, quarter(j)], r.ga_r.at[m, j], z_dev(j)))
        push(("gd", m), r.gfin.at[m, c], r.gfin.at[m, c], r.gd_s.at[m], r.gd_r.at[m], core, r.gfin.at[m, 1 - c], r.gd_r.at[m])

    def sum_done(m):
        arrive(("gd", m))
        store(r.gfin.at[m], g_hbm.at[m])

    def sum_sends_done(m):
        for j in z_peers:
            when_owner(j, lambda: copy(*to_owner(m, j)).wait_send())

        def body():
            for j in z_peers:
                copy(*to_all(m, j)).wait_send()

        when_owner(b, body)

    def keep_grad(m, grad):
        r.gsrc[m, 0] = grad[:, 0:s.half].astype(bf16)
        r.gsrc[m, 1] = grad[:, s.half:].astype(bf16)

    keep_grad(0, nt(r.dffn[...], r.act[...]))
    sum_start(0)
    keep_grad(1, nt(r.midl[...], r.dpre[...]))
    sum_start(1)
    vgl = r.vgl
    vgl[12:16, :] = jnp.zeros((4, G), f32)
    vgl[3:4, :] = lane_sums_f32(r.dmn1[...])
    vgl[4:5, :] = lane_sums_f32(r.dmid[...])
    hid_sum = lane_sums(r.dpre[...])
    for k in range(bias_rows):
        vgl[5 + k:6 + k, :] = hid_sum[:, k * G:(k + 1) * G]
    vgl[5 + bias_rows:6 + bias_rows, :] = lane_sums(r.dffn[...])
    vgl[6 + bias_rows:7 + bias_rows, :] = lane_sums_f32(r.cn2[...])
    vgl[7 + bias_rows:8 + bias_rows, :] = lane_sums(r.cot[...])
    r.upd[...] = jnp.zeros((8, 128), f32)
    if s.line:
        sum_spread(0)
        sum_spread(1)

    def context_chunk(k):
        tp_arrive(("st2", k))
        stats = [r.st2[k, d] for d in range(ntp)]
        first = sum(a[0:1] for a in stats) / s.d
        second = sum(a[1:2] for a in stats) / s.d
        inv = r.inv1[k]
        own = inv * (r.dmid[:, lanes(k)] * gain1 - first - r.n1f[k, group(t), :] * second)
        r.dxo[:, lanes(k)] = own
        tp_arrive(("dmg", k))
        for d in range(ntp):
            rows = slice(d * G, (d + 1) * G)
            part = inv * (r.dmgg[k, rows, :].astype(f32) - first - r.n1f[k, rows, :] * second)
            r.datt[rows, lanes(k)] = part.astype(bf16)
        dctx = nn(output_rows(t), r.datt[:, lanes(k)]).astype(bf16).astype(f32)
        r.dcz[k] = by_head(dctx)
        parts = [
            jnp.sum(dctx[head_rows(h)] * r.acc[head_rows(h), lanes(k)], axis=0, keepdims=True)
            for h in range(s.heads)
        ]
        r.delta[k] = jnp.concatenate(parts, axis=1)

    r.dqt[...] = jnp.zeros((G, T), f32)
    r.gkv[...] = jnp.zeros((2, G, G), f32)
    r.vb[...] = jnp.zeros((1, G), f32)

    def pair_terms(j, chunks):
        if s.keep:
            keys_t, vals = r.keys_t[j], r.vals[j]
        else:
            x_jt = r.xt[j]
            x_j = flip(x_jt).astype(bf16)
            keys_t = nn(r.wk_t[...], x_jt).astype(bf16)
            vals = (nn(x_j, r.wv[...]) + bias_v_row).astype(bf16)
            keys = nn(x_j, r.wk[...]).astype(bf16)
        dk = dv = None
        for k in chunks:
            if s.keep:
                p_low = r.ebuf[j, k]
                p = p_low.astype(f32)
            else:
                p = jnp.exp(jnp.where(same_doc(j, k), nn(keys, r.qz[k]), NEG) - r.lse[k])
                p_low = p.astype(bf16)
            ds = (p * (nn(vals, r.dcz[k]) - r.delta[k])).astype(bf16)
            for h in range(s.heads):
                r.dqt[head_rows(h), lanes(k)] += nn(keys_t[head_rows(h), :], ds[:, lanes(h)])
            dk_k, dv_k = nt(ds, r.qz[k]), nt(p_low, r.dcz[k])
            dk, dv = (dk_k, dv_k) if dk is None else (dk + dk_k, dv + dv_k)
        return dk, dv

    def finish_block(j, dk, dv):
        dk, dv = dk.astype(bf16), dv.astype(bf16)
        x_jt = r.xt[j]
        r.gkv[0] += nn(x_jt, dk)
        r.gkv[1] += nn(x_jt, dv)
        r.vb[...] += jnp.sum(dv.astype(f32), axis=0, keepdims=True)
        return nt(r.wk[...], dk) + nt(r.wv[...], dv)

    def dx_send(j):
        return r.dxs.at[j], r.dxr.at[b], r.dx_s.at[j], r.dx_r.at[b], z_dev(j)

    if s.keep:
        context_chunk(0)
        for j in z_peers + [b]:
            r.dkb[j], r.dvb[j] = pair_terms(j, [0])
        for k in range(1, nc):
            context_chunk(k)
        keep_grad(2, nt(r.ctxl[...], r.datt[...]))
        sum_start(2)
        vgl[2:3, :] = lane_sums(r.dxo[...].astype(bf16))
        for i in (1, 2, 0):
            j = z_peers[i]
            dk, dv = pair_terms(j, range(1, nc))
            r.dxs[j] = finish_block(j, dk + r.dkb[j], dv + r.dvb[j]).astype(bf16)
            if i == 0:
                push(("dx", 0), *dx_send(j), r.dxr.at[j], r.dx_r.at[j])
                sum_cross(1)
            else:
                push_if(outer, r.dxs.at[j], r.dxa.at[j], r.da_s.at[j], r.da_r.at[j], z_dev(beside))
                if i == 1:
                    sum_spread(2)
                else:
                    sum_cross(0)
        dk, dv = pair_terms(b, range(1, nc))
        r.dxo[...] += finish_block(b, dk + r.dkb[b], dv + r.dvb[b])
    else:
        for k in range(nc):
            context_chunk(k)
        keep_grad(2, nt(r.ctxl[...], r.datt[...]))
        sum_start(2)
        vgl[2:3, :] = lane_sums(r.dxo[...].astype(bf16))

        def backward_remote(o, _):
            j = (b + o) % nb
            r.dxs[j] = finish_block(j, *pair_terms(j, range(nc))).astype(bf16)
            copy(*dx_send(j)).start()
            return 0

        lax.fori_loop(1, nb, backward_remote, 0)
        r.dxo[...] += finish_block(b, *pair_terms(b, range(nc)))
        for m in (0, 1, 2):
            sum_spread(m)
        sum_own(0)
        sum_own(1)
    dq_t = (r.dqt[...] * scaling).astype(bf16)
    r.qsrc[...] = packed(jnp.concatenate([nt(r.xt[b], dq_t), r.gkv[0], r.gkv[1]], axis=1)).astype(bf16)

    def part(k, n):
        return pl.ds(pl.multiple_of(k * n, 16), n)

    push("qc", r.qsrc.at[part(1 - c, s.ph)], r.qcore, r.qc_s.at[0], r.qc_r.at[0], core, r.qcore, r.qc_r.at[0])
    vgl[0:1, :] = lane_sums(dq_t)
    vgl[1:2, :] = r.vb[...]
    push("vc", vgl, r.vgc, r.vc_s.at[0], r.vc_r.at[0], core, r.vgc, r.vc_r.at[0])
    arrive("qc")
    r.qhalf[...] = add_low(r.qsrc[part(c, s.ph)], r.qcore[...])

    def q_to_owner(j):
        return r.qhalf.at[part(j, s.pr)], r.qz_in.at[b], r.qz_s.at[j], r.qz_r.at[b], z_dev(j)

    def q_to_all(j):
        mine = r.qfin.at[part(c * s.owners + b, s.pr)]
        return mine, mine, r.qa_s.at[j], r.qa_r.at[b], z_dev(j)

    for j in z_peers:
        when_owner(j, lambda: copy(*q_to_owner(j)).start())
    arrive("vc")
    r.vgs[...] = vgl[...] + r.vgc[...]
    r.vgz[b] = r.vgs[...]
    for i, j in enumerate(z_peers):
        push(("vz", i), r.vgs, r.vgz.at[b], r.vz_s.at[j], r.vz_r.at[b], z_dev(j), r.vgz.at[j], r.vz_r.at[j])
    if s.line:
        sum_own(0)
        sum_cross(2)
        sum_own(1)

        @pl.when(inner)
        def _():
            for i in (1, 2):
                j = z_peers[i]
                landed(r.dxa.at[j], r.da_r.at[j], z_dev(beside))
                r.dxs[j] = add_low(r.dxs[j], r.dxa[j])
                copy(*dx_send(j)).start()

        for i in (1, 2):
            sent_if.append((inner, copy(*dx_send(z_peers[i]))))
    else:
        sum_own(2)
    r.dxo[...] += nn(r.wq[...], dq_t)

    mine = jnp.zeros((s.pr, 128), f32)
    for j in z_peers:
        when_owner(b, lambda: landed(r.qz_in.at[j], r.qz_r.at[j], z_dev(j)))
    r.qz_in[b] = r.qhalf[part(b % s.owners, s.pr)]
    for j in range(nb):
        mine = mine + r.qz_in[j].astype(f32)
    mine = mine.astype(bf16)

    @partial(when_owner, b)
    def _():
        r.qfin[part(c * s.owners + b, s.pr), :] = mine
        for j in z_peers:
            copy(*q_to_all(j)).start()

    first_row = (c * s.owners + b % s.owners) * s.pr
    here = part(c * s.owners + b % s.owners, s.pr)
    _, _, u = lamb_moments(mine.astype(f32), r.pm[here, :], r.ps[here, :])
    u = u + decay_rate * r.pw[here, :]
    u = jnp.where(b < s.owners, u * u, 0.0)
    row = first_row + lax.broadcasted_iota(jnp.int32, (s.pr, 128), 0)
    lane = lax.broadcasted_iota(jnp.int32, (s.pr, 128), 1)
    column = row // G * 128 + lane
    is_q = column < G
    is_k = (column >= G) & (column < 2 * G)
    is_v = column >= 2 * G
    lead = [total(jnp.where(a, u, 0.0)) for a in (is_q, is_k, is_v)]
    if s.line:
        sum_own(2)
        rest = jnp.where(b == 1, r.upd[...], 0.0)
    else:
        rest = r.upd[...]
    r.nq[c, b] = jnp.concatenate(lead + [rest[m:m + 1] for m in (2, 1, 0)] + [jnp.zeros((2, 128), f32)], axis=0)
    same_tp = [(1 - c, b)] + [(i, j) for j in z_peers for i in (c, 1 - c)]
    for n, (i, j) in enumerate(same_tp):
        push(("nq", n), r.nq.at[c, b], r.nq.at[c, b], r.nq_s.at[i, j], r.nq_r.at[c, b], (i, j, t), r.nq.at[i, j], r.nq_r.at[i, j])
    sum_share(0)
    sum_share(1)
    if s.line:
        other = jnp.where(b < 2, 2, 1)
        arrive(("dx", 0))
        landed(r.dxr.at[other], r.dx_r.at[other], z_dev(other))
        r.dxo[...] += r.dxr[beside].astype(f32) + r.dxr[other].astype(f32)
    else:
        for j in z_peers:
            landed(r.dxr.at[j], r.dx_r.at[j], z_dev(j))
            r.dxo[...] += r.dxr[j].astype(f32)
    ig_ref[...] = r.dxo[...]
    store(ig_ref, ig_hbm)
    sum_share(2)
    for n in range(len(same_tp)):
        arrive(("nq", n))
    sums = jnp.zeros((8, 128), f32)
    for i in range(s.nr):
        for j in range(nb):
            sums = sums + r.nq[i, j]
    r.nqt[t] = sums
    tp_push("nqt", lambda k: r.nqt.at[k], sems(r.nqt_s, r.nqt_r))
    for j in z_peers:
        when_owner(j, lambda: landed(r.qfin.at[part(c * s.owners + j, s.pr)], r.qa_r.at[j], z_dev(j)))
    push("qd", r.qfin.at[part(c, s.ph)], r.qfin.at[part(c, s.ph)], r.qd_s.at[0], r.qd_r.at[0], core, r.qfin.at[part(1 - c, s.ph)], r.qd_r.at[0])
    for m in range(3):
        sum_done(m)
    for i in range(nb - 1):
        arrive(("vz", i))
    vg = r.vgz[0]
    for j in range(1, nb):
        vg = vg + r.vgz[j]
    vg_ref[...] = vg[0:12]
    store(vg_ref, vg_hbm)
    arrive("qd")
    lead = unpacked(r.qfin[...])
    r.gq[0] = lead[:, 0:s.half]
    r.gq[1, :, 0:G] = lead[:, s.half:]
    r.gq[1, :, G:2 * G] = jnp.zeros((G, G), bf16)
    store(r.gq, g_hbm.at[3])
    tp_arrive("nqt")
    norms = r.nrm[0]
    lead = r.nqt[0]
    for k in range(1, ntp):
        norms = norms + r.nrm[k]
        lead = lead + r.nqt[k]
    ratio_ref[...] = jnp.sqrt(norms / (lead + 1e-12))
    store(ratio_ref, ratio_hbm)

    for one in sent:
        one.wait_send()
    for who, one in sent_if:
        pl.when(who)(lambda: one.wait_send())
    if not s.line:
        for m in range(3):
            sum_sends_done(m)
        for j in z_peers:
            copy(*dx_send(j)).wait_send()
    for j in z_peers:
        when_owner(j, lambda: copy(*q_to_owner(j)).wait_send())

    @partial(when_owner, b)
    def _():
        for j in z_peers:
            copy(*q_to_all(j)).wait_send()

    for one in stored:
        one.wait()


def finish_kernel(s, out_in, ig_in, w_ref, mom_ref, squ_ref, g_ref, ratio_ref, v_ref, vg_ref, mv_ref, sv_ref,
                  out_ref, ig_ref, gm_ref, gv_ref, nm_ref, ns_ref, nmv_ref, nsv_ref, nw_ref, nv_ref, grad):
    out_ref[...] = out_in[...]
    ig_ref[...] = ig_in[...]
    for m in range(4):
        for h in range(2):
            lo = s.lo[m] + h * s.half
            wide = min(s.half, s.lo[m] + s.width[m] - lo)
            grad[:, lo:lo + wide] = g_ref[m, h, :, 0:wide].astype(f32)
    cols = s.cols
    g = grad[...]
    gm_ref[...] = g
    new_m, new_s, u = lamb_moments(g, mom_ref[...], squ_ref[...])
    nm_ref[...] = new_m
    ns_ref[...] = new_s
    w = w_ref[...]
    u = u + decay_rate * w
    col = lax.broadcasted_iota(jnp.int32, (1, cols), 1)
    ratio = jnp.broadcast_to(ratio_ref[5:6, 0:1], (1, cols))
    for k, edge in ((4, s.lo[0]), (3, s.lo[1]), (2, s.lo[2]), (1, 2 * s.g), (0, s.g)):
        ratio = jnp.where(col < edge, ratio_ref[k:k + 1, 0:1], ratio)
    nw_ref[...] = w - matrix_rate * ratio * u

    @pl.when(pl.program_id(0) == 0)
    def _():
        vg = vg_ref[...]
        gv_ref[...] = vg
        new_mv, new_sv, uv = lamb_moments(vg, mv_ref[...], sv_ref[...])
        nmv_ref[...] = new_mv
        nsv_ref[...] = new_sv
        nv_ref[...] = v_ref[...] - learn_rate * uv


def local(mesh_shape, tokens, cotangent, segment_ids, matrices, vectors, moment_mat, square_mat, moment_vec, square_vec):
    tokens, cotangent = tokens.T, cotangent.T
    s = Sizes(mesh_shape, tokens.shape, segment_ids.shape[1])
    names, scratch = scratch_of(s)
    hbm = pl.BlockSpec(memory_space=pltpu.HBM)
    S = jax.ShapeDtypeStruct
    small = [
        pltpu.VMEM(tokens.shape, bf16), pltpu.VMEM(tokens.shape, f32),
        pltpu.VMEM(vectors.shape, f32), pltpu.VMEM((8, 128), f32),
    ]
    given = (tokens, cotangent, segment_ids, matrices, vectors, moment_mat, square_mat)
    output, input_grad, grads, vector_grad, ratio = pl.pallas_call(
        partial(layer_kernel, s, names),
        out_shape=(
            S(tokens.shape, bf16),
            S(tokens.shape, f32),
            S((4, 2, s.g, s.half), bf16),
            S(vectors.shape, f32),
            S((8, 128), f32),
        ),
        in_specs=[hbm] * 7,
        out_specs=(hbm,) * 5,
        scratch_shapes=small + scratch,
        compiler_params=pltpu.CompilerParams(
            collective_id=0, has_side_effects=True, vmem_limit_bytes=s.vmem
        ),
        name="layer",
    )(*(pltpu.with_memory_space_constraint(a, pltpu.HBM) for a in given))

    steps = s.owners

    def rows(a, n):
        return pl.BlockSpec((n, a.shape[1]), lambda i: (i, 0))

    def whole(a):
        return pl.BlockSpec(a.shape, lambda i: (0, 0))

    mat = rows(matrices, s.rq)
    vec = whole(vectors)
    results = pl.pallas_call(
        partial(finish_kernel, s),
        grid=(steps,),
        out_shape=(
            S(tokens.shape, bf16),
            S(tokens.shape, f32),
            S(matrices.shape, f32),
            S(vectors.shape, f32),
            S(matrices.shape, f32),
            S(matrices.shape, f32),
            S(vectors.shape, f32),
            S(vectors.shape, f32),
            S(matrices.shape, f32),
            S(vectors.shape, f32),
        ),
        in_specs=[
            rows(tokens, s.rq), rows(tokens, s.rq), mat, mat, mat,
            pl.BlockSpec((4, 2, s.rq, s.half), lambda i: (0, 0, i, 0)),
            pl.BlockSpec((8, 128), lambda i: (0, 0)), vec, vec, vec, vec,
        ],
        out_specs=(rows(tokens, s.rq), rows(tokens, s.rq), mat, vec, mat, mat, vec, vec, mat, vec),
        scratch_shapes=[pltpu.VMEM((s.rq, s.lo[0] + HG), f32)],
        compiler_params=pltpu.CompilerParams(vmem_limit_bytes=40 * 2**20),
        name="finish",
    )(output, input_grad, matrices, moment_mat, square_mat, grads, ratio, vectors, vector_grad, moment_vec, square_vec)
    return (results[0].T, results[1].T) + tuple(results[2:])


def solution(mesh):
    return jax.shard_map(
        partial(local, dict(mesh.shape)),
        mesh=mesh,
        in_specs=(
            P(("rows", "blk"), "tp"),
            P(("rows", "blk"), "tp"),
            P("rows", None),
            P("tp", None),
            P(None, "tp"),
            P("tp", None),
            P("tp", None),
            P(None, "tp"),
            P(None, "tp"),
        ),
        out_specs=(
            P(("rows", "blk"), "tp"),
            P(("rows", "blk"), "tp"),
            P("tp", None),
            P(None, "tp"),
            P("tp", None),
            P("tp", None),
            P(None, "tp"),
            P(None, "tp"),
            P("tp", None),
            P(None, "tp"),
        ),
        check_vma=False,
    )
```

```python
import math
from functools import partial
from types import SimpleNamespace

import jax
import jax.numpy as jnp
from jax import lax
from jax.experimental import pallas as pl
from jax.experimental.pallas import tpu as pltpu
from jax.sharding import PartitionSpec as P

HD = 64
HG = 768
MESH = pl.DeviceIdType.MESH
f32 = jnp.float32
bf16 = jnp.bfloat16

eps_norm = 1e-12
beta_one = 0.9
beta_two = 0.999
adam_eps = 1e-06
step_count = 100.0
decay_rate = 0.01
learn_rate = 0.04
matrix_rate = 1.0
NEG = -1e30
RELAY = 0


def nn(a, b):
    return jnp.dot(a, b, preferred_element_type=f32)


def nt(a, b, **kw):
    return lax.dot_general(a, b, (((1,), (1,)), ((), ())), preferred_element_type=f32, **kw)


def eye(n, dtype=bf16):
    rows = lax.broadcasted_iota(jnp.int32, (n, n), 0)
    cols = lax.broadcasted_iota(jnp.int32, (n, n), 1)
    return (rows == cols).astype(dtype)


def flip(a):
    return nt(eye(a.shape[1]), a)


def split_bf16(a):
    high = a.astype(bf16)
    return high, (a - high.astype(f32)).astype(bf16)


def lane_sums(a):
    return nt(jnp.ones((8, a.shape[1]), bf16), a)[0:1]


def lane_sums_f32(a):
    high, low = split_bf16(a)
    return lane_sums(high) + lane_sums(low)


def lamb_moments(gradient, first_moment, second_moment):
    first_new = beta_one * first_moment + (1.0 - beta_one) * gradient
    second_new = beta_two * second_moment + (1.0 - beta_two) * gradient * gradient
    update = (
        first_new
        / (1.0 - beta_one**step_count)
        / (jnp.sqrt(second_new / (1.0 - beta_two**step_count)) + adam_eps)
    )
    return first_new, second_new, update


def gelu_pair(pre):
    half = 0.5 * (1.0 + lax.erf(pre * (2.0**-0.5)))
    slope = half + pre * (jnp.exp(-0.5 * pre * pre) * ((2.0 * math.pi) ** -0.5))
    return pre * half, slope


class Sizes:
    def __init__(self, mesh_shape, tokens, row_count):
        self.nr = mesh_shape["rows"]
        self.nb = mesh_shape["blk"]
        self.nt = mesh_shape["tp"]
        self.g, self.t = tokens
        self.d = self.g * self.nt
        self.heads = self.g // HD
        self.row = row_count
        self.ch = 128
        self.nc = self.t // self.ch
        self.wc = self.heads * self.ch
        self.half = HG // 2
        self.keep = self.nb <= 4
        self.line = self.nb == 4
        owners = self.nb
        while self.nb % owners or self.g % (16 * owners):
            owners -= 1
        self.owners = owners
        self.rq = self.g // owners
        tiles = 3 * self.g * self.g // (16 * 128)
        self.pr = -(-tiles // (self.nr * owners)) * 16
        self.ph = self.pr * owners
        self.pack = self.ph * self.nr
        o = 3 * self.g
        self.lo = (o + self.d + HG, o + self.d, o, 0)
        self.width = (HG, HG, self.d, o)
        self.cols = self.lo[0] + HG
        self.vmem = (48 if self.keep else 62) * 2**20


def scratch_of(s):
    V = pltpu.VMEM
    D = pltpu.SemaphoreType.DMA
    T, G, nb, ntp, nc, CH = s.t, s.g, s.nb, s.nt, s.nc, s.ch
    kept = nb if s.keep else 1
    shapes = dict(
        w=V((G, s.cols), f32),
        v=V((12, G), f32),
        ids=V((1, s.row), jnp.int32),
        cot=V((G, T), bf16),
        mom=V((G, s.cols), f32),
        squ=V((G, s.cols), f32),
        xt=V((nb, G, T), bf16),
        xtf=V((ntp, G, T), bf16),
        wot=V((ntp, 2, G // 2, s.d), bf16),
        vec=V((ntp, 16, G), f32),
        ctxg=V((nc, s.d, CH), bf16),
        st1=V((nc, ntp, 8, CH), f32),
        dmgg=V((nc, s.d, CH), bf16),
        st2=V((nc, ntp, 8, CH), f32),
        nrm=V((ntp, 8, 128), f32),
        dxr=V((nb, G, T), bf16),
        dxa=V((nb if s.line else 1, G, T), bf16),
        gcore=V((3, G, s.half), bf16),
        gend=V((3, G, s.half) if s.line else (1, 16, 128), bf16),
        gcross=V((3, G, s.half) if s.line else (1, 16, 128), bf16),
        gz=V((1, 1, 16, 128) if s.line else (3, nb, s.rq, s.half), bf16),
        gfin=V((3, 2, G, s.half), bf16),
        qcore=V((s.ph, 128), bf16),
        qz_in=V((nb, s.pr, 128), bf16),
        qfin=V((s.pack, 128), bf16),
        nq=V((s.nr, nb, 8, 128), f32),
        nqt=V((ntp, 8, 128), f32),
        upd=V((8, 128), f32),
        vgc=V((16, G), f32),
        vgz=V((nb, 16, G), f32),
        dxs=V((nb, G, T), bf16),
        gsrc=V((3, 2, G, s.half), bf16),
        ghalf=V((3, G, s.half), bf16),
        gmid=V((3, G, s.half) if s.line else (1, 16, 128), bf16),
        qsrc=V((s.pack, 128), bf16),
        qhalf=V((s.ph, 128), bf16),
        gq=V((2, G, s.half), bf16),
        pw=V((s.pack, 128), f32),
        pm=V((s.pack, 128), f32),
        ps=V((s.pack, 128), f32),
        vgl=V((16, G), f32),
        vgs=V((16, G), f32),
        x=V((kept, T, G), bf16),
        keys_t=V((kept, G, T), bf16),
        vals=V((kept, T, G), bf16),
        wq=V((G, G), bf16),
        wq_t=V((G, G), bf16),
        wk=V((G, G), bf16),
        wk_t=V((G, G), bf16),
        wv=V((G, G), bf16),
        wv_t=V((G, G), bf16),
        wof=V((s.d, s.d), bf16),
        w1=V((G, HG), bf16),
        w1_t=V((HG, G), bf16),
        w2=V((G, HG), bf16),
        w2_t=V((HG, G), bf16),
        qz=V((nc, G, s.wc), bf16),
        dcz=V((nc, G, s.wc), bf16),
        idk=V((kept, T, 128), f32),
        ebuf=V((kept, nc, T, s.wc), bf16),
        mrec=V((kept, nc, 1, s.wc), f32),
        mrun=V((nc, 1, s.wc), f32),
        lrun=V((nc, 1, s.wc), f32),
        acc=V((G, T), f32),
        ctxl=V((G, T), bf16),
        delta=V((nc, 1, s.wc), f32),
        lse=V((nc, 1, s.wc), f32),
        n1f=V((nc, s.d, CH), f32),
        inv1=V((nc, 1, CH), f32),
        datt=V((s.d, T), bf16),
        act=V((HG, T), bf16),
        slope=V((HG, T), f32),
        dpre=V((HG, T), bf16),
        midl=V((G, T), bf16),
        dffn=V((G, T), bf16),
        h2=V((G, T), f32),
        cn2=V((G, T), f32),
        dmid=V((G, T), f32),
        dmn1=V((G, T), f32),
        dqt=V((G, T), f32),
        dkb=V((kept, T, G), f32),
        dvb=V((kept, T, G), f32),
        gkv=V((2, G, G), f32),
        vb=V((1, G), f32),
        dxo=V((G, T), f32),
        x_s=D((nb,)), x_r=D((nb,)), xf_s=D((1,)),
        xtf_s=D((ntp,)), xtf_r=D((ntp,)),
        wot_s=D((ntp,)), wot_r=D((ntp,)),
        woc_s=D((ntp,)), woc_r=D((ntp,)),
        xth_s=D((2,)), xth_r=D((2,)),
        woh_s=D((2,)), woh_r=D((2,)),
        vec_s=D((ntp,)), vec_r=D((ntp,)),
        ctx_s=D((nc, ntp)), ctx_r=D((nc, ntp)),
        st1_s=D((nc, ntp)), st1_r=D((nc, ntp)),
        dmg_s=D((nc, ntp)), dmg_r=D((nc, ntp)),
        st2_s=D((nc, ntp)), st2_r=D((nc, ntp)),
        nrm_s=D((ntp,)), nrm_r=D((ntp,)),
        dx_s=D((nb,)), dx_r=D((nb,)),
        da_s=D((nb,)), da_r=D((nb,)),
        gc_s=D((3,)), gc_r=D((3,)),
        ge_s=D((3,)), ge_r=D((3,)),
        gx_s=D((3,)), gx_r=D((3,)),
        gz_s=D((3, nb)), gz_r=D((3, nb)),
        ga_s=D((3, nb)), ga_r=D((3, nb)),
        gd_s=D((3,)), gd_r=D((3,)),
        qc_s=D((1,)), qc_r=D((1,)),
        qz_s=D((nb,)), qz_r=D((nb,)),
        qa_s=D((nb,)), qa_r=D((nb,)),
        qd_s=D((1,)), qd_r=D((1,)),
        nq_s=D((s.nr, nb)), nq_r=D((s.nr, nb)),
        nqt_s=D((ntp,)), nqt_r=D((ntp,)),
        vc_s=D((1,)), vc_r=D((1,)),
        vz_s=D((nb,)), vz_r=D((nb,)),
        loc=D((8,)),
        put=D((8,)),
    )
    return list(shapes.keys()), list(shapes.values())


def layer_kernel(s, names, x_hbm, cot_hbm, ids_hbm, w_hbm, v_hbm, mom_hbm, squ_hbm,
                 out_hbm, ig_hbm, g_hbm, vg_hbm, ratio_hbm, out_ref, ig_ref, vg_ref, ratio_ref, *scratch):
    r = SimpleNamespace(**dict(zip(names, scratch)))
    T, G, nb, ntp, nc, CH = s.t, s.g, s.nb, s.nt, s.nc, s.ch
    c, b, t = lax.axis_index("rows"), lax.axis_index("blk"), lax.axis_index("tp")
    core = (1 - c, b, t)
    tx, ty = t % 2, t // 2
    tp_peers = [ty * 2 + (1 - tx), (1 - ty) * 2 + tx, 3 - t]
    if nb == 4:
        z_peers = [b + 1 - 2 * (b % 2), (b + 2) % 4, 3 - b]
    else:
        z_peers = [(b + o) % nb for o in range(1, nb)]

    def tp_dev(k):
        return (c, b, k)

    def z_dev(k):
        return (c, k, t)

    sent = []
    pending = {}

    def copy(src, dst, ssem, rsem, dev):
        return pltpu.make_async_remote_copy(
            src_ref=src, dst_ref=dst, send_sem=ssem, recv_sem=rsem, device_id=dev, device_id_type=MESH
        )

    def push(key, src, dst, ssem, rsem, dev, here, here_sem):
        one = copy(src, dst, ssem, rsem, dev)
        one.start()
        sent.append(one)
        pending[key] = copy(here, here, ssem, here_sem, dev)

    def arrive(key):
        pending.pop(key).wait_recv()

    sent_if = []

    def push_if(who, src, dst, ssem, rsem, dev):
        one = copy(src, dst, ssem, rsem, dev)
        pl.when(who)(lambda: one.start())
        sent_if.append((who, one))

    def tp_push(key, at, sems):
        ssem, rsem = sems
        for i, k in enumerate(tp_peers):
            push((key, i), at(t), at(t), ssem(k), rsem(t), tp_dev(k), at(k), rsem(k))

    def tp_arrive(key):
        for i in range(ntp - 1):
            arrive((key, i))

    def sems(leaving, landing, *lead):
        return lambda k: leaving.at[lead + (k,)], lambda k: landing.at[lead + (k,)]

    def group(k):
        return pl.ds(pl.multiple_of(k * G, G), G)

    def load(i, src, dst):
        one = pltpu.make_async_copy(src, dst, r.loc.at[i])
        one.start()
        return one

    stored = []

    def store(src, dst):
        one = pltpu.make_async_copy(src, dst, r.put.at[len(stored)])
        one.start()
        stored.append(one)

    barrier = pltpu.get_barrier_semaphore()
    pl.semaphore_signal(barrier, 1, device_id=core, device_id_type=MESH)
    for k in tp_peers:
        pl.semaphore_signal(barrier, 1, device_id=tp_dev(k), device_id_type=MESH)
    for k in z_peers:
        pl.semaphore_signal(barrier, 1, device_id=z_dev(k), device_id_type=MESH)
        pl.semaphore_signal(barrier, 1, device_id=(1 - c, k, t), device_id_type=MESH)
    load_x = load(0, x_hbm, r.xt.at[b])
    load_v = load(1, v_hbm, r.v)
    load_ids = load(2, ids_hbm, r.ids)
    load_w = load(3, w_hbm, r.w)
    load_cot = load(4, cot_hbm, r.cot)
    load_m = load(5, mom_hbm, r.mom)
    load_s = load(6, squ_hbm, r.squ)
    load_x.wait()
    load_v.wait()
    r.vec[t, 0:12, :] = r.v[...]
    r.vec[t, 12:16, :] = jnp.zeros((4, G), f32)
    pl.semaphore_wait(barrier, 1 + (ntp - 1) + 2 * (nb - 1))

    if s.line:
        inner = (b == 1) | (b == 2)
        outer = (b == 0) | (b == 3)
        for i in (1, 0):
            j = z_peers[i]
            push(("x", i), r.xt.at[b], r.xt.at[b], r.x_s.at[j], r.x_r.at[b], z_dev(j), r.xt.at[j], r.x_r.at[j])
        j = z_peers[2]
        push_if(inner, r.xt.at[b], r.xt.at[b], r.x_s.at[j], r.x_r.at[b], z_dev(j))
        pending[("x", 2)] = copy(r.xt.at[j], r.xt.at[j], r.x_s.at[j], r.x_r.at[j], z_dev(j))
    else:
        for i, j in enumerate(z_peers):
            push(("x", i), r.xt.at[b], r.xt.at[b], r.x_s.at[j], r.x_r.at[b], z_dev(j), r.xt.at[j], r.x_r.at[j])
    for i, k in enumerate(tp_peers[:2]):
        push(("xtf", i), r.xt.at[b], r.xtf.at[t], r.xtf_s.at[k], r.xtf_r.at[t], tp_dev(k), r.xtf.at[k], r.xtf_r.at[k])
    tp_push("vec", lambda k: r.vec.at[k], sems(r.vec_s, r.vec_r))
    load_w.wait()
    w_ref = r.w
    w_o = w_ref[:, s.lo[2]:s.lo[2] + s.d].astype(bf16)
    for h in range(2):
        r.wot[t, h] = w_o[h * (G // 2):(h + 1) * (G // 2)]
    for i, k in enumerate(tp_peers[:2]):
        push(("wot", i), r.wot.at[t, c], r.wot.at[t, c], r.wot_s.at[k], r.wot_r.at[t], tp_dev(k), r.wot.at[k, c], r.wot_r.at[k])
    r.xtf[t] = r.xt[b]
    load_ids.wait()

    w_q = w_ref[:, 0:G].astype(bf16)
    w_k = w_ref[:, G:2 * G].astype(bf16)
    w_v = w_ref[:, 2 * G:3 * G].astype(bf16)
    r.wq[...] = w_q
    r.wq_t[...] = flip(w_q).astype(bf16)
    r.wk[...] = w_k
    r.wk_t[...] = flip(w_k).astype(bf16)
    r.wv[...] = w_v
    r.wv_t[...] = flip(w_v).astype(bf16)

    def columns_of(vec):
        return nt(eye(G, f32), vec, precision=lax.Precision.HIGHEST)

    v_cols = columns_of(r.vec[t])

    def v_col(k):
        return v_cols[:, k:k + 1]

    bias_v_row = r.v[1:2, :]
    bias_v_col = v_col(1)

    scaling = HD**-0.5
    q_t = (nn(r.wq_t[...], r.xt[b]) + v_col(0)).astype(bf16)
    q_t = q_t.astype(f32) * scaling
    head_of = lax.broadcasted_iota(jnp.int32, (G, CH), 0) // HD

    def by_head(a):
        return jnp.concatenate([jnp.where(head_of == h, a, 0.0).astype(bf16) for h in range(s.heads)], axis=1)

    def lanes(k):
        return slice(k * CH, (k + 1) * CH)

    def head_rows(h):
        return slice(h * HD, (h + 1) * HD)

    for k in range(nc):
        r.qz[k] = by_head(q_t[:, lanes(k)])

    def ids_of(j):
        return r.ids[:, pl.ds(pl.multiple_of(j * T, 128), T)].astype(f32)

    def id_columns(j):
        ids = ids_of(j)
        high = jnp.floor(ids * (1.0 / 128.0))
        low = ids - 128.0 * high
        high, low = (jnp.broadcast_to(a, (128, T)).astype(bf16) for a in (high, low))
        return 128.0 * nt(eye(T), high) + nt(eye(T), low)

    if s.keep:
        for k in range(nb):
            r.idk[k] = id_columns(k)
    id_q = ids_of(b)

    r.mrun[...] = jnp.full((nc, 1, s.wc), NEG, f32)
    r.lrun[...] = jnp.zeros((nc, 1, s.wc), f32)
    r.acc[...] = jnp.zeros((G, T), f32)

    def same_doc(j, k):
        ids = r.idk[j] if s.keep else id_columns(j)
        return jnp.concatenate([ids == id_q[:, lanes(k)]] * s.heads, axis=1)

    def forward_block(j, after=None):
        x_jt = r.xt[j]
        x_j = flip(x_jt).astype(bf16)
        keys = nn(x_j, r.wk[...]).astype(bf16)
        vals_t = (nn(r.wv_t[...], x_jt) + bias_v_col).astype(bf16)
        for k in range(nc):
            score = jnp.where(same_doc(j, k), nn(keys, r.qz[k]), NEG)
            old = r.mrun[k]
            top = jnp.maximum(old, jnp.max(score, axis=0, keepdims=True))
            fade = jnp.exp(old - top)
            e = jnp.exp(score - top)
            r.lrun[k] = r.lrun[k] * fade + jnp.sum(e, axis=0, keepdims=True)
            e = e.astype(bf16)
            if s.keep:
                r.ebuf[j, k] = e
                r.mrec[j, k] = top
            r.mrun[k] = top
            for h in range(s.heads):
                rows = head_rows(h)
                r.acc[rows, lanes(k)] = r.acc[rows, lanes(k)] * fade[:, lanes(h)] + nn(vals_t[rows, :], e[:, lanes(h)])
            if after is not None:
                after(k)
        if s.keep:
            r.x[j] = x_j
            r.keys_t[j] = nn(r.wk_t[...], x_jt).astype(bf16)
            r.vals[j] = (nn(x_j, r.wv[...]) + bias_v_row).astype(bf16)

    forward_block(b)
    if s.line:
        far = z_peers[1]
        here = copy(r.xt.at[far], r.xt.at[far], r.x_s.at[far], r.x_r.at[far], z_dev(far))
        on = copy(r.xt.at[far], r.xt.at[far], r.xf_s.at[0], r.x_r.at[far], z_dev(3 - far))

        @pl.when(inner)
        def _():
            here.wait_recv()
            on.start()

        sent_if.append((inner, on))

    w_1 = w_ref[:, s.lo[1]:s.lo[1] + HG].astype(bf16)
    w_2 = w_ref[:, s.lo[0]:s.lo[0] + HG].astype(bf16)
    r.w1[...] = w_1
    r.w1_t[...] = flip(w_1).astype(bf16)
    r.w2[...] = w_2
    r.w2_t[...] = flip(w_2).astype(bf16)
    load_cot.wait()
    load_m.wait()
    load_s.wait()

    def packed(a):
        parts = [a[:, k * 128:(k + 1) * 128] for k in range(3 * G // 128)]
        rest = a[:, 3 * G // 128 * 128:]
        parts += [jnp.concatenate([rest[:G // 2], rest[G // 2:]], axis=1)]
        parts += [jnp.zeros((s.pack - 3 * G * G // 128, 128), a.dtype)]
        return jnp.concatenate(parts, axis=0)

    def unpacked(a):
        parts = [a[k * G:(k + 1) * G] for k in range(3 * G // 128)]
        rest = a[3 * G // 128 * G:3 * G * G // 128]
        parts += [jnp.concatenate([rest[:, :64], rest[:, 64:]], axis=0)]
        return jnp.concatenate(parts, axis=1)

    r.pw[...] = packed(w_ref[:, 0:3 * G])
    r.pm[...] = packed(r.mom[:, 0:3 * G])
    r.ps[...] = packed(r.squ[:, 0:3 * G])

    def total(a):
        return jnp.broadcast_to(jnp.sum(jnp.sum(a, axis=0, keepdims=True), axis=1, keepdims=True), (1, 128))

    def columns(m):
        return w_ref[:, s.lo[m]:s.lo[m] + s.width[m]]

    lead = columns(3)
    weight_sums = [total(a * a) for a in (lead[:, 0:G], lead[:, G:2 * G], lead[:, 2 * G:], columns(2), columns(1), columns(0))]
    r.nrm[t] = jnp.concatenate(weight_sums + [jnp.zeros((2, 128), f32)], axis=0)
    tp_push("nrm", lambda k: r.nrm.at[k], sems(r.nrm_s, r.nrm_r))

    def half_rows(ref, h):
        n = ref.shape[0] // 2
        return ref.at[pl.ds(h * n, n)]

    def relay(key, at, leaving, landing):
        for h in range(2):
            arrive((key, h))
            block = half_rows(at(tp_peers[h]), h)
            here = half_rows(at(tp_peers[2]), h)
            push((key, 2 + h), block, block, leaving.at[h], landing.at[h], tp_dev(tp_peers[1 - h]), here, landing.at[h])

    def relays():
        relay("xtf", lambda k: r.xtf.at[k], r.xth_s, r.xth_r)
        relay("wot", lambda k: r.wot.at[k, c], r.woh_s, r.woh_r)

    def context_ready(k):
        r.lse[k] = r.mrun[k] + jnp.log(r.lrun[k])
        inverse = 1.0 / r.lrun[k]
        parts = [r.acc[head_rows(h), lanes(k)] * inverse[:, lanes(h)] for h in range(s.heads)]
        context = jnp.concatenate(parts, axis=0)
        r.acc[:, lanes(k)] = context
        context = context.astype(bf16)
        r.ctxl[:, lanes(k)] = context
        r.ctxg[k, group(t), :] = context
        tp_push(("ctx", k), lambda d: r.ctxg.at[k, group(d), :], sems(r.ctx_s, r.ctx_r, k))

    if s.keep:
        for i, j in enumerate(z_peers):
            if s.line and i == 1:
                pl.when(outer)(lambda: pending.pop(("x", 1)).wait_recv())
            else:
                arrive(("x", i))
            forward_block(j, context_ready if i == nb - 2 else None)
            if i == RELAY:
                relays()
    else:
        def forward_remote(o, _):
            j = (b + o) % nb
            copy(r.xt.at[j], r.xt.at[j], r.x_s.at[j], r.x_r.at[j], z_dev(j)).wait_recv()
            forward_block(j)
            return 0

        relays()
        lax.fori_loop(1, nb, forward_remote, 0)
        for i in range(nb - 1):
            pending.pop(("x", i))
        for k in range(nc):
            context_ready(k)

    if s.keep:
        for j in range(nb):
            for k in range(nc):
                r.ebuf[j, k] = (r.ebuf[j, k].astype(f32) * jnp.exp(r.mrec[j, k] - r.lse[k])).astype(bf16)

    for h in range(2):
        arrive(("wot", 2 + h))
    for i, k in enumerate(tp_peers):
        push(("woc", i), r.wot.at[k, c], r.wot.at[k, c], r.woc_s.at[k], r.woc_r.at[k], core, r.wot.at[k, 1 - c], r.woc_r.at[k])
    tp_arrive("vec")
    for h in range(2):
        arrive(("xtf", 2 + h))
    tp_arrive("nrm")
    out_bias = [columns_of(r.vec[k])[:, 2:3] for k in range(ntp)]
    tp_arrive("woc")

    def output_rows(k):
        return jnp.concatenate([r.wot[k, 0], r.wot[k, 1]], axis=0)

    for k in range(ntp):
        r.wof[:, k * G:(k + 1) * G] = flip(output_rows(k)).astype(bf16)

    gain1 = v_col(3)
    bias_rows = HG // G
    hid_bias = jnp.concatenate([v_col(5 + k) for k in range(bias_rows)], axis=0)
    gain2 = v_col(6 + bias_rows)
    shift2 = v_col(7 + bias_rows)

    def forward_chunk(k):
        tp_arrive(("ctx", k))
        att = nn(r.wof[...], r.ctxg[k])
        hidden = [
            r.xtf[d][:, lanes(k)].astype(f32) + att[d * G:(d + 1) * G] + out_bias[d] for d in range(ntp)
        ]
        mean = sum(jnp.sum(a, axis=0, keepdims=True) for a in hidden) / s.d
        hidden = [a - mean for a in hidden]
        var = sum(jnp.sum(a * a, axis=0, keepdims=True) for a in hidden) / s.d
        inv = lax.rsqrt(var + eps_norm)
        r.inv1[k] = inv
        for d in range(ntp):
            r.n1f[k, d * G:(d + 1) * G, :] = hidden[d] * inv
        mid = r.n1f[k, group(t), :] * gain1 + v_col(4)
        mid_low = mid.astype(bf16)
        r.midl[:, lanes(k)] = mid_low
        act, slope = gelu_pair(nn(r.w1_t[...], mid_low) + hid_bias)
        act = act.astype(bf16)
        r.act[:, lanes(k)] = act
        r.slope[:, lanes(k)] = slope
        h2 = mid + nn(r.w2[...], act) + v_col(5 + bias_rows)
        r.h2[:, lanes(k)] = h2
        scaled = r.cot[:, lanes(k)].astype(f32) * gain2
        sum1 = jnp.sum(h2, axis=0, keepdims=True)
        h2c = h2 - sum1 / G
        sum2 = jnp.sum(h2c * h2c, axis=0, keepdims=True)
        sum3 = jnp.sum(scaled, axis=0, keepdims=True)
        sum4 = jnp.sum(scaled * h2c, axis=0, keepdims=True)
        r.st1[k, t] = jnp.concatenate([sum1, sum2, sum3, sum4, jnp.zeros((4, CH), f32)], axis=0)
        tp_push(("st1", k), lambda d: r.st1.at[k, d], sems(r.st1_s, r.st1_r, k))

    def backward_chunk(k):
        tp_arrive(("st1", k))
        stats = [r.st1[k, d] for d in range(ntp)]
        mean = sum(a[0:1] for a in stats) / s.d
        offs = [a[0:1] / G - mean for a in stats]
        var = sum(a[1:2] + G * o * o for a, o in zip(stats, offs)) / s.d
        inv = lax.rsqrt(var + eps_norm)
        first = sum(a[2:3] for a in stats) / s.d
        second = sum(a[3:4] + a[2:3] * o for a, o in zip(stats, offs)) * inv / s.d
        n2 = (r.h2[:, lanes(k)] - mean) * inv
        out_ref[:, lanes(k)] = (n2 * gain2 + shift2).astype(bf16)
        cot = r.cot[:, lanes(k)].astype(f32)
        r.cn2[:, lanes(k)] = cot * n2
        d2 = inv * (cot * gain2 - first - n2 * second)
        dffn = d2.astype(bf16)
        r.dffn[:, lanes(k)] = dffn
        dpre = (nn(r.w2_t[...], dffn) * r.slope[:, lanes(k)]).astype(bf16)
        r.dpre[:, lanes(k)] = dpre
        dmid = d2 + nn(r.w1[...], dpre)
        r.dmid[:, lanes(k)] = dmid
        n1 = r.n1f[k, group(t), :]
        r.dmn1[:, lanes(k)] = dmid * n1
        dmg = dmid * gain1
        part1 = jnp.sum(dmg, axis=0, keepdims=True)
        part2 = jnp.sum(dmg * n1, axis=0, keepdims=True)
        r.st2[k, t] = jnp.concatenate([part1, part2, jnp.zeros((6, CH), f32)], axis=0)
        r.dmgg[k, group(t), :] = dmg.astype(bf16)
        tp_push(("st2", k), lambda d: r.st2.at[k, d], sems(r.st2_s, r.st2_r, k))
        tp_push(("dmg", k), lambda d: r.dmgg.at[k, group(d), :], sems(r.dmg_s, r.dmg_r, k))

    for k in range(nc):
        forward_chunk(k)
    for k in range(nc):
        backward_chunk(k)
    store(out_ref, out_hbm)

    def sum_start(m):
        push(("gc", m), r.gsrc.at[m, 1 - c], r.gcore.at[m], r.gc_s.at[m], r.gc_r.at[m], core, r.gcore.at[m], r.gc_r.at[m])

    def add_low(a, b):
        return (a.astype(f32) + b.astype(f32)).astype(bf16)

    def when_owner(j, body):
        if s.owners < nb:
            pl.when(j < s.owners)(body)
        else:
            body()

    def quarter(j):
        return pl.ds(pl.multiple_of(j * s.rq, 16), s.rq)

    def to_owner(m, j):
        return r.ghalf.at[m, quarter(j)], r.gz.at[m, b], r.gz_s.at[m, j], r.gz_r.at[m, b], z_dev(j)

    def to_all(m, j):
        mine = r.gfin.at[m, c, quarter(b)]
        return mine, mine, r.ga_s.at[m, j], r.ga_r.at[m, b], z_dev(j)

    beside, across = (z_peers[0], z_peers[2]) if s.line else (None, None)

    def landed(ref, sem, dev):
        copy(ref, ref, sem, sem, dev).wait_recv()

    def sum_spread(m):
        arrive(("gc", m))
        r.ghalf[m] = add_low(r.gsrc[m, c], r.gcore[m])
        if s.line:
            push_if(outer, r.ghalf.at[m], r.gend.at[m], r.ge_s.at[m], r.ge_r.at[m], z_dev(beside))
        else:
            for j in z_peers:
                when_owner(j, lambda: copy(*to_owner(m, j)).start())

    def sum_cross(m):
        if s.line:
            one = copy(r.gmid.at[m], r.gcross.at[m], r.gx_s.at[m], r.gx_r.at[m], z_dev(across))

            @pl.when(inner)
            def _():
                landed(r.gend.at[m], r.ge_r.at[m], z_dev(beside))
                r.gmid[m] = add_low(r.ghalf[m], r.gend[m])
                one.start()

            sent_if.append((inner, one))

    def sum_own(m):
        if s.line:
            mine = r.gfin.at[m, c]
            one = copy(mine, mine, r.ga_s.at[m, 0], r.ga_r.at[m, 0], z_dev(beside))

            @pl.when(inner)
            def _():
                landed(r.gcross.at[m], r.gx_r.at[m], z_dev(across))
                r.gfin[m, c] = add_low(r.gmid[m], r.gcross[m])
                one.start()

            sent_if.append((inner, one))
        else:
            def body():
                for j in z_peers:
                    landed(r.gz.at[m, j], r.gz_r.at[m, j], z_dev(j))
                r.gz[m, b] = r.ghalf[m, quarter(b)]
                sums = r.gz[m, 0].astype(f32)
                for j in range(1, nb):
                    sums = sums + r.gz[m, j].astype(f32)
                r.gfin[m, c, quarter(b)] = sums.astype(bf16)
                for j in z_peers:
                    copy(*to_all(m, j)).start()
                r.upd[m:m + 1, :] = norm_of(m, b)

            when_owner(b, body)

    def norm_of(m, piece=None):
        here = slice(None) if piece is None else quarter(piece)

        def own_half(ref):
            first, second = (ref[here, s.lo[m] + h * s.half:s.lo[m] + (h + 1) * s.half] for h in range(2))
            return jnp.where(c == 0, first, second)

        _, _, u = lamb_moments(r.gfin[m, c, here].astype(f32), own_half(r.mom), own_half(r.squ))
        u = u + decay_rate * own_half(w_ref)
        return total(u * u)

    def sum_norm(m):
        if s.line:
            @pl.when(inner)
            def _():
                r.upd[m:m + 1, :] = norm_of(m)

    def sum_share(m):
        if s.line:
            pl.when(outer)(lambda: landed(r.gfin.at[m, c], r.ga_r.at[m, 0], z_dev(beside)))
        else:
            for j in z_peers:
                when_owner(j, lambda: landed(r.gfin.at[m, c, quarter(j)], r.ga_r.at[m, j], z_dev(j)))
        push(("gd", m), r.gfin.at[m, c], r.gfin.at[m, c], r.gd_s.at[m], r.gd_r.at[m], core, r.gfin.at[m, 1 - c], r.gd_r.at[m])

    def sum_done(m):
        arrive(("gd", m))
        store(r.gfin.at[m], g_hbm.at[m])

    def sum_sends_done(m):
        for j in z_peers:
            when_owner(j, lambda: copy(*to_owner(m, j)).wait_send())

        def body():
            for j in z_peers:
                copy(*to_all(m, j)).wait_send()

        when_owner(b, body)

    def keep_grad(m, grad):
        r.gsrc[m, 0] = grad[:, 0:s.half].astype(bf16)
        r.gsrc[m, 1] = grad[:, s.half:].astype(bf16)

    keep_grad(0, nt(r.dffn[...], r.act[...]))
    sum_start(0)
    keep_grad(1, nt(r.midl[...], r.dpre[...]))
    sum_start(1)
    vgl = r.vgl
    vgl[12:16, :] = jnp.zeros((4, G), f32)
    vgl[3:4, :] = lane_sums_f32(r.dmn1[...])
    vgl[4:5, :] = lane_sums_f32(r.dmid[...])
    hid_sum = lane_sums(r.dpre[...])
    for k in range(bias_rows):
        vgl[5 + k:6 + k, :] = hid_sum[:, k * G:(k + 1) * G]
    vgl[5 + bias_rows:6 + bias_rows, :] = lane_sums(r.dffn[...])
    vgl[6 + bias_rows:7 + bias_rows, :] = lane_sums_f32(r.cn2[...])
    vgl[7 + bias_rows:8 + bias_rows, :] = lane_sums(r.cot[...])
    r.upd[...] = jnp.zeros((8, 128), f32)
    if s.line:
        sum_spread(0)
        sum_spread(1)

    def context_chunk(k):
        tp_arrive(("st2", k))
        stats = [r.st2[k, d] for d in range(ntp)]
        first = sum(a[0:1] for a in stats) / s.d
        second = sum(a[1:2] for a in stats) / s.d
        inv = r.inv1[k]
        own = inv * (r.dmid[:, lanes(k)] * gain1 - first - r.n1f[k, group(t), :] * second)
        r.dxo[:, lanes(k)] = own
        tp_arrive(("dmg", k))
        for d in range(ntp):
            rows = slice(d * G, (d + 1) * G)
            part = inv * (r.dmgg[k, rows, :].astype(f32) - first - r.n1f[k, rows, :] * second)
            r.datt[rows, lanes(k)] = part.astype(bf16)
        dctx = nn(output_rows(t), r.datt[:, lanes(k)]).astype(bf16).astype(f32)
        r.dcz[k] = by_head(dctx)
        parts = [
            jnp.sum(dctx[head_rows(h)] * r.acc[head_rows(h), lanes(k)], axis=0, keepdims=True)
            for h in range(s.heads)
        ]
        r.delta[k] = jnp.concatenate(parts, axis=1)

    r.dqt[...] = jnp.zeros((G, T), f32)
    r.gkv[...] = jnp.zeros((2, G, G), f32)
    r.vb[...] = jnp.zeros((1, G), f32)

    def pair_terms(j, chunks):
        if s.keep:
            keys_t, vals = r.keys_t[j], r.vals[j]
        else:
            x_jt = r.xt[j]
            x_j = flip(x_jt).astype(bf16)
            keys_t = nn(r.wk_t[...], x_jt).astype(bf16)
            vals = (nn(x_j, r.wv[...]) + bias_v_row).astype(bf16)
            keys = nn(x_j, r.wk[...]).astype(bf16)
        dk = dv = None
        for k in chunks:
            if s.keep:
                p_low = r.ebuf[j, k]
                p = p_low.astype(f32)
            else:
                p = jnp.exp(jnp.where(same_doc(j, k), nn(keys, r.qz[k]), NEG) - r.lse[k])
                p_low = p.astype(bf16)
            ds = (p * (nn(vals, r.dcz[k]) - r.delta[k])).astype(bf16)
            for h in range(s.heads):
                r.dqt[head_rows(h), lanes(k)] += nn(keys_t[head_rows(h), :], ds[:, lanes(h)])
            dk_k, dv_k = nt(ds, r.qz[k]), nt(p_low, r.dcz[k])
            dk, dv = (dk_k, dv_k) if dk is None else (dk + dk_k, dv + dv_k)
        return dk, dv

    def finish_block(j, dk, dv):
        dk, dv = dk.astype(bf16), dv.astype(bf16)
        x_jt = r.xt[j]
        r.gkv[0] += nn(x_jt, dk)
        r.gkv[1] += nn(x_jt, dv)
        r.vb[...] += jnp.sum(dv.astype(f32), axis=0, keepdims=True)
        return nt(r.wk[...], dk) + nt(r.wv[...], dv)

    def dx_send(j):
        return r.dxs.at[j], r.dxr.at[b], r.dx_s.at[j], r.dx_r.at[b], z_dev(j)

    if s.keep:
        context_chunk(0)
        for j in z_peers + [b]:
            r.dkb[j], r.dvb[j] = pair_terms(j, [0])
        for k in range(1, nc):
            context_chunk(k)
        keep_grad(2, nt(r.ctxl[...], r.datt[...]))
        sum_start(2)
        vgl[2:3, :] = lane_sums(r.dxo[...].astype(bf16))
        for i in (1, 2, 0):
            j = z_peers[i]
            dk, dv = pair_terms(j, range(1, nc))
            r.dxs[j] = finish_block(j, dk + r.dkb[j], dv + r.dvb[j]).astype(bf16)
            if i == 0:
                push(("dx", 0), *dx_send(j), r.dxr.at[j], r.dx_r.at[j])
                sum_cross(1)
            else:
                push_if(outer, r.dxs.at[j], r.dxa.at[j], r.da_s.at[j], r.da_r.at[j], z_dev(beside))
                if i == 1:
                    sum_spread(2)
                else:
                    sum_cross(0)
        dk, dv = pair_terms(b, range(1, nc))
        r.dxo[...] += finish_block(b, dk + r.dkb[b], dv + r.dvb[b])
    else:
        for k in range(nc):
            context_chunk(k)
        keep_grad(2, nt(r.ctxl[...], r.datt[...]))
        sum_start(2)
        vgl[2:3, :] = lane_sums(r.dxo[...].astype(bf16))

        def backward_remote(o, _):
            j = (b + o) % nb
            r.dxs[j] = finish_block(j, *pair_terms(j, range(nc))).astype(bf16)
            copy(*dx_send(j)).start()
            return 0

        lax.fori_loop(1, nb, backward_remote, 0)
        r.dxo[...] += finish_block(b, *pair_terms(b, range(nc)))
        for m in (0, 1, 2):
            sum_spread(m)
        sum_own(0)
        sum_own(1)
    dq_t = (r.dqt[...] * scaling).astype(bf16)
    r.qsrc[...] = packed(jnp.concatenate([nt(r.xt[b], dq_t), r.gkv[0], r.gkv[1]], axis=1)).astype(bf16)

    def part(k, n):
        return pl.ds(pl.multiple_of(k * n, 16), n)

    push("qc", r.qsrc.at[part(1 - c, s.ph)], r.qcore, r.qc_s.at[0], r.qc_r.at[0], core, r.qcore, r.qc_r.at[0])
    vgl[0:1, :] = lane_sums(dq_t)
    vgl[1:2, :] = r.vb[...]
    push("vc", vgl, r.vgc, r.vc_s.at[0], r.vc_r.at[0], core, r.vgc, r.vc_r.at[0])
    arrive("qc")
    r.qhalf[...] = add_low(r.qsrc[part(c, s.ph)], r.qcore[...])

    def q_to_owner(j):
        return r.qhalf.at[part(j, s.pr)], r.qz_in.at[b], r.qz_s.at[j], r.qz_r.at[b], z_dev(j)

    def q_to_all(j):
        mine = r.qfin.at[part(c * s.owners + b, s.pr)]
        return mine, mine, r.qa_s.at[j], r.qa_r.at[b], z_dev(j)

    for j in z_peers:
        when_owner(j, lambda: copy(*q_to_owner(j)).start())
    if s.line:
        sum_own(0)
        sum_cross(2)
        sum_own(1)

        @pl.when(inner)
        def _():
            for i in (1, 2):
                j = z_peers[i]
                landed(r.dxa.at[j], r.da_r.at[j], z_dev(beside))
                r.dxs[j] = add_low(r.dxs[j], r.dxa[j])
                copy(*dx_send(j)).start()

        for i in (1, 2):
            sent_if.append((inner, copy(*dx_send(z_peers[i]))))
    else:
        sum_own(2)
    r.dxo[...] += nn(r.wq[...], dq_t)
    sum_norm(0)
    sum_norm(1)

    mine = jnp.zeros((s.pr, 128), f32)
    for j in z_peers:
        when_owner(b, lambda: landed(r.qz_in.at[j], r.qz_r.at[j], z_dev(j)))
    r.qz_in[b] = r.qhalf[part(b % s.owners, s.pr)]
    for j in range(nb):
        mine = mine + r.qz_in[j].astype(f32)
    mine = mine.astype(bf16)

    @partial(when_owner, b)
    def _():
        r.qfin[part(c * s.owners + b, s.pr), :] = mine
        for j in z_peers:
            copy(*q_to_all(j)).start()

    first_row = (c * s.owners + b % s.owners) * s.pr
    here = part(c * s.owners + b % s.owners, s.pr)
    _, _, u = lamb_moments(mine.astype(f32), r.pm[here, :], r.ps[here, :])
    u = u + decay_rate * r.pw[here, :]
    u = jnp.where(b < s.owners, u * u, 0.0)
    row = first_row + lax.broadcasted_iota(jnp.int32, (s.pr, 128), 0)
    lane = lax.broadcasted_iota(jnp.int32, (s.pr, 128), 1)
    column = row // G * 128 + lane
    is_q = column < G
    is_k = (column >= G) & (column < 2 * G)
    is_v = column >= 2 * G
    lead = [total(jnp.where(a, u, 0.0)) for a in (is_q, is_k, is_v)]
    if s.line:
        sum_own(2)
        sum_norm(2)
        rest = jnp.where(b == 1, r.upd[...], 0.0)
    else:
        rest = r.upd[...]
    r.nq[c, b] = jnp.concatenate(lead + [rest[m:m + 1] for m in (2, 1, 0)] + [jnp.zeros((2, 128), f32)], axis=0)
    same_tp = [(1 - c, b)] + [(i, j) for j in z_peers for i in (c, 1 - c)]
    for n, (i, j) in enumerate(same_tp):
        push(("nq", n), r.nq.at[c, b], r.nq.at[c, b], r.nq_s.at[i, j], r.nq_r.at[c, b], (i, j, t), r.nq.at[i, j], r.nq_r.at[i, j])
    arrive("vc")
    r.vgs[...] = vgl[...] + r.vgc[...]
    r.vgz[b] = r.vgs[...]
    for i, j in enumerate(z_peers):
        push(("vz", i), r.vgs, r.vgz.at[b], r.vz_s.at[j], r.vz_r.at[b], z_dev(j), r.vgz.at[j], r.vz_r.at[j])
    sum_share(0)
    sum_share(1)
    if s.line:
        other = jnp.where(b < 2, 2, 1)
        arrive(("dx", 0))
        landed(r.dxr.at[other], r.dx_r.at[other], z_dev(other))
        r.dxo[...] += r.dxr[beside].astype(f32) + r.dxr[other].astype(f32)
    else:
        for j in z_peers:
            landed(r.dxr.at[j], r.dx_r.at[j], z_dev(j))
            r.dxo[...] += r.dxr[j].astype(f32)
    ig_ref[...] = r.dxo[...]
    store(ig_ref, ig_hbm)
    sum_share(2)
    for n in range(len(same_tp)):
        arrive(("nq", n))
    sums = jnp.zeros((8, 128), f32)
    for i in range(s.nr):
        for j in range(nb):
            sums = sums + r.nq[i, j]
    r.nqt[t] = sums
    tp_push("nqt", lambda k: r.nqt.at[k], sems(r.nqt_s, r.nqt_r))
    for j in z_peers:
        when_owner(j, lambda: landed(r.qfin.at[part(c * s.owners + j, s.pr)], r.qa_r.at[j], z_dev(j)))
    push("qd", r.qfin.at[part(c, s.ph)], r.qfin.at[part(c, s.ph)], r.qd_s.at[0], r.qd_r.at[0], core, r.qfin.at[part(1 - c, s.ph)], r.qd_r.at[0])
    for m in range(3):
        sum_done(m)
    for i in range(nb - 1):
        arrive(("vz", i))
    vg = r.vgz[0]
    for j in range(1, nb):
        vg = vg + r.vgz[j]
    vg_ref[...] = vg[0:12]
    store(vg_ref, vg_hbm)
    arrive("qd")
    lead = unpacked(r.qfin[...])
    r.gq[0] = lead[:, 0:s.half]
    r.gq[1, :, 0:G] = lead[:, s.half:]
    r.gq[1, :, G:2 * G] = jnp.zeros((G, G), bf16)
    store(r.gq, g_hbm.at[3])
    tp_arrive("nqt")
    norms = r.nrm[0]
    lead = r.nqt[0]
    for k in range(1, ntp):
        norms = norms + r.nrm[k]
        lead = lead + r.nqt[k]
    ratio_ref[...] = jnp.sqrt(norms / (lead + 1e-12))
    store(ratio_ref, ratio_hbm)

    for one in sent:
        one.wait_send()
    for who, one in sent_if:
        pl.when(who)(lambda: one.wait_send())
    if not s.line:
        for m in range(3):
            sum_sends_done(m)
        for j in z_peers:
            copy(*dx_send(j)).wait_send()
    for j in z_peers:
        when_owner(j, lambda: copy(*q_to_owner(j)).wait_send())

    @partial(when_owner, b)
    def _():
        for j in z_peers:
            copy(*q_to_all(j)).wait_send()

    for one in stored:
        one.wait()


def finish_kernel(s, out_in, ig_in, w_ref, mom_ref, squ_ref, g_ref, ratio_ref, v_ref, vg_ref, mv_ref, sv_ref,
                  out_ref, ig_ref, gm_ref, gv_ref, nm_ref, ns_ref, nmv_ref, nsv_ref, nw_ref, nv_ref, grad):
    out_ref[...] = out_in[...]
    ig_ref[...] = ig_in[...]
    for m in range(4):
        for h in range(2):
            lo = s.lo[m] + h * s.half
            wide = min(s.half, s.lo[m] + s.width[m] - lo)
            grad[:, lo:lo + wide] = g_ref[m, h, :, 0:wide].astype(f32)
    cols = s.cols
    g = grad[...]
    gm_ref[...] = g
    new_m, new_s, u = lamb_moments(g, mom_ref[...], squ_ref[...])
    nm_ref[...] = new_m
    ns_ref[...] = new_s
    w = w_ref[...]
    u = u + decay_rate * w
    col = lax.broadcasted_iota(jnp.int32, (1, cols), 1)
    ratio = jnp.broadcast_to(ratio_ref[5:6, 0:1], (1, cols))
    for k, edge in ((4, s.lo[0]), (3, s.lo[1]), (2, s.lo[2]), (1, 2 * s.g), (0, s.g)):
        ratio = jnp.where(col < edge, ratio_ref[k:k + 1, 0:1], ratio)
    nw_ref[...] = w - matrix_rate * ratio * u

    @pl.when(pl.program_id(0) == 0)
    def _():
        vg = vg_ref[...]
        gv_ref[...] = vg
        new_mv, new_sv, uv = lamb_moments(vg, mv_ref[...], sv_ref[...])
        nmv_ref[...] = new_mv
        nsv_ref[...] = new_sv
        nv_ref[...] = v_ref[...] - learn_rate * uv


def local(mesh_shape, tokens, cotangent, segment_ids, matrices, vectors, moment_mat, square_mat, moment_vec, square_vec):
    tokens, cotangent = tokens.T, cotangent.T
    s = Sizes(mesh_shape, tokens.shape, segment_ids.shape[1])
    names, scratch = scratch_of(s)
    hbm = pl.BlockSpec(memory_space=pltpu.HBM)
    S = jax.ShapeDtypeStruct
    small = [
        pltpu.VMEM(tokens.shape, bf16), pltpu.VMEM(tokens.shape, f32),
        pltpu.VMEM(vectors.shape, f32), pltpu.VMEM((8, 128), f32),
    ]
    given = (tokens, cotangent, segment_ids, matrices, vectors, moment_mat, square_mat)
    output, input_grad, grads, vector_grad, ratio = pl.pallas_call(
        partial(layer_kernel, s, names),
        out_shape=(
            S(tokens.shape, bf16),
            S(tokens.shape, f32),
            S((4, 2, s.g, s.half), bf16),
            S(vectors.shape, f32),
            S((8, 128), f32),
        ),
        in_specs=[hbm] * 7,
        out_specs=(hbm,) * 5,
        scratch_shapes=small + scratch,
        compiler_params=pltpu.CompilerParams(
            collective_id=0, has_side_effects=True, vmem_limit_bytes=s.vmem
        ),
        name="layer",
    )(*(pltpu.with_memory_space_constraint(a, pltpu.HBM) for a in given))

    steps = s.owners

    def rows(a, n):
        return pl.BlockSpec((n, a.shape[1]), lambda i: (i, 0))

    def whole(a):
        return pl.BlockSpec(a.shape, lambda i: (0, 0))

    mat = rows(matrices, s.rq)
    vec = whole(vectors)
    results = pl.pallas_call(
        partial(finish_kernel, s),
        grid=(steps,),
        out_shape=(
            S(tokens.shape, bf16),
            S(tokens.shape, f32),
            S(matrices.shape, f32),
            S(vectors.shape, f32),
            S(matrices.shape, f32),
            S(matrices.shape, f32),
            S(vectors.shape, f32),
            S(vectors.shape, f32),
            S(matrices.shape, f32),
            S(vectors.shape, f32),
        ),
        in_specs=[
            rows(tokens, s.rq), rows(tokens, s.rq), mat, mat, mat,
            pl.BlockSpec((4, 2, s.rq, s.half), lambda i: (0, 0, i, 0)),
            pl.BlockSpec((8, 128), lambda i: (0, 0)), vec, vec, vec, vec,
        ],
        out_specs=(rows(tokens, s.rq), rows(tokens, s.rq), mat, vec, mat, mat, vec, vec, mat, vec),
        scratch_shapes=[pltpu.VMEM((s.rq, s.lo[0] + HG), f32)],
        compiler_params=pltpu.CompilerParams(vmem_limit_bytes=40 * 2**20),
        name="finish",
    )(output, input_grad, matrices, moment_mat, square_mat, grads, ratio, vectors, vector_grad, moment_vec, square_vec)
    return (results[0].T, results[1].T) + tuple(results[2:])


def solution(mesh):
    return jax.shard_map(
        partial(local, dict(mesh.shape)),
        mesh=mesh,
        in_specs=(
            P(("rows", "blk"), "tp"),
            P(("rows", "blk"), "tp"),
            P("rows", None),
            P("tp", None),
            P(None, "tp"),
            P("tp", None),
            P("tp", None),
            P(None, "tp"),
            P(None, "tp"),
        ),
        out_specs=(
            P(("rows", "blk"), "tp"),
            P(("rows", "blk"), "tp"),
            P("tp", None),
            P(None, "tp"),
            P("tp", None),
            P("tp", None),
            P(None, "tp"),
            P(None, "tp"),
            P("tp", None),
            P(None, "tp"),
        ),
        check_vma=False,
    )
```

```python
import math
from functools import partial
from types import SimpleNamespace

import jax
import jax.numpy as jnp
from jax import lax
from jax.experimental import pallas as pl
from jax.experimental.pallas import tpu as pltpu
from jax.sharding import PartitionSpec as P

HD = 64
HG = 768
MESH = pl.DeviceIdType.MESH
f32 = jnp.float32
bf16 = jnp.bfloat16

eps_norm = 1e-12
beta_one = 0.9
beta_two = 0.999
adam_eps = 1e-06
step_count = 100.0
decay_rate = 0.01
learn_rate = 0.04
matrix_rate = 1.0
NEG = -1e30
RELAY = 0


def nn(a, b):
    return jnp.dot(a, b, preferred_element_type=f32)


def nt(a, b, **kw):
    return lax.dot_general(a, b, (((1,), (1,)), ((), ())), preferred_element_type=f32, **kw)


def eye(n, dtype=bf16):
    rows = lax.broadcasted_iota(jnp.int32, (n, n), 0)
    cols = lax.broadcasted_iota(jnp.int32, (n, n), 1)
    return (rows == cols).astype(dtype)


def flip(a):
    return nt(eye(a.shape[1]), a)


def split_bf16(a):
    high = a.astype(bf16)
    return high, (a - high.astype(f32)).astype(bf16)


def lane_sums(a):
    return nt(jnp.ones((8, a.shape[1]), bf16), a)[0:1]


def lane_sums_f32(a):
    high, low = split_bf16(a)
    return lane_sums(high) + lane_sums(low)


def lamb_moments(gradient, first_moment, second_moment):
    first_new = beta_one * first_moment + (1.0 - beta_one) * gradient
    second_new = beta_two * second_moment + (1.0 - beta_two) * gradient * gradient
    update = (
        first_new
        / (1.0 - beta_one**step_count)
        / (jnp.sqrt(second_new / (1.0 - beta_two**step_count)) + adam_eps)
    )
    return first_new, second_new, update


def gelu_pair(pre):
    half = 0.5 * (1.0 + lax.erf(pre * (2.0**-0.5)))
    slope = half + pre * (jnp.exp(-0.5 * pre * pre) * ((2.0 * math.pi) ** -0.5))
    return pre * half, slope


class Sizes:
    def __init__(self, mesh_shape, tokens, row_count):
        self.nr = mesh_shape["rows"]
        self.nb = mesh_shape["blk"]
        self.nt = mesh_shape["tp"]
        self.g, self.t = tokens
        self.d = self.g * self.nt
        self.heads = self.g // HD
        self.row = row_count
        self.ch = 128
        self.nc = self.t // self.ch
        self.wc = self.heads * self.ch
        self.half = HG // 2
        self.keep = self.nb <= 4
        self.line = self.nb == 4
        owners = self.nb
        while self.nb % owners or self.g % (16 * owners):
            owners -= 1
        self.owners = owners
        self.rq = self.g // owners
        tiles = 3 * self.g * self.g // (16 * 128)
        self.pr = -(-tiles // (self.nr * owners)) * 16
        self.ph = self.pr * owners
        self.pack = self.ph * self.nr
        o = 3 * self.g
        self.lo = (o + self.d + HG, o + self.d, o, 0)
        self.width = (HG, HG, self.d, o)
        self.cols = self.lo[0] + HG
        self.vmem = (48 if self.keep else 62) * 2**20


def scratch_of(s):
    V = pltpu.VMEM
    D = pltpu.SemaphoreType.DMA
    T, G, nb, ntp, nc, CH = s.t, s.g, s.nb, s.nt, s.nc, s.ch
    kept = nb if s.keep else 1
    shapes = dict(
        w=V((G, s.cols), f32),
        v=V((12, G), f32),
        ids=V((1, s.row), jnp.int32),
        cot=V((G, T), bf16),
        mom=V((G, s.cols), f32),
        squ=V((G, s.cols), f32),
        xt=V((nb, G, T), bf16),
        xtf=V((ntp, G, T), bf16),
        wot=V((ntp, 2, G // 2, s.d), bf16),
        vec=V((ntp, 16, G), f32),
        ctxg=V((nc, s.d, CH), bf16),
        st1=V((nc, ntp, 8, CH), f32),
        dmgg=V((nc, s.d, CH), bf16),
        st2=V((nc, ntp, 8, CH), f32),
        nrm=V((ntp, 8, 128), f32),
        dxr=V((nb, G, T), bf16),
        dxa=V((nb if s.line else 1, G, T), bf16),
        gcore=V((3, G, s.half), bf16),
        gend=V((3, G, s.half) if s.line else (1, 16, 128), bf16),
        gcross=V((3, G, s.half) if s.line else (1, 16, 128), bf16),
        gz=V((1, 1, 16, 128) if s.line else (3, nb, s.rq, s.half), bf16),
        gfin=V((3, 2, G, s.half), bf16),
        qcore=V((s.ph, 128), bf16),
        qz_in=V((nb, s.pr, 128), bf16),
        qfin=V((s.pack, 128), bf16),
        nq=V((s.nr, nb, 8, 128), f32),
        nqt=V((ntp, 8, 128), f32),
        upd=V((8, 128), f32),
        vgc=V((16, G), f32),
        vgz=V((nb, 16, G), f32),
        dxs=V((nb, G, T), bf16),
        gsrc=V((3, 2, G, s.half), bf16),
        ghalf=V((3, G, s.half), bf16),
        gmid=V((3, G, s.half) if s.line else (1, 16, 128), bf16),
        qsrc=V((s.pack, 128), bf16),
        qhalf=V((s.ph, 128), bf16),
        gq=V((2, G, s.half), bf16),
        pw=V((s.pack, 128), f32),
        pm=V((s.pack, 128), f32),
        ps=V((s.pack, 128), f32),
        vgl=V((16, G), f32),
        vgs=V((16, G), f32),
        x=V((kept, T, G), bf16),
        keys_t=V((kept, G, T), bf16),
        vals=V((kept, T, G), bf16),
        wq=V((G, G), bf16),
        wq_t=V((G, G), bf16),
        wk=V((G, G), bf16),
        wk_t=V((G, G), bf16),
        wv=V((G, G), bf16),
        wv_t=V((G, G), bf16),
        wof=V((s.d, s.d), bf16),
        w1=V((G, HG), bf16),
        w1_t=V((HG, G), bf16),
        w2=V((G, HG), bf16),
        w2_t=V((HG, G), bf16),
        qz=V((nc, G, s.wc), bf16),
        dcz=V((nc, G, s.wc), bf16),
        idk=V((kept, T, 128), f32),
        ebuf=V((kept, nc, T, s.wc), bf16),
        mrec=V((kept, nc, 1, s.wc), f32),
        mrun=V((nc, 1, s.wc), f32),
        lrun=V((nc, 1, s.wc), f32),
        acc=V((G, T), f32),
        ctxl=V((G, T), bf16),
        delta=V((nc, 1, s.wc), f32),
        lse=V((nc, 1, s.wc), f32),
        n1f=V((nc, s.d, CH), f32),
        inv1=V((nc, 1, CH), f32),
        datt=V((s.d, T), bf16),
        act=V((HG, T), bf16),
        slope=V((HG, T), f32),
        dpre=V((HG, T), bf16),
        midl=V((G, T), bf16),
        dffn=V((G, T), bf16),
        h2=V((G, T), f32),
        cn2=V((G, T), f32),
        dmid=V((G, T), f32),
        dmn1=V((G, T), f32),
        dqt=V((G, T), f32),
        dkb=V((kept, T, G), f32),
        dvb=V((kept, T, G), f32),
        gkv=V((2, G, G), f32),
        vb=V((1, G), f32),
        dxo=V((G, T), f32),
        x_s=D((nb,)), x_r=D((nb,)), xf_s=D((1,)),
        xtf_s=D((ntp,)), xtf_r=D((ntp,)),
        wot_s=D((ntp,)), wot_r=D((ntp,)),
        woc_s=D((ntp,)), woc_r=D((ntp,)),
        xth_s=D((2,)), xth_r=D((2,)),
        woh_s=D((2,)), woh_r=D((2,)),
        vec_s=D((ntp,)), vec_r=D((ntp,)),
        ctx_s=D((nc, ntp)), ctx_r=D((nc, ntp)),
        st1_s=D((nc, ntp)), st1_r=D((nc, ntp)),
        dmg_s=D((nc, ntp)), dmg_r=D((nc, ntp)),
        st2_s=D((nc, ntp)), st2_r=D((nc, ntp)),
        nrm_s=D((ntp,)), nrm_r=D((ntp,)),
        dx_s=D((nb,)), dx_r=D((nb,)),
        da_s=D((nb,)), da_r=D((nb,)),
        gc_s=D((3,)), gc_r=D((3,)),
        ge_s=D((3,)), ge_r=D((3,)),
        gx_s=D((3,)), gx_r=D((3,)),
        gz_s=D((3, nb)), gz_r=D((3, nb)),
        ga_s=D((3, nb)), ga_r=D((3, nb)),
        gd_s=D((3,)), gd_r=D((3,)),
        qc_s=D((1,)), qc_r=D((1,)),
        qz_s=D((nb,)), qz_r=D((nb,)),
        qa_s=D((nb,)), qa_r=D((nb,)),
        qd_s=D((1,)), qd_r=D((1,)),
        nq_s=D((s.nr, nb)), nq_r=D((s.nr, nb)),
        nqt_s=D((ntp,)), nqt_r=D((ntp,)),
        vc_s=D((1,)), vc_r=D((1,)),
        vz_s=D((nb,)), vz_r=D((nb,)),
        loc=D((8,)),
        put=D((8,)),
    )
    return list(shapes.keys()), list(shapes.values())


def layer_kernel(s, names, x_hbm, cot_hbm, ids_hbm, w_hbm, v_hbm, mom_hbm, squ_hbm,
                 out_hbm, ig_hbm, g_hbm, vg_hbm, ratio_hbm, out_ref, ig_ref, vg_ref, ratio_ref, *scratch):
    r = SimpleNamespace(**dict(zip(names, scratch)))
    T, G, nb, ntp, nc, CH = s.t, s.g, s.nb, s.nt, s.nc, s.ch
    c, b, t = lax.axis_index("rows"), lax.axis_index("blk"), lax.axis_index("tp")
    core = (1 - c, b, t)
    tx, ty = t % 2, t // 2
    tp_peers = [ty * 2 + (1 - tx), (1 - ty) * 2 + tx, 3 - t]
    if nb == 4:
        z_peers = [b + 1 - 2 * (b % 2), (b + 2) % 4, 3 - b]
    else:
        z_peers = [(b + o) % nb for o in range(1, nb)]

    def tp_dev(k):
        return (c, b, k)

    def z_dev(k):
        return (c, k, t)

    sent = []
    pending = {}

    def copy(src, dst, ssem, rsem, dev):
        return pltpu.make_async_remote_copy(
            src_ref=src, dst_ref=dst, send_sem=ssem, recv_sem=rsem, device_id=dev, device_id_type=MESH
        )

    def push(key, src, dst, ssem, rsem, dev, here, here_sem):
        one = copy(src, dst, ssem, rsem, dev)
        one.start()
        sent.append(one)
        pending[key] = copy(here, here, ssem, here_sem, dev)

    def arrive(key):
        pending.pop(key).wait_recv()

    sent_if = []

    def push_if(who, src, dst, ssem, rsem, dev):
        one = copy(src, dst, ssem, rsem, dev)
        pl.when(who)(lambda: one.start())
        sent_if.append((who, one))

    def tp_push(key, at, sems):
        ssem, rsem = sems
        for i, k in reversed(list(enumerate(tp_peers))):
            push((key, i), at(t), at(t), ssem(k), rsem(t), tp_dev(k), at(k), rsem(k))

    def tp_arrive(key):
        for i in range(ntp - 1):
            arrive((key, i))

    def sems(leaving, landing, *lead):
        return lambda k: leaving.at[lead + (k,)], lambda k: landing.at[lead + (k,)]

    def group(k):
        return pl.ds(pl.multiple_of(k * G, G), G)

    def load(i, src, dst):
        one = pltpu.make_async_copy(src, dst, r.loc.at[i])
        one.start()
        return one

    stored = []

    def store(src, dst):
        one = pltpu.make_async_copy(src, dst, r.put.at[len(stored)])
        one.start()
        stored.append(one)

    barrier = pltpu.get_barrier_semaphore()
    pl.semaphore_signal(barrier, 1, device_id=core, device_id_type=MESH)
    for k in tp_peers:
        pl.semaphore_signal(barrier, 1, device_id=tp_dev(k), device_id_type=MESH)
    for k in z_peers:
        pl.semaphore_signal(barrier, 1, device_id=z_dev(k), device_id_type=MESH)
        pl.semaphore_signal(barrier, 1, device_id=(1 - c, k, t), device_id_type=MESH)
    load_x = load(0, x_hbm, r.xt.at[b])
    load_v = load(1, v_hbm, r.v)
    load_ids = load(2, ids_hbm, r.ids)
    load_w = load(3, w_hbm, r.w)
    load_cot = load(4, cot_hbm, r.cot)
    load_m = load(5, mom_hbm, r.mom)
    load_s = load(6, squ_hbm, r.squ)
    load_x.wait()
    load_v.wait()
    r.vec[t, 0:12, :] = r.v[...]
    r.vec[t, 12:16, :] = jnp.zeros((4, G), f32)
    pl.semaphore_wait(barrier, 1 + (ntp - 1) + 2 * (nb - 1))

    if s.line:
        inner = (b == 1) | (b == 2)
        outer = (b == 0) | (b == 3)
        for i in (1, 0):
            j = z_peers[i]
            push(("x", i), r.xt.at[b], r.xt.at[b], r.x_s.at[j], r.x_r.at[b], z_dev(j), r.xt.at[j], r.x_r.at[j])
        j = z_peers[2]
        push_if(inner, r.xt.at[b], r.xt.at[b], r.x_s.at[j], r.x_r.at[b], z_dev(j))
        pending[("x", 2)] = copy(r.xt.at[j], r.xt.at[j], r.x_s.at[j], r.x_r.at[j], z_dev(j))
    else:
        for i, j in enumerate(z_peers):
            push(("x", i), r.xt.at[b], r.xt.at[b], r.x_s.at[j], r.x_r.at[b], z_dev(j), r.xt.at[j], r.x_r.at[j])
    for i, k in enumerate(tp_peers[:2]):
        push(("xtf", i), r.xt.at[b], r.xtf.at[t], r.xtf_s.at[k], r.xtf_r.at[t], tp_dev(k), r.xtf.at[k], r.xtf_r.at[k])
    tp_push("vec", lambda k: r.vec.at[k], sems(r.vec_s, r.vec_r))
    load_w.wait()
    w_ref = r.w
    w_o = w_ref[:, s.lo[2]:s.lo[2] + s.d].astype(bf16)
    for h in range(2):
        r.wot[t, h] = w_o[h * (G // 2):(h + 1) * (G // 2)]
    for i, k in enumerate(tp_peers[:2]):
        push(("wot", i), r.wot.at[t, c], r.wot.at[t, c], r.wot_s.at[k], r.wot_r.at[t], tp_dev(k), r.wot.at[k, c], r.wot_r.at[k])
    r.xtf[t] = r.xt[b]
    load_ids.wait()

    w_q = w_ref[:, 0:G].astype(bf16)
    w_k = w_ref[:, G:2 * G].astype(bf16)
    w_v = w_ref[:, 2 * G:3 * G].astype(bf16)
    r.wq[...] = w_q
    r.wq_t[...] = flip(w_q).astype(bf16)
    r.wk[...] = w_k
    r.wk_t[...] = flip(w_k).astype(bf16)
    r.wv[...] = w_v
    r.wv_t[...] = flip(w_v).astype(bf16)

    def columns_of(vec):
        return nt(eye(G, f32), vec, precision=lax.Precision.HIGHEST)

    v_cols = columns_of(r.vec[t])

    def v_col(k):
        return v_cols[:, k:k + 1]

    bias_v_row = r.v[1:2, :]
    bias_v_col = v_col(1)

    scaling = HD**-0.5
    q_t = (nn(r.wq_t[...], r.xt[b]) + v_col(0)).astype(bf16)
    q_t = q_t.astype(f32) * scaling
    head_of = lax.broadcasted_iota(jnp.int32, (G, CH), 0) // HD

    def by_head(a):
        return jnp.concatenate([jnp.where(head_of == h, a, 0.0).astype(bf16) for h in range(s.heads)], axis=1)

    def lanes(k):
        return slice(k * CH, (k + 1) * CH)

    def head_rows(h):
        return slice(h * HD, (h + 1) * HD)

    for k in range(nc):
        r.qz[k] = by_head(q_t[:, lanes(k)])

    def ids_of(j):
        return r.ids[:, pl.ds(pl.multiple_of(j * T, 128), T)].astype(f32)

    def id_columns(j):
        ids = ids_of(j)
        high = jnp.floor(ids * (1.0 / 128.0))
        low = ids - 128.0 * high
        high, low = (jnp.broadcast_to(a, (128, T)).astype(bf16) for a in (high, low))
        return 128.0 * nt(eye(T), high) + nt(eye(T), low)

    if s.keep:
        for k in range(nb):
            r.idk[k] = id_columns(k)
    id_q = ids_of(b)

    r.mrun[...] = jnp.full((nc, 1, s.wc), NEG, f32)
    r.lrun[...] = jnp.zeros((nc, 1, s.wc), f32)
    r.acc[...] = jnp.zeros((G, T), f32)

    def same_doc(j, k):
        ids = r.idk[j] if s.keep else id_columns(j)
        return jnp.concatenate([ids == id_q[:, lanes(k)]] * s.heads, axis=1)

    def forward_block(j, after=None):
        x_jt = r.xt[j]
        x_j = flip(x_jt).astype(bf16)
        keys = nn(x_j, r.wk[...]).astype(bf16)
        vals_t = (nn(r.wv_t[...], x_jt) + bias_v_col).astype(bf16)
        for k in range(nc):
            score = jnp.where(same_doc(j, k), nn(keys, r.qz[k]), NEG)
            old = r.mrun[k]
            top = jnp.maximum(old, jnp.max(score, axis=0, keepdims=True))
            fade = jnp.exp(old - top)
            e = jnp.exp(score - top)
            r.lrun[k] = r.lrun[k] * fade + jnp.sum(e, axis=0, keepdims=True)
            e = e.astype(bf16)
            if s.keep:
                r.ebuf[j, k] = e
                r.mrec[j, k] = top
            r.mrun[k] = top
            for h in range(s.heads):
                rows = head_rows(h)
                r.acc[rows, lanes(k)] = r.acc[rows, lanes(k)] * fade[:, lanes(h)] + nn(vals_t[rows, :], e[:, lanes(h)])
            if after is not None:
                after(k)
        if s.keep:
            r.x[j] = x_j
            r.keys_t[j] = nn(r.wk_t[...], x_jt).astype(bf16)
            r.vals[j] = (nn(x_j, r.wv[...]) + bias_v_row).astype(bf16)

    forward_block(b)
    if s.line:
        far = z_peers[1]
        here = copy(r.xt.at[far], r.xt.at[far], r.x_s.at[far], r.x_r.at[far], z_dev(far))
        on = copy(r.xt.at[far], r.xt.at[far], r.xf_s.at[0], r.x_r.at[far], z_dev(3 - far))

        @pl.when(inner)
        def _():
            here.wait_recv()
            on.start()

        sent_if.append((inner, on))

    w_1 = w_ref[:, s.lo[1]:s.lo[1] + HG].astype(bf16)
    w_2 = w_ref[:, s.lo[0]:s.lo[0] + HG].astype(bf16)
    r.w1[...] = w_1
    r.w1_t[...] = flip(w_1).astype(bf16)
    r.w2[...] = w_2
    r.w2_t[...] = flip(w_2).astype(bf16)
    load_cot.wait()
    load_m.wait()
    load_s.wait()

    def packed(a):
        parts = [a[:, k * 128:(k + 1) * 128] for k in range(3 * G // 128)]
        rest = a[:, 3 * G // 128 * 128:]
        parts += [jnp.concatenate([rest[:G // 2], rest[G // 2:]], axis=1)]
        parts += [jnp.zeros((s.pack - 3 * G * G // 128, 128), a.dtype)]
        return jnp.concatenate(parts, axis=0)

    def unpacked(a):
        parts = [a[k * G:(k + 1) * G] for k in range(3 * G // 128)]
        rest = a[3 * G // 128 * G:3 * G * G // 128]
        parts += [jnp.concatenate([rest[:, :64], rest[:, 64:]], axis=0)]
        return jnp.concatenate(parts, axis=1)

    r.pw[...] = packed(w_ref[:, 0:3 * G])
    r.pm[...] = packed(r.mom[:, 0:3 * G])
    r.ps[...] = packed(r.squ[:, 0:3 * G])

    def total(a):
        return jnp.broadcast_to(jnp.sum(jnp.sum(a, axis=0, keepdims=True), axis=1, keepdims=True), (1, 128))

    def columns(m):
        return w_ref[:, s.lo[m]:s.lo[m] + s.width[m]]

    lead = columns(3)
    weight_sums = [total(a * a) for a in (lead[:, 0:G], lead[:, G:2 * G], lead[:, 2 * G:], columns(2), columns(1), columns(0))]
    r.nrm[t] = jnp.concatenate(weight_sums + [jnp.zeros((2, 128), f32)], axis=0)
    tp_push("nrm", lambda k: r.nrm.at[k], sems(r.nrm_s, r.nrm_r))

    def half_rows(ref, h):
        n = ref.shape[0] // 2
        return ref.at[pl.ds(h * n, n)]

    def relay(key, at, leaving, landing):
        for h in range(2):
            arrive((key, h))
            block = half_rows(at(tp_peers[h]), h)
            here = half_rows(at(tp_peers[2]), h)
            push((key, 2 + h), block, block, leaving.at[h], landing.at[h], tp_dev(tp_peers[1 - h]), here, landing.at[h])

    def relays():
        relay("xtf", lambda k: r.xtf.at[k], r.xth_s, r.xth_r)
        relay("wot", lambda k: r.wot.at[k, c], r.woh_s, r.woh_r)

    def context_ready(k):
        r.lse[k] = r.mrun[k] + jnp.log(r.lrun[k])
        inverse = 1.0 / r.lrun[k]
        parts = [r.acc[head_rows(h), lanes(k)] * inverse[:, lanes(h)] for h in range(s.heads)]
        context = jnp.concatenate(parts, axis=0)
        r.acc[:, lanes(k)] = context
        context = context.astype(bf16)
        r.ctxl[:, lanes(k)] = context
        r.ctxg[k, group(t), :] = context
        tp_push(("ctx", k), lambda d: r.ctxg.at[k, group(d), :], sems(r.ctx_s, r.ctx_r, k))

    if s.keep:
        for i, j in enumerate(z_peers):
            if s.line and i == 1:
                pl.when(outer)(lambda: pending.pop(("x", 1)).wait_recv())
            else:
                arrive(("x", i))
            forward_block(j, context_ready if i == nb - 2 else None)
            if i == RELAY:
                relays()
    else:
        def forward_remote(o, _):
            j = (b + o) % nb
            copy(r.xt.at[j], r.xt.at[j], r.x_s.at[j], r.x_r.at[j], z_dev(j)).wait_recv()
            forward_block(j)
            return 0

        relays()
        lax.fori_loop(1, nb, forward_remote, 0)
        for i in range(nb - 1):
            pending.pop(("x", i))
        for k in range(nc):
            context_ready(k)

    if s.keep:
        for j in range(nb):
            for k in range(nc):
                r.ebuf[j, k] = (r.ebuf[j, k].astype(f32) * jnp.exp(r.mrec[j, k] - r.lse[k])).astype(bf16)

    for h in range(2):
        arrive(("wot", 2 + h))
    for i, k in enumerate(tp_peers):
        push(("woc", i), r.wot.at[k, c], r.wot.at[k, c], r.woc_s.at[k], r.woc_r.at[k], core, r.wot.at[k, 1 - c], r.woc_r.at[k])
    tp_arrive("vec")
    for h in range(2):
        arrive(("xtf", 2 + h))
    tp_arrive("nrm")
    out_bias = [columns_of(r.vec[k])[:, 2:3] for k in range(ntp)]
    tp_arrive("woc")

    def output_rows(k):
        return jnp.concatenate([r.wot[k, 0], r.wot[k, 1]], axis=0)

    for k in range(ntp):
        r.wof[:, k * G:(k + 1) * G] = flip(output_rows(k)).astype(bf16)

    gain1 = v_col(3)
    bias_rows = HG // G
    hid_bias = jnp.concatenate([v_col(5 + k) for k in range(bias_rows)], axis=0)
    gain2 = v_col(6 + bias_rows)
    shift2 = v_col(7 + bias_rows)

    def forward_chunk(k):
        tp_arrive(("ctx", k))
        att = nn(r.wof[...], r.ctxg[k])
        hidden = [
            r.xtf[d][:, lanes(k)].astype(f32) + att[d * G:(d + 1) * G] + out_bias[d] for d in range(ntp)
        ]
        mean = sum(jnp.sum(a, axis=0, keepdims=True) for a in hidden) / s.d
        hidden = [a - mean for a in hidden]
        var = sum(jnp.sum(a * a, axis=0, keepdims=True) for a in hidden) / s.d
        inv = lax.rsqrt(var + eps_norm)
        r.inv1[k] = inv
        for d in range(ntp):
            r.n1f[k, d * G:(d + 1) * G, :] = hidden[d] * inv
        mid = r.n1f[k, group(t), :] * gain1 + v_col(4)
        mid_low = mid.astype(bf16)
        r.midl[:, lanes(k)] = mid_low
        act, slope = gelu_pair(nn(r.w1_t[...], mid_low) + hid_bias)
        act = act.astype(bf16)
        r.act[:, lanes(k)] = act
        r.slope[:, lanes(k)] = slope
        h2 = mid + nn(r.w2[...], act) + v_col(5 + bias_rows)
        r.h2[:, lanes(k)] = h2
        scaled = r.cot[:, lanes(k)].astype(f32) * gain2
        sum1 = jnp.sum(h2, axis=0, keepdims=True)
        h2c = h2 - sum1 / G
        sum2 = jnp.sum(h2c * h2c, axis=0, keepdims=True)
        sum3 = jnp.sum(scaled, axis=0, keepdims=True)
        sum4 = jnp.sum(scaled * h2c, axis=0, keepdims=True)
        r.st1[k, t] = jnp.concatenate([sum1, sum2, sum3, sum4, jnp.zeros((4, CH), f32)], axis=0)
        tp_push(("st1", k), lambda d: r.st1.at[k, d], sems(r.st1_s, r.st1_r, k))

    def backward_chunk(k):
        tp_arrive(("st1", k))
        stats = [r.st1[k, d] for d in range(ntp)]
        mean = sum(a[0:1] for a in stats) / s.d
        offs = [a[0:1] / G - mean for a in stats]
        var = sum(a[1:2] + G * o * o for a, o in zip(stats, offs)) / s.d
        inv = lax.rsqrt(var + eps_norm)
        first = sum(a[2:3] for a in stats) / s.d
        second = sum(a[3:4] + a[2:3] * o for a, o in zip(stats, offs)) * inv / s.d
        n2 = (r.h2[:, lanes(k)] - mean) * inv
        out_ref[:, lanes(k)] = (n2 * gain2 + shift2).astype(bf16)
        cot = r.cot[:, lanes(k)].astype(f32)
        r.cn2[:, lanes(k)] = cot * n2
        d2 = inv * (cot * gain2 - first - n2 * second)
        dffn = d2.astype(bf16)
        r.dffn[:, lanes(k)] = dffn
        dpre = (nn(r.w2_t[...], dffn) * r.slope[:, lanes(k)]).astype(bf16)
        r.dpre[:, lanes(k)] = dpre
        dmid = d2 + nn(r.w1[...], dpre)
        r.dmid[:, lanes(k)] = dmid
        n1 = r.n1f[k, group(t), :]
        r.dmn1[:, lanes(k)] = dmid * n1
        dmg = dmid * gain1
        part1 = jnp.sum(dmg, axis=0, keepdims=True)
        part2 = jnp.sum(dmg * n1, axis=0, keepdims=True)
        r.st2[k, t] = jnp.concatenate([part1, part2, jnp.zeros((6, CH), f32)], axis=0)
        r.dmgg[k, group(t), :] = dmg.astype(bf16)
        tp_push(("st2", k), lambda d: r.st2.at[k, d], sems(r.st2_s, r.st2_r, k))
        tp_push(("dmg", k), lambda d: r.dmgg.at[k, group(d), :], sems(r.dmg_s, r.dmg_r, k))

    for k in range(nc):
        forward_chunk(k)
    for k in range(nc):
        backward_chunk(k)
    store(out_ref, out_hbm)

    def sum_start(m):
        push(("gc", m), r.gsrc.at[m, 1 - c], r.gcore.at[m], r.gc_s.at[m], r.gc_r.at[m], core, r.gcore.at[m], r.gc_r.at[m])

    def add_low(a, b):
        return (a.astype(f32) + b.astype(f32)).astype(bf16)

    def when_owner(j, body):
        if s.owners < nb:
            pl.when(j < s.owners)(body)
        else:
            body()

    def quarter(j):
        return pl.ds(pl.multiple_of(j * s.rq, 16), s.rq)

    def to_owner(m, j):
        return r.ghalf.at[m, quarter(j)], r.gz.at[m, b], r.gz_s.at[m, j], r.gz_r.at[m, b], z_dev(j)

    def to_all(m, j):
        mine = r.gfin.at[m, c, quarter(b)]
        return mine, mine, r.ga_s.at[m, j], r.ga_r.at[m, b], z_dev(j)

    beside, across = (z_peers[0], z_peers[2]) if s.line else (None, None)

    def landed(ref, sem, dev):
        copy(ref, ref, sem, sem, dev).wait_recv()

    def sum_spread(m):
        arrive(("gc", m))
        r.ghalf[m] = add_low(r.gsrc[m, c], r.gcore[m])
        if s.line:
            push_if(outer, r.ghalf.at[m], r.gend.at[m], r.ge_s.at[m], r.ge_r.at[m], z_dev(beside))
        else:
            for j in z_peers:
                when_owner(j, lambda: copy(*to_owner(m, j)).start())

    def sum_cross(m):
        if s.line:
            one = copy(r.gmid.at[m], r.gcross.at[m], r.gx_s.at[m], r.gx_r.at[m], z_dev(across))

            @pl.when(inner)
            def _():
                landed(r.gend.at[m], r.ge_r.at[m], z_dev(beside))
                r.gmid[m] = add_low(r.ghalf[m], r.gend[m])
                one.start()

            sent_if.append((inner, one))

    def sum_own(m):
        if s.line:
            mine = r.gfin.at[m, c]
            one = copy(mine, mine, r.ga_s.at[m, 0], r.ga_r.at[m, 0], z_dev(beside))

            @pl.when(inner)
            def _():
                landed(r.gcross.at[m], r.gx_r.at[m], z_dev(across))
                r.gfin[m, c] = add_low(r.gmid[m], r.gcross[m])
                one.start()

            sent_if.append((inner, one))
        else:
            def body():
                for j in z_peers:
                    landed(r.gz.at[m, j], r.gz_r.at[m, j], z_dev(j))
                r.gz[m, b] = r.ghalf[m, quarter(b)]
                sums = r.gz[m, 0].astype(f32)
                for j in range(1, nb):
                    sums = sums + r.gz[m, j].astype(f32)
                r.gfin[m, c, quarter(b)] = sums.astype(bf16)
                for j in z_peers:
                    copy(*to_all(m, j)).start()
                r.upd[m:m + 1, :] = norm_of(m, b)

            when_owner(b, body)

    def norm_of(m, piece=None):
        here = slice(None) if piece is None else quarter(piece)

        def own_half(ref):
            first, second = (ref[here, s.lo[m] + h * s.half:s.lo[m] + (h + 1) * s.half] for h in range(2))
            return jnp.where(c == 0, first, second)

        _, _, u = lamb_moments(r.gfin[m, c, here].astype(f32), own_half(r.mom), own_half(r.squ))
        u = u + decay_rate * own_half(w_ref)
        return total(u * u)

    def sum_norm(m):
        if s.line:
            @pl.when(inner)
            def _():
                r.upd[m:m + 1, :] = norm_of(m)

    def sum_share(m):
        if s.line:
            pl.when(outer)(lambda: landed(r.gfin.at[m, c], r.ga_r.at[m, 0], z_dev(beside)))
        else:
            for j in z_peers:
                when_owner(j, lambda: landed(r.gfin.at[m, c, quarter(j)], r.ga_r.at[m, j], z_dev(j)))
        push(("gd", m), r.gfin.at[m, c], r.gfin.at[m, c], r.gd_s.at[m], r.gd_r.at[m], core, r.gfin.at[m, 1 - c], r.gd_r.at[m])

    def sum_done(m):
        arrive(("gd", m))
        store(r.gfin.at[m], g_hbm.at[m])

    def sum_sends_done(m):
        for j in z_peers:
            when_owner(j, lambda: copy(*to_owner(m, j)).wait_send())

        def body():
            for j in z_peers:
                copy(*to_all(m, j)).wait_send()

        when_owner(b, body)

    def keep_grad(m, grad):
        r.gsrc[m, 0] = grad[:, 0:s.half].astype(bf16)
        r.gsrc[m, 1] = grad[:, s.half:].astype(bf16)

    keep_grad(0, nt(r.dffn[...], r.act[...]))
    sum_start(0)
    keep_grad(1, nt(r.midl[...], r.dpre[...]))
    sum_start(1)
    vgl = r.vgl
    vgl[12:16, :] = jnp.zeros((4, G), f32)
    vgl[3:4, :] = lane_sums_f32(r.dmn1[...])
    vgl[4:5, :] = lane_sums_f32(r.dmid[...])
    hid_sum = lane_sums(r.dpre[...])
    for k in range(bias_rows):
        vgl[5 + k:6 + k, :] = hid_sum[:, k * G:(k + 1) * G]
    vgl[5 + bias_rows:6 + bias_rows, :] = lane_sums(r.dffn[...])
    vgl[6 + bias_rows:7 + bias_rows, :] = lane_sums_f32(r.cn2[...])
    vgl[7 + bias_rows:8 + bias_rows, :] = lane_sums(r.cot[...])
    r.upd[...] = jnp.zeros((8, 128), f32)
    if s.line:
        sum_spread(0)
        sum_spread(1)

    def context_chunk(k):
        tp_arrive(("st2", k))
        stats = [r.st2[k, d] for d in range(ntp)]
        first = sum(a[0:1] for a in stats) / s.d
        second = sum(a[1:2] for a in stats) / s.d
        inv = r.inv1[k]
        own = inv * (r.dmid[:, lanes(k)] * gain1 - first - r.n1f[k, group(t), :] * second)
        r.dxo[:, lanes(k)] = own
        tp_arrive(("dmg", k))
        for d in range(ntp):
            rows = slice(d * G, (d + 1) * G)
            part = inv * (r.dmgg[k, rows, :].astype(f32) - first - r.n1f[k, rows, :] * second)
            r.datt[rows, lanes(k)] = part.astype(bf16)
        dctx = nn(output_rows(t), r.datt[:, lanes(k)]).astype(bf16).astype(f32)
        r.dcz[k] = by_head(dctx)
        parts = [
            jnp.sum(dctx[head_rows(h)] * r.acc[head_rows(h), lanes(k)], axis=0, keepdims=True)
            for h in range(s.heads)
        ]
        r.delta[k] = jnp.concatenate(parts, axis=1)

    r.dqt[...] = jnp.zeros((G, T), f32)
    r.gkv[...] = jnp.zeros((2, G, G), f32)
    r.vb[...] = jnp.zeros((1, G), f32)

    def pair_terms(j, chunks):
        if s.keep:
            keys_t, vals = r.keys_t[j], r.vals[j]
        else:
            x_jt = r.xt[j]
            x_j = flip(x_jt).astype(bf16)
            keys_t = nn(r.wk_t[...], x_jt).astype(bf16)
            vals = (nn(x_j, r.wv[...]) + bias_v_row).astype(bf16)
            keys = nn(x_j, r.wk[...]).astype(bf16)
        dk = dv = None
        for k in chunks:
            if s.keep:
                p_low = r.ebuf[j, k]
                p = p_low.astype(f32)
            else:
                p = jnp.exp(jnp.where(same_doc(j, k), nn(keys, r.qz[k]), NEG) - r.lse[k])
                p_low = p.astype(bf16)
            ds = (p * (nn(vals, r.dcz[k]) - r.delta[k])).astype(bf16)
            for h in range(s.heads):
                r.dqt[head_rows(h), lanes(k)] += nn(keys_t[head_rows(h), :], ds[:, lanes(h)])
            dk_k, dv_k = nt(ds, r.qz[k]), nt(p_low, r.dcz[k])
            dk, dv = (dk_k, dv_k) if dk is None else (dk + dk_k, dv + dv_k)
        return dk, dv

    def finish_block(j, dk, dv):
        dk, dv = dk.astype(bf16), dv.astype(bf16)
        x_jt = r.xt[j]
        r.gkv[0] += nn(x_jt, dk)
        r.gkv[1] += nn(x_jt, dv)
        r.vb[...] += jnp.sum(dv.astype(f32), axis=0, keepdims=True)
        return nt(r.wk[...], dk) + nt(r.wv[...], dv)

    def dx_send(j):
        return r.dxs.at[j], r.dxr.at[b], r.dx_s.at[j], r.dx_r.at[b], z_dev(j)

    if s.keep:
        context_chunk(0)
        for j in z_peers + [b]:
            r.dkb[j], r.dvb[j] = pair_terms(j, [0])
        for k in range(1, nc):
            context_chunk(k)
        keep_grad(2, nt(r.ctxl[...], r.datt[...]))
        sum_start(2)
        vgl[2:3, :] = lane_sums(r.dxo[...].astype(bf16))
        for i in (1, 2, 0):
            j = z_peers[i]
            dk, dv = pair_terms(j, range(1, nc))
            r.dxs[j] = finish_block(j, dk + r.dkb[j], dv + r.dvb[j]).astype(bf16)
            if i == 0:
                push(("dx", 0), *dx_send(j), r.dxr.at[j], r.dx_r.at[j])
                sum_cross(1)
            else:
                push_if(outer, r.dxs.at[j], r.dxa.at[j], r.da_s.at[j], r.da_r.at[j], z_dev(beside))
                if i == 1:
                    sum_spread(2)
                else:
                    sum_cross(0)
        dk, dv = pair_terms(b, range(1, nc))
        r.dxo[...] += finish_block(b, dk + r.dkb[b], dv + r.dvb[b])
    else:
        for k in range(nc):
            context_chunk(k)
        keep_grad(2, nt(r.ctxl[...], r.datt[...]))
        sum_start(2)
        vgl[2:3, :] = lane_sums(r.dxo[...].astype(bf16))

        def backward_remote(o, _):
            j = (b + o) % nb
            r.dxs[j] = finish_block(j, *pair_terms(j, range(nc))).astype(bf16)
            copy(*dx_send(j)).start()
            return 0

        lax.fori_loop(1, nb, backward_remote, 0)
        r.dxo[...] += finish_block(b, *pair_terms(b, range(nc)))
        for m in (0, 1, 2):
            sum_spread(m)
        sum_own(0)
        sum_own(1)
    dq_t = (r.dqt[...] * scaling).astype(bf16)
    r.qsrc[...] = packed(jnp.concatenate([nt(r.xt[b], dq_t), r.gkv[0], r.gkv[1]], axis=1)).astype(bf16)

    def part(k, n):
        return pl.ds(pl.multiple_of(k * n, 16), n)

    push("qc", r.qsrc.at[part(1 - c, s.ph)], r.qcore, r.qc_s.at[0], r.qc_r.at[0], core, r.qcore, r.qc_r.at[0])
    vgl[0:1, :] = lane_sums(dq_t)
    vgl[1:2, :] = r.vb[...]
    push("vc", vgl, r.vgc, r.vc_s.at[0], r.vc_r.at[0], core, r.vgc, r.vc_r.at[0])
    arrive("qc")
    r.qhalf[...] = add_low(r.qsrc[part(c, s.ph)], r.qcore[...])

    def q_to_owner(j):
        return r.qhalf.at[part(j, s.pr)], r.qz_in.at[b], r.qz_s.at[j], r.qz_r.at[b], z_dev(j)

    def q_to_all(j):
        mine = r.qfin.at[part(c * s.owners + b, s.pr)]
        return mine, mine, r.qa_s.at[j], r.qa_r.at[b], z_dev(j)

    for j in reversed(z_peers):
        when_owner(j, lambda: copy(*q_to_owner(j)).start())
    if s.line:
        sum_own(0)
        sum_cross(2)
        sum_own(1)

        @pl.when(inner)
        def _():
            for i in (1, 2):
                j = z_peers[i]
                landed(r.dxa.at[j], r.da_r.at[j], z_dev(beside))
                r.dxs[j] = add_low(r.dxs[j], r.dxa[j])
                copy(*dx_send(j)).start()

        for i in (1, 2):
            sent_if.append((inner, copy(*dx_send(z_peers[i]))))
    else:
        sum_own(2)
    r.dxo[...] += nn(r.wq[...], dq_t)
    sum_norm(0)
    sum_norm(1)

    mine = jnp.zeros((s.pr, 128), f32)
    for j in z_peers:
        when_owner(b, lambda: landed(r.qz_in.at[j], r.qz_r.at[j], z_dev(j)))
    r.qz_in[b] = r.qhalf[part(b % s.owners, s.pr)]
    for j in range(nb):
        mine = mine + r.qz_in[j].astype(f32)
    mine = mine.astype(bf16)

    @partial(when_owner, b)
    def _():
        r.qfin[part(c * s.owners + b, s.pr), :] = mine
        for j in reversed(z_peers):
            copy(*q_to_all(j)).start()

    first_row = (c * s.owners + b % s.owners) * s.pr
    here = part(c * s.owners + b % s.owners, s.pr)
    _, _, u = lamb_moments(mine.astype(f32), r.pm[here, :], r.ps[here, :])
    u = u + decay_rate * r.pw[here, :]
    u = jnp.where(b < s.owners, u * u, 0.0)
    row = first_row + lax.broadcasted_iota(jnp.int32, (s.pr, 128), 0)
    lane = lax.broadcasted_iota(jnp.int32, (s.pr, 128), 1)
    column = row // G * 128 + lane
    is_q = column < G
    is_k = (column >= G) & (column < 2 * G)
    is_v = column >= 2 * G
    lead = [total(jnp.where(a, u, 0.0)) for a in (is_q, is_k, is_v)]
    if s.line:
        sum_own(2)
        sum_norm(2)
        rest = jnp.where(b == 1, r.upd[...], 0.0)
    else:
        rest = r.upd[...]
    r.nq[c, b] = jnp.concatenate(lead + [rest[m:m + 1] for m in (2, 1, 0)] + [jnp.zeros((2, 128), f32)], axis=0)
    same_tp = [(1 - c, b)] + [(i, j) for j in z_peers for i in (c, 1 - c)]
    for n, (i, j) in enumerate(same_tp):
        push(("nq", n), r.nq.at[c, b], r.nq.at[c, b], r.nq_s.at[i, j], r.nq_r.at[c, b], (i, j, t), r.nq.at[i, j], r.nq_r.at[i, j])
    arrive("vc")
    r.vgs[...] = vgl[...] + r.vgc[...]
    r.vgz[b] = r.vgs[...]
    for i, j in enumerate(z_peers):
        push(("vz", i), r.vgs, r.vgz.at[b], r.vz_s.at[j], r.vz_r.at[b], z_dev(j), r.vgz.at[j], r.vz_r.at[j])
    sum_share(0)
    sum_share(1)
    if s.line:
        other = jnp.where(b < 2, 2, 1)
        arrive(("dx", 0))
        landed(r.dxr.at[other], r.dx_r.at[other], z_dev(other))
        r.dxo[...] += r.dxr[beside].astype(f32) + r.dxr[other].astype(f32)
    else:
        for j in z_peers:
            landed(r.dxr.at[j], r.dx_r.at[j], z_dev(j))
            r.dxo[...] += r.dxr[j].astype(f32)
    ig_ref[...] = r.dxo[...]
    store(ig_ref, ig_hbm)
    sum_share(2)
    for n in range(len(same_tp)):
        arrive(("nq", n))
    sums = jnp.zeros((8, 128), f32)
    for i in range(s.nr):
        for j in range(nb):
            sums = sums + r.nq[i, j]
    r.nqt[t] = sums
    tp_push("nqt", lambda k: r.nqt.at[k], sems(r.nqt_s, r.nqt_r))
    for j in z_peers:
        when_owner(j, lambda: landed(r.qfin.at[part(c * s.owners + j, s.pr)], r.qa_r.at[j], z_dev(j)))
    push("qd", r.qfin.at[part(c, s.ph)], r.qfin.at[part(c, s.ph)], r.qd_s.at[0], r.qd_r.at[0], core, r.qfin.at[part(1 - c, s.ph)], r.qd_r.at[0])
    for m in range(3):
        sum_done(m)
    for i in range(nb - 1):
        arrive(("vz", i))
    vg = r.vgz[0]
    for j in range(1, nb):
        vg = vg + r.vgz[j]
    vg_ref[...] = vg[0:12]
    store(vg_ref, vg_hbm)
    arrive("qd")
    lead = unpacked(r.qfin[...])
    r.gq[0] = lead[:, 0:s.half]
    r.gq[1, :, 0:G] = lead[:, s.half:]
    r.gq[1, :, G:2 * G] = jnp.zeros((G, G), bf16)
    store(r.gq, g_hbm.at[3])
    tp_arrive("nqt")
    norms = r.nrm[0]
    lead = r.nqt[0]
    for k in range(1, ntp):
        norms = norms + r.nrm[k]
        lead = lead + r.nqt[k]
    ratio_ref[...] = jnp.sqrt(norms / (lead + 1e-12))
    store(ratio_ref, ratio_hbm)

    for one in sent:
        one.wait_send()
    for who, one in sent_if:
        pl.when(who)(lambda: one.wait_send())
    if not s.line:
        for m in range(3):
            sum_sends_done(m)
        for j in z_peers:
            copy(*dx_send(j)).wait_send()
    for j in z_peers:
        when_owner(j, lambda: copy(*q_to_owner(j)).wait_send())

    @partial(when_owner, b)
    def _():
        for j in z_peers:
            copy(*q_to_all(j)).wait_send()

    for one in stored:
        one.wait()


def finish_kernel(s, out_in, ig_in, w_ref, mom_ref, squ_ref, g_ref, ratio_ref, v_ref, vg_ref, mv_ref, sv_ref,
                  out_ref, ig_ref, gm_ref, gv_ref, nm_ref, ns_ref, nmv_ref, nsv_ref, nw_ref, nv_ref, grad):
    out_ref[...] = out_in[...]
    ig_ref[...] = ig_in[...]
    for m in range(4):
        for h in range(2):
            lo = s.lo[m] + h * s.half
            wide = min(s.half, s.lo[m] + s.width[m] - lo)
            grad[:, lo:lo + wide] = g_ref[m, h, :, 0:wide].astype(f32)
    cols = s.cols
    g = grad[...]
    gm_ref[...] = g
    new_m, new_s, u = lamb_moments(g, mom_ref[...], squ_ref[...])
    nm_ref[...] = new_m
    ns_ref[...] = new_s
    w = w_ref[...]
    u = u + decay_rate * w
    col = lax.broadcasted_iota(jnp.int32, (1, cols), 1)
    ratio = jnp.broadcast_to(ratio_ref[5:6, 0:1], (1, cols))
    for k, edge in ((4, s.lo[0]), (3, s.lo[1]), (2, s.lo[2]), (1, 2 * s.g), (0, s.g)):
        ratio = jnp.where(col < edge, ratio_ref[k:k + 1, 0:1], ratio)
    nw_ref[...] = w - matrix_rate * ratio * u

    @pl.when(pl.program_id(0) == 0)
    def _():
        vg = vg_ref[...]
        gv_ref[...] = vg
        new_mv, new_sv, uv = lamb_moments(vg, mv_ref[...], sv_ref[...])
        nmv_ref[...] = new_mv
        nsv_ref[...] = new_sv
        nv_ref[...] = v_ref[...] - learn_rate * uv


def local(mesh_shape, tokens, cotangent, segment_ids, matrices, vectors, moment_mat, square_mat, moment_vec, square_vec):
    tokens, cotangent = tokens.T, cotangent.T
    s = Sizes(mesh_shape, tokens.shape, segment_ids.shape[1])
    names, scratch = scratch_of(s)
    hbm = pl.BlockSpec(memory_space=pltpu.HBM)
    S = jax.ShapeDtypeStruct
    small = [
        pltpu.VMEM(tokens.shape, bf16), pltpu.VMEM(tokens.shape, f32),
        pltpu.VMEM(vectors.shape, f32), pltpu.VMEM((8, 128), f32),
    ]
    given = (tokens, cotangent, segment_ids, matrices, vectors, moment_mat, square_mat)
    output, input_grad, grads, vector_grad, ratio = pl.pallas_call(
        partial(layer_kernel, s, names),
        out_shape=(
            S(tokens.shape, bf16),
            S(tokens.shape, f32),
            S((4, 2, s.g, s.half), bf16),
            S(vectors.shape, f32),
            S((8, 128), f32),
        ),
        in_specs=[hbm] * 7,
        out_specs=(hbm,) * 5,
        scratch_shapes=small + scratch,
        compiler_params=pltpu.CompilerParams(
            collective_id=0, has_side_effects=True, vmem_limit_bytes=s.vmem
        ),
        name="layer",
    )(*(pltpu.with_memory_space_constraint(a, pltpu.HBM) for a in given))

    steps = s.owners

    def rows(a, n):
        return pl.BlockSpec((n, a.shape[1]), lambda i: (i, 0))

    def whole(a):
        return pl.BlockSpec(a.shape, lambda i: (0, 0))

    mat = rows(matrices, s.rq)
    vec = whole(vectors)
    results = pl.pallas_call(
        partial(finish_kernel, s),
        grid=(steps,),
        out_shape=(
            S(tokens.shape, bf16),
            S(tokens.shape, f32),
            S(matrices.shape, f32),
            S(vectors.shape, f32),
            S(matrices.shape, f32),
            S(matrices.shape, f32),
            S(vectors.shape, f32),
            S(vectors.shape, f32),
            S(matrices.shape, f32),
            S(vectors.shape, f32),
        ),
        in_specs=[
            rows(tokens, s.rq), rows(tokens, s.rq), mat, mat, mat,
            pl.BlockSpec((4, 2, s.rq, s.half), lambda i: (0, 0, i, 0)),
            pl.BlockSpec((8, 128), lambda i: (0, 0)), vec, vec, vec, vec,
        ],
        out_specs=(rows(tokens, s.rq), rows(tokens, s.rq), mat, vec, mat, mat, vec, vec, mat, vec),
        scratch_shapes=[pltpu.VMEM((s.rq, s.lo[0] + HG), f32)],
        compiler_params=pltpu.CompilerParams(vmem_limit_bytes=40 * 2**20),
        name="finish",
    )(output, input_grad, matrices, moment_mat, square_mat, grads, ratio, vectors, vector_grad, moment_vec, square_vec)
    return (results[0].T, results[1].T) + tuple(results[2:])


def solution(mesh):
    return jax.shard_map(
        partial(local, dict(mesh.shape)),
        mesh=mesh,
        in_specs=(
            P(("rows", "blk"), "tp"),
            P(("rows", "blk"), "tp"),
            P("rows", None),
            P("tp", None),
            P(None, "tp"),
            P("tp", None),
            P("tp", None),
            P(None, "tp"),
            P(None, "tp"),
        ),
        out_specs=(
            P(("rows", "blk"), "tp"),
            P(("rows", "blk"), "tp"),
            P("tp", None),
            P(None, "tp"),
            P("tp", None),
            P("tp", None),
            P(None, "tp"),
            P(None, "tp"),
            P("tp", None),
            P(None, "tp"),
        ),
        check_vma=False,
    )
```
